128 devices in a mesh: lat: 8 (over x, y_lo), lon: 16 (over y_hi, z, core).
Axes of the slice: x: 4, y: 4 (y_hi: 2, y_lo: 2; y = y_hi * 2 + y_lo), z: 4, core: 2. Of those that a mesh axis runs over, the one named last changes fastest.
Arguments:
- tokens: bfloat16 [2, 192, 192, 512], P(None, 'lat', 'lon'), may hold values from -6 to 6
- mask_ids: int32 [2, 192, 192], P(None, 'lat', 'lon'), may hold values from 0 to 8, as said below
- fine_bias: float32 [8, 144, 144], replicated, may hold values from -4 to 300
- fine_qkv: bfloat16 [512, 1536], replicated, may hold values from -0.25 to 0.25
- fine_out: bfloat16 [512, 512], replicated, may hold values from -0.25 to 0.25
- merge_weight: bfloat16 [2048, 1024], replicated, may hold values from -0.125 to 0.125
- coarse_bias: float32 [16, 144, 144], replicated, may hold values from -4 to 300
- coarse_qkv: bfloat16 [1024, 3072], replicated, may hold values from -0.1875 to 0.1875
- coarse_out: bfloat16 [1024, 1024], replicated, may hold values from -0.1875 to 0.1875
- cotangent: bfloat16 [2, 96, 96, 1024], P(None, 'lat', 'lon'), may hold values from -6 to 6
Outputs:
- coarse_result: bfloat16 [2, 96, 96, 1024], P(None, 'lat', 'lon')
- token_grad: bfloat16 [2, 192, 192, 512], P(None, 'lat', 'lon')
The draws below stay inside these ranges and needn't reach their ends.
Inputs may be any that keep to these rules, and one draw needn't show every extreme that they name: mask_ids = 3 * level region + latitude region of the shifted grid: the level region is 0 below level 0, 1 below 1, else 2; the latitude region is 0 below row 186, 2 in the last r rows, else 1, where r, from 1 to 5, is drawn separately for each level and each longitude column.
All inputs are finite; a program needn't handle non-finite values.
Results may differ from the reference program's by a relative error of at most 0.022.
Values may be sent and summed in bfloat16 or wider, within the bound.
A program may use at most 128 MiB of HBM per device.

```python
import jax
import jax.numpy as jnp
from jax import lax

WIDTH = 512
HEADS_F = 8
LEV = 2
WL = 2
WA = 6
WO = 12
CWIDTH = 1024
HEADS_C = 16
WIN = 144
LAT = 192
LON = 192
CLAT = 96
CLON = 96


def spiked_bias(key, head_count, span):
    first = jax.random.fold_in(key, 0)
    return jnp.clip(jax.random.normal(first, (head_count, span, span), jnp.float32), -4.0, 4.0)


def draw_mask_ids(key, part):
    key = jax.random.fold_in(key, 13)
    cut_rows = jax.random.randint(key, (LEV, 1, LON), 1, WA).astype(jnp.int32)
    levels = jnp.arange(LEV, dtype=jnp.int32)
    level_region = (levels >= LEV - WL).astype(jnp.int32) + (levels >= LEV - WL // 2).astype(jnp.int32)
    rows = jnp.arange(LAT, dtype=jnp.int32)[None, :, None]
    lat_region = (rows >= LAT - WA).astype(jnp.int32) + (rows >= LAT - cut_rows).astype(jnp.int32)
    region = 3 * level_region[:, None, None] + lat_region
    return (region + jnp.zeros((LEV, LAT, LON), jnp.int32)).astype(jnp.int32)


def draw_fine_bias(key, part):
    key = jax.random.fold_in(key, 5)
    return spiked_bias(key, HEADS_F, WIN)


def draw_coarse_bias(key, part):
    key = jax.random.fold_in(key, 9)
    return spiked_bias(key, HEADS_C, WIN)


def shard_levels(own_key, dims, shards, smallest, high):
    def one(axis_at, shards_of):
        steps = jax.random.uniform(jax.random.fold_in(jax.random.fold_in(own_key, 6), axis_at), (shards_of,), jnp.float32, smallest / len(shards), high / len(shards))
        return jnp.repeat(jnp.exp(steps), dims[axis_at] // shards_of).reshape((-1,) + (1,) * (len(dims) - axis_at - 1))

    factor_of = one(*shards[0])
    for cut in shards[1:]:
        factor_of = factor_of * one(*cut)
    return factor_of


def bell_draw(stream_key, dims, deviation, limit, cuts=(), held_as=jnp.bfloat16):
    drawn = jax.random.normal(stream_key, dims, jnp.float32) * deviation
    if len(cuts) > 0:
        drawn = shard_levels(stream_key, dims, cuts, -0.22, 0.18) * drawn
    return jnp.clip(drawn, min=-limit, max=limit).astype(held_as)


def setup_inputs(seed: int = 0) -> dict:
    key_list = jax.random.split(jax.random.key(seed), 11)
    tokens = bell_draw(key_list[0], (LEV, LAT, LON, WIDTH), 1.0, 6.0, ((1, 8), (2, 16)))
    mask_ids = draw_mask_ids(jax.random.fold_in(key_list[10], 71), 0)
    fine_bias = draw_fine_bias(jax.random.fold_in(key_list[10], 71), 0)
    fine_qkv = bell_draw(key_list[3], (WIDTH, 3 * WIDTH), WIDTH ** -0.5, 0.25)
    fine_out = bell_draw(key_list[4], (WIDTH, WIDTH), WIDTH ** -0.5, 0.25)
    merge_weight = bell_draw(key_list[5], (4 * WIDTH, CWIDTH), (4 * WIDTH) ** -0.5, 0.125)
    coarse_bias = draw_coarse_bias(jax.random.fold_in(key_list[10], 71), 0)
    coarse_qkv = bell_draw(key_list[7], (CWIDTH, 3 * CWIDTH), CWIDTH ** -0.5, 0.1875)
    coarse_out = bell_draw(key_list[8], (CWIDTH, CWIDTH), CWIDTH ** -0.5, 0.1875)
    cotangent = bell_draw(key_list[9], (LEV, CLAT, CLON, CWIDTH), 1.0, 6.0, ((1, 8), (2, 16)))
    return {"tokens": tokens, "mask_ids": mask_ids, "fine_bias": fine_bias, "fine_qkv": fine_qkv, "fine_out": fine_out, "merge_weight": merge_weight, "coarse_bias": coarse_bias, "coarse_qkv": coarse_qkv, "coarse_out": coarse_out, "cotangent": cotangent}


EPSILON = 1e-05

def layer_norm(values):
    center = values - lax.optimization_barrier(jnp.mean(values, axis=-1, keepdims=True))
    spread = lax.optimization_barrier(jnp.mean(center * center, axis=-1, keepdims=True))
    return center * lax.rsqrt(spread + EPSILON)

def to_windows(grid_in, lon_span):
    levels, lat_rows, lon_cols, channels = grid_in.shape
    shaped = grid_in.reshape(levels // WL, WL, lat_rows // WA, WA, lon_cols // lon_span, lon_span, channels)
    shaped = shaped.transpose(0, 2, 4, 1, 3, 5, 6)
    return shaped.reshape(-1, WL * WA * lon_span, channels)

def from_windows(windowed, levels, lat_rows, lon_cols, lon_span):
    channels = windowed.shape[-1]
    shaped = windowed.reshape(levels // WL, lat_rows // WA, lon_cols // lon_span, WL, WA, lon_span, channels)
    return shaped.transpose(0, 3, 1, 4, 2, 5, 6).reshape(levels, lat_rows, lon_cols, channels)

def window_attention(queries, key_vecs, value_vecs, bias_table, allowed):
    scale = queries.shape[-1] ** (-0.5)
    scores = jnp.einsum('wqhd,wkhd->whqk', queries.astype(jnp.float32), key_vecs.astype(jnp.float32)) * scale
    scores = scores + bias_table[None]
    if allowed is not None:
        scores = jnp.where(allowed[:, None], scores, -1e+30)
    row_max = lax.stop_gradient(lax.optimization_barrier(jnp.max(scores, axis=-1, keepdims=True)))
    exponentials = jnp.exp(scores - row_max)
    probabilities = (exponentials / lax.optimization_barrier(jnp.sum(exponentials, axis=-1, keepdims=True))).astype(jnp.bfloat16)
    mixed = jnp.einsum('whqk,wkhd->wqhd', probabilities.astype(jnp.float32), value_vecs.astype(jnp.float32))
    mixed = mixed.astype(jnp.bfloat16)
    return mixed.reshape(mixed.shape[0], mixed.shape[1], -1)

def window_block(windowed, allowed, bias_table, w_qkv, w_out):
    count, span, channels = windowed.shape
    head_count = bias_table.shape[0]
    residual_in = windowed.astype(jnp.float32)
    normed = layer_norm(residual_in).astype(jnp.bfloat16)
    projected = jnp.dot(normed.reshape(count * span, channels), w_qkv, preferred_element_type=jnp.float32)
    projected = projected.astype(jnp.bfloat16).reshape(count, span, 3, head_count, channels // head_count)
    attended = window_attention(projected[:, :, 0], projected[:, :, 1], projected[:, :, 2], bias_table, allowed)
    mixed = jnp.dot(attended.reshape(count * span, channels), w_out, preferred_element_type=jnp.float32)
    return (residual_in + mixed.reshape(count, span, channels)).astype(jnp.bfloat16)

def merge_patches(grid_in, merge_weight):
    stacked = jnp.concatenate([grid_in[:, 0::2, 0::2], grid_in[:, 1::2, 0::2], grid_in[:, 0::2, 1::2], grid_in[:, 1::2, 1::2]], axis=-1)
    normed = layer_norm(stacked.astype(jnp.float32)).astype(jnp.bfloat16)
    shape_in = stacked.shape
    merged = jnp.dot(normed.reshape(-1, shape_in[-1]), merge_weight, preferred_element_type=jnp.float32)
    return merged.astype(jnp.bfloat16).reshape(shape_in[0], shape_in[1], shape_in[2], -1)

def fine_layer(shifted, mask_ids, fine_bias, fine_qkv, fine_out):
    levels, lat_rows, lon_cols, channels = shifted.shape
    windowed = to_windows(shifted, WO)
    group_ids = to_windows(mask_ids[..., None], WO)[..., 0]
    groups = levels // WL * (lat_rows // WA)

    def one_group(packed):
        window_part, id_part = packed
        allowed = id_part[:, :, None] == id_part[:, None, :]
        return window_block(window_part, allowed, fine_bias, fine_qkv, fine_out)
    mixed = lax.map(jax.checkpoint(one_group), (windowed.reshape(groups, -1, WIN, channels), group_ids.reshape(groups, -1, WIN)))
    return from_windows(mixed.reshape(-1, WIN, channels), levels, lat_rows, lon_cols, WO)

def coarse_layer(merged, coarse_bias, coarse_qkv, coarse_out):
    levels, lat_rows, lon_cols, channels = merged.shape
    windowed = to_windows(merged, WO)
    groups = levels // WL * (lat_rows // WA)

    def one_group(window_part):
        return window_block(window_part, None, coarse_bias, coarse_qkv, coarse_out)
    mixed = lax.map(jax.checkpoint(one_group), windowed.reshape(groups, -1, WIN, channels))
    return from_windows(mixed.reshape(-1, WIN, channels), levels, lat_rows, lon_cols, WO)

def reference(tokens, mask_ids, fine_bias, fine_qkv, fine_out, merge_weight, coarse_bias, coarse_qkv, coarse_out, cotangent):

    def forward(field):
        shifted = jnp.roll(field, (-(WL // 2), -(WA // 2), -(WO // 2)), (0, 1, 2))
        mixed = fine_layer(shifted, mask_ids, fine_bias, fine_qkv, fine_out)
        restored = jnp.roll(mixed, (WL // 2, WA // 2, WO // 2), (0, 1, 2))
        merged = merge_patches(restored, merge_weight)
        return coarse_layer(merged, coarse_bias, coarse_qkv, coarse_out)
    coarse_result, pullback = jax.vjp(forward, tokens)
    token_grad, = pullback(cotangent)
    return (coarse_result, token_grad)
```

```python
import functools

import jax
import jax.numpy as jnp
import numpy as np
from jax import lax
from jax.experimental import pallas as pl
from jax.experimental.pallas import tpu as pltpu
from jax.sharding import PartitionSpec as P

F32 = jnp.float32
BF16 = jnp.bfloat16
EPSILON = 1e-05
MASKED = -1e30
MESH = pl.DeviceIdType.MESH

UNIT = 80
PART = 176
QUARTER = 96
NEIGHBOURS = [(a, b) for a in (-1, 0, 1) for b in (-1, 0, 1) if (a, b) != (0, 0)] + [(0, 2), (0, -2)]


def one_hot(pairs, rows, columns):
    out = np.zeros((rows, columns), np.float32)
    for r, c in pairs:
        out[r, c] = 1.0
    return out


def region_of(row, col):
    if row >= 3:
        return (row - 3) * 6 + col - 6 if col >= 6 else 128 + (row - 3) * 6 + col
    return 256 + row * 6 + col - 6 if col >= 6 else 288 + row * 6 + col


def part_of(s, o):
    half, c = divmod(o, 6)
    if s < 9:
        at = s * 6 + c
    elif s < 21:
        at = 64 + (s - 9) * 6 + c
    else:
        at = 144 + (s - 21) * 6 + c
    return half * PART + at


@functools.cache
def row_orders():
    to_region = one_hot([(region_of(r, c), r * 16 + c) for r in range(24) for c in range(12)], 320, 384)
    unit_pairs, part_pairs = [], []
    for s in range(24):
        for o in range(12):
            unit = UNIT * (s // 6) + 12 * (s % 6) + o
            unit_pairs.append((unit, region_of((s + 3) % 24, (o + 6) % 12)))
            part_pairs.append((part_of(s, o), unit))
    to_unit = one_hot(unit_pairs, 320, 320)
    to_part = one_hot(part_pairs, 2 * PART, 320)
    merge = np.zeros((2, 4, 72, 4 * QUARTER), np.float32)
    for u in range(2):
        for k, (dr, dc) in enumerate([(0, 0), (1, 0), (0, 1), (1, 1)]):
            for r in range(6):
                for c in range(12):
                    quarter, col = divmod(2 * c + dc, 6)
                    s = 12 * u + 2 * r + dr - 3
                    if u == 1:
                        at = (s - 9) * 6 + col
                    else:
                        at = 64 + (s + 3) * 6 + col if s < 0 else s * 6 + col
                    merge[u, k, r * 12 + c, quarter * QUARTER + at] = 1.0
    coarse = one_hot(
        [
            (l * 72 + r * 12 + c, (((c // 6) * 2 + l) * 6 + r) * 16 + c % 6)
            for l in range(2)
            for r in range(6)
            for c in range(12)
        ],
        144,
        384,
    )
    id_row = one_hot([(t, t // 12 + 2) for t in range(72)], UNIT, 8)
    id_col = one_hot([(t, t % 12) for t in range(72)], UNIT, 12)
    both = lambda m: [m, np.swapaxes(m, -1, -2)]
    orders = both(to_region) + both(to_unit) + both(to_part) + both(merge) + both(coarse)
    return [np.ascontiguousarray(m).astype(jnp.bfloat16) for m in orders] + [id_row, id_col]


def dot(a, b):
    return lax.dot_general(a, b, (((1,), (0,)), ((), ())), preferred_element_type=F32)


def dot_nt(a, b):
    return lax.dot_general(a, b, (((1,), (1,)), ((), ())), preferred_element_type=F32)


def dot_tn(a, b):
    return lax.dot_general(a, b, (((0,), (0,)), ((), ())), preferred_element_type=F32)


def normed_rows(x):
    center = x - jnp.mean(x, axis=-1, keepdims=True)
    scale = lax.rsqrt(jnp.mean(center * center, axis=-1, keepdims=True) + EPSILON)
    return center * scale, scale


def norm_grad(grad, hat, scale):
    inner = jnp.mean(grad * hat, axis=-1, keepdims=True)
    return scale * (grad - jnp.mean(grad, axis=-1, keepdims=True) - hat * inner)


def one_row(x):
    span = x.shape[0] // 2
    low = lax.broadcasted_iota(jnp.int32, (span, 128), 1) < 64
    return jnp.where(low, x[:span], x[span:])


def rows_at(start, size, unit=16):
    return pl.ds(pl.multiple_of(start, unit), size)


def loop(count, body):
    lax.fori_loop(0, count, lambda t, c: (body(t), c)[1], 0)


class Box:
    def __init__(self, **fields):
        self.__dict__.update(fields)


ARGS = dict(
    tokens=0, mask_ids=1, fine_bias=0, fine_qkv=0, fine_out=0, merge_weight=0, coarse_bias=0, coarse_qkv=0,
    coarse_out=0, cotangent=2, to_region=0, to_region_t=0, to_unit=0, to_unit_t=0, to_part=0, to_part_t=0,
    merge=0, merge_t=0, coarse=0, coarse_t=0, id_row=1, id_col=1,
)
LOADED = dict(
    tokens=0, to_region=0, to_unit=0, fine_bias=0, fine_qkv=0, fine_out=0, to_part=0, coarse=0, coarse_bias=0,
    merge=1, merge_weight=0, coarse_qkv=0, coarse_out=0, coarse_t=0, merge_t=1, to_part_t=0, to_unit_t=0,
    to_region_t=0,
)
SCRATCH = dict(
    x16=((2, 24, 16, 512), BF16),
    heads2=((160, 128), BF16),
    heads2_c=((288, 128), BF16),
    send1=((2, 192, 512), BF16),
    region=((2, 320, 512), BF16),
    unit_x=((640, 512), BF16),
    unit_n=((640, 512), BF16),
    hat_f=((640, 512), F32),
    scale_f=((640, 128), F32),
    proj=((704, 1536), BF16),
    bias_f=((2, 2, 4, 160, 128), F32),
    raised_f=((8, 4, 160, 128), BF16),
    recip_f=((640, 512), F32),
    heads_f=((640, 512), BF16),
    send2=((2, 2, PART, 512), BF16),
    quarters=((2, 4, QUARTER, 512), BF16),
    hat_m=((144, 2048), F32),
    scale_m=((144, 128), F32),
    normed_m=((144, 2048), BF16),
    merged=((144, 1024), BF16),
    hat_c=((144, 1024), F32),
    scale_c=((144, 128), F32),
    normed_c=((144, 1024), BF16),
    proj_c=((256, 3072), BF16),
    bias_c=((16, 144, 256), F32),
    raised_c=((8, 288, 256), BF16),
    recip_c=((144, 1024), F32),
    heads_c=((144, 1024), BF16),
    result=((144, 1024), BF16),
    result16=((2, 2, 6, 6, 1024), BF16),
    cot_raw=((2, 2, 6, 6, 1024), BF16),
    cot16=((2, 2, 6, 16, 1024), BF16),
    cot=((144, 1024), BF16),
    dheads_c=((144, 1024), BF16),
    dprod_c=((144, 1024), BF16),
    dproj_c=((144, 3072), BF16),
    grad_c=((144, 1024), F32),
    dmerged=((144, 1024), BF16),
    grad_m=((144, 2048), F32),
    send3=((2, 4, QUARTER, 512), BF16),
    part=((2, 2, PART, 512), BF16),
    dmixed=((640, 512), BF16),
    dheads_f=((640, 512), BF16),
    dprod_f=((640, 512), BF16),
    dproj_f=((640, 1536), BF16),
    send4=((2, 192, 512), BF16),
    region4=((2, 320, 512), BF16),
)
def kernel(n_lat, n_lon, *refs):
    rest = list(refs)
    hbm = Box(**{name: rest.pop(0) for name in ARGS})
    result_ref, grad_ref = rest.pop(0), rest.pop(0)
    vm = Box(**{name: rest.pop(0) for name in SCRATCH})
    ld = Box(**{name: rest.pop(0) for name in LOADED})
    load_sem, send_sem, recv_sem, near_sem = rest

    i, j = lax.axis_index("lat"), lax.axis_index("lon")
    odd = lax.rem(j, 2)
    even = odd == 0

    def device(di, dj):
        return (lax.rem(i + di + n_lat, n_lat), lax.rem(j + dj + n_lon, n_lon))

    def remote(src, dst, sem, l, target):
        return pltpu.make_async_remote_copy(
            src_ref=src,
            dst_ref=dst,
            send_sem=send_sem.at[sem, l],
            recv_sem=recv_sem.at[sem, l],
            device_id=target,
            device_id_type=MESH,
        )

    vm.quarters[:, :, 80:, :] = jnp.zeros((2, 4, QUARTER - 80, 512), BF16)
    barrier = pltpu.get_barrier_semaphore()
    for di, dj in NEIGHBOURS:
        pl.semaphore_signal(barrier, inc=1, device_id=device(di, dj), device_id_type=MESH)

    loads = Box()
    for at, (name, paired) in enumerate(LOADED.items()):
        src = getattr(hbm, name)
        if paired:
            src = src.at[odd]
        copy = pltpu.make_async_copy(src, getattr(ld, name), load_sem.at[at])
        copy.start()
        setattr(loads, name, copy)
    own_cot = pltpu.make_async_copy(
        hbm.cotangent.at[:, pl.ds(6 * odd, 6)], vm.cot_raw.at[odd], near_sem.at[0, 0]
    )
    own_cot.start()

    vm.x16[:, :, 12:, :] = jnp.zeros((2, 24, 4, 512), BF16)
    vm.cot16[:, :, :, 6:, :] = jnp.zeros((2, 2, 6, 10, 1024), BF16)
    for end in (320, 640):
        vm.proj[end : end + 64, :] = jnp.zeros((64, 1536), BF16)
    vm.proj_c[144:, :] = jnp.zeros((112, 3072), BF16)
    for ref in (vm.heads2, vm.heads2_c):
        low = lax.broadcasted_iota(jnp.int32, ref.shape, 1) < 64
        first = lax.broadcasted_iota(jnp.int32, ref.shape, 0) < ref.shape[0] // 2
        ref[...] = jnp.where(low == first, 1.0, 0.0).astype(BF16)

    def two_heads(x, mask):
        return jnp.concatenate([x, x], axis=0) * mask[...]

    loads.tokens.wait()
    loads.to_region.wait()
    vm.x16[:, :, :12, :] = ld.tokens[...]
    pl.semaphore_wait(barrier, len(NEIGHBOURS))
    pieces = [(0, 128, (0, -1)), (128, 32, (-1, 0)), (160, 32, (-1, -1))]

    def first(l):
        return [
            remote(
                vm.send1.at[l, pl.ds(at, size)], vm.region.at[l, pl.ds(128 + at, size)], n, l, device(*to)
            )
            for n, (at, size, to) in enumerate(pieces)
        ]

    def regions(l):
        ordered = dot(ld.to_region[...], vm.x16[l].reshape(384, 512)).astype(BF16)
        vm.region[l, :128, :] = ordered[:128]
        vm.send1[l] = ordered[128:]
        for copy in first(l):
            copy.start()

    loop(2, regions)
    partner_cot = remote(
        hbm.cotangent.at[:, pl.ds(6 - 6 * odd, 6)], vm.cot_raw.at[odd], 3, 0, device(0, 1 - 2 * odd)
    )
    partner_cot.start()

    loads.fine_bias.wait()
    lanes = lax.broadcasted_iota(jnp.int32, (UNIT, 128), 1)
    subs = lax.broadcasted_iota(jnp.int32, (UNIT, 128), 0)
    past = jnp.where(lanes >= 72, MASKED, 0.0).astype(F32)
    for level in range(2):
        spread = dot(hbm.id_row[...], hbm.mask_ids[level, 16:24, :].astype(F32))
        id_of = jnp.sum(spread * hbm.id_col[...], axis=-1, keepdims=True)
        id_at = dot(jnp.ones((8, UNIT), F32), jnp.where(lanes == subs, id_of, 0.0))[:1]
        apart = jnp.where(id_of == id_at, past, MASKED)
        for head in range(8):
            span = slice(72 * level, 72 * level + 72)
            block = ld.fine_bias[head, span, span]
            block = jnp.concatenate([block, jnp.zeros((72, 56), F32)], axis=1)
            block = jnp.concatenate([block, jnp.zeros((8, 128), F32)], axis=0)
            at = slice(UNIT * (head % 2), UNIT * (head % 2) + UNIT)
            vm.bias_f[0, level, head // 2, at, :] = block + past
            vm.bias_f[1, level, head // 2, at, :] = block + apart

    loads.coarse_bias.wait()

    def coarse_pad(h):
        vm.bias_c[h] = jnp.concatenate([ld.coarse_bias[h], jnp.full((144, 112), MASKED, F32)], axis=1)

    loop(16, coarse_pad)
    loads.to_unit.wait()
    loads.fine_qkv.wait()
    loads.fine_out.wait()
    loads.to_part.wait()

    own, next_, before = (0, 64, 0), (64, 80, 0), (144, 32, 64)

    def second(l, kind, half, sem, q, to):
        at, size, into = kind
        return remote(
            vm.send2.at[l, half, pl.ds(at, size)], vm.quarters.at[l, q, pl.ds(into, size)], sem, l, device(*to)
        )

    def second_near(l, kind, half, sem, q):
        at, size, into = kind
        return pltpu.make_async_copy(
            vm.send2.at[l, half, pl.ds(at, size)], vm.quarters.at[l, q, pl.ds(into, size)], near_sem.at[sem, l]
        )

    side = (0, 1)
    even_sends = [
        (next_, 0, 5, 1, (0, 1)), (next_, 1, 6, 2, (0, 1)), (before, 0, 9, 1, (1, 0)), (before, 1, 10, 2, (1, 0)),
    ]
    even_near = [(own, 0, 1, 1), (own, 1, 2, 2)]
    even_takes = [
        (own, 0, 4, 0, side), (own, 0, 7, 3, side), (before, 0, 8, 0, side), (before, 0, 9, 1, side),
        (before, 0, 10, 2, side), (before, 0, 11, 3, side),
    ]
    odd_sends = [
        (own, 1, 4, 0, (0, 1)), (next_, 1, 12, 0, (0, 2)), (before, 1, 8, 0, (1, 1)), (own, 0, 7, 3, (0, -1)),
        (before, 0, 11, 3, (1, -1)),
    ]
    odd_near = [(next_, 0, 1, 3)]
    odd_takes = [(next_, 0, 12, 0, side), (next_, 0, 5, 1, side), (next_, 0, 6, 2, side)]

    def by_parity(of_even, of_odd):
        @pl.when(even)
        def _():
            of_even()

        @pl.when(odd == 1)
        def _():
            of_odd()

    def start_all(far, near, far_list, near_list, l):
        for args in far_list:
            far(l, *args).start()
        for args in near_list:
            near(l, *args).start()

    def take_all(far, near, take_list, near_list, l):
        for args in near_list:
            near(l, *args).wait()
        for args in take_list:
            far(l, *args).wait_recv()

    def sent_all(far, far_list, l):
        for args in far_list:
            far(l, *args).wait_send()

    def fine_forward(l):
        base = l * 320
        level = rows_at(base, 320)
        for copy in first(l):
            copy.wait()
        vm.unit_x[level, :] = dot(ld.to_unit[...], vm.region[l]).astype(BF16)

        def fine_norm(t):
            at = rows_at(base + t * 80, 80)
            hat, scale = normed_rows(vm.unit_x[at, :].astype(F32))
            vm.hat_f[at, :] = hat
            vm.scale_f[at, :] = jnp.broadcast_to(scale, (80, 128))
            vm.unit_n[at, :] = hat.astype(BF16)

        loop(4, fine_norm)

        def fine_project(t):
            cols = rows_at(t * 512, 512, 512)
            scale = jnp.where(t < 1, 0.125, 1.0).astype(F32)
            vm.proj[level, cols] = (dot(vm.unit_n[level, :], ld.fine_qkv[:, cols]) * scale).astype(BF16)

        loop(3, fine_project)

        def fine_attend(m):
            last = lax.div(m, 3)
            at, wide = rows_at(base + m * UNIT, UNIT), rows_at(base + m * UNIT, 128)
            pairs = [slice(128 * p, 128 * p + 128) for p in range(4)]
            ones = jnp.ones((128, 128), BF16)
            scores = [
                dot_nt(two_heads(vm.proj[at, pair], vm.heads2), vm.proj[wide, 512 + pair.start : 512 + pair.stop])
                + vm.bias_f[last, 1 - l, p]
                for p, pair in enumerate(pairs)
            ]
            tops = [jnp.max(s, axis=-1, keepdims=True) for s in scores]
            raised = [jnp.exp(s - t).astype(BF16) for s, t in zip(scores, tops)]
            sums = [
                dot(e, jnp.concatenate([vm.proj[wide, 1024 + pair.start : 1024 + pair.stop], ones], axis=1))
                for e, pair in zip(raised, pairs)
            ]
            for p, pair in enumerate(pairs):
                recip = 1.0 / one_row(sums[p][:, 128:])
                vm.raised_f[l * 4 + m, p] = raised[p]
                vm.recip_f[at, pair] = recip
                vm.heads_f[at, pair] = (one_row(sums[p][:, :128]) * recip).astype(BF16)

        loop(4, fine_attend)
        mixed = vm.unit_x[level, :].astype(F32) + dot(vm.heads_f[level, :], ld.fine_out[...])
        ordered = dot(ld.to_part[...], mixed.astype(BF16))
        vm.send2[l] = ordered.astype(BF16).reshape(2, PART, 512)
        by_parity(
            lambda: start_all(second, second_near, even_sends, even_near, l),
            lambda: start_all(second, second_near, odd_sends, odd_near, l),
        )

    loop(2, fine_forward)

    own_cot.wait()
    partner_cot.wait()
    loads.coarse.wait()
    vm.cot16[:, :, :, :6, :] = vm.cot_raw[...]
    vm.cot[...] = dot(ld.coarse[...], vm.cot16[...].reshape(384, 1024)).astype(BF16)
    loads.coarse_out.wait()
    loads.merge.wait()
    loads.merge_weight.wait()
    loads.coarse_qkv.wait()
    loads.coarse_t.wait()

    def coarse_cot(t):
        cols = rows_at(t * 512, 512, 512)
        vm.grad_c[:, cols] = dot_nt(vm.cot[...], ld.coarse_out[cols, :])

    loop(2, coarse_cot)

    def gather(l):
        by_parity(
            lambda: take_all(second, second_near, even_takes, even_near, l),
            lambda: take_all(second, second_near, odd_takes, odd_near, l),
        )
        source = vm.quarters[l].reshape(4 * QUARTER, 512)
        for k in range(4):
            vm.hat_m[rows_at(l * 72, 72, 8), 512 * k : 512 * k + 512] = dot(ld.merge[k], source)

    loop(2, gather)

    def merge_norm(t):
        at = rows_at(t * 48, 48)
        hat, scale = normed_rows(vm.hat_m[at, :])
        vm.hat_m[at, :] = hat
        vm.scale_m[at, :] = jnp.broadcast_to(scale, (48, 128))
        vm.normed_m[at, :] = hat.astype(BF16)

    loop(3, merge_norm)

    def merge_project(t):
        cols = rows_at(t * 512, 512, 512)
        vm.merged[:, cols] = dot(vm.normed_m[...], ld.merge_weight[:, cols]).astype(BF16)

    loop(2, merge_project)

    def coarse_norm(t):
        at = rows_at(t * 48, 48)
        hat, scale = normed_rows(vm.merged[at, :].astype(F32))
        vm.hat_c[at, :] = hat
        vm.scale_c[at, :] = jnp.broadcast_to(scale, (48, 128))
        vm.normed_c[at, :] = hat.astype(BF16)

    loop(3, coarse_norm)

    def coarse_project(t):
        cols = rows_at(t * 512, 512, 512)
        scale = jnp.where(t < 2, 0.125, 1.0).astype(F32)
        vm.proj_c[:144, cols] = (dot(vm.normed_c[...], ld.coarse_qkv[:, cols]) * scale).astype(BF16)

    loop(6, coarse_project)

    def cols_at(p, base):
        return rows_at(p * 128 + base, 128, 128)

    def coarse_attend(t):
        pairs = [2 * t, 2 * t + 1]
        ones = jnp.ones((256, 128), BF16)
        scores = [
            dot_nt(two_heads(vm.proj_c[:144, cols_at(p, 0)], vm.heads2_c), vm.proj_c[:, cols_at(p, 1024)])
            + vm.bias_c[pl.ds(2 * p, 2)].reshape(288, 256)
            for p in pairs
        ]
        tops = [jnp.max(s, axis=-1, keepdims=True) for s in scores]
        raised = [jnp.exp(s - top).astype(BF16) for s, top in zip(scores, tops)]
        sums = [
            dot(e, jnp.concatenate([vm.proj_c[:, cols_at(p, 2048)], ones], axis=1))
            for e, p in zip(raised, pairs)
        ]
        for p, e, total in zip(pairs, raised, sums):
            recip = 1.0 / one_row(total[:, 128:])
            vm.raised_c[p] = e
            vm.recip_c[:, cols_at(p, 0)] = recip
            vm.heads_c[:, cols_at(p, 0)] = (one_row(total[:, :128]) * recip).astype(BF16)

    loop(4, coarse_attend)

    def coarse_mix(t):
        cols = rows_at(t * 512, 512, 512)
        mixed = dot(vm.heads_c[...], ld.coarse_out[:, cols])
        vm.result[:, cols] = (vm.merged[:, cols].astype(F32) + mixed).astype(BF16)
        grad = vm.grad_c[:, cols] * vm.recip_c[:, cols]
        vm.dheads_c[:, cols] = grad.astype(BF16)
        vm.dprod_c[:, cols] = (grad * vm.heads_c[:, cols].astype(F32)).astype(BF16)

    loop(2, coarse_mix)

    def spread_result(h):
        rows = dot(ld.coarse_t[rows_at(h * 192, 192), :], vm.result[...]).astype(BF16)
        vm.result16[h] = rows.reshape(2, 6, 16, 1024)[:, :, :6]

    loop(2, spread_result)
    into = result_ref.at[:, pl.ds(6 * odd, 6)]
    result_near = pltpu.make_async_copy(vm.result16.at[odd], into, near_sem.at[3, 0])
    result_far = remote(vm.result16.at[1 - odd], into, 13, 0, device(0, 1 - 2 * odd))
    result_near.start()
    result_far.start()

    def coarse_attend_grad(t):
        pairs = [2 * t, 2 * t + 1]
        minus = jnp.full((256, 128), -1.0, BF16)
        grads = [two_heads(vm.dheads_c[:, cols_at(p, 0)], vm.heads2_c) for p in pairs]
        prods = [two_heads(vm.dprod_c[:, cols_at(p, 0)], vm.heads2_c) for p in pairs]
        queries = [two_heads(vm.proj_c[:144, cols_at(p, 0)], vm.heads2_c) for p in pairs]
        inner = [
            dot_nt(
                jnp.concatenate([g, d], axis=1), jnp.concatenate([vm.proj_c[:, cols_at(p, 2048)], minus], axis=1)
            )
            for p, g, d in zip(pairs, grads, prods)
        ]
        dscores = [(vm.raised_c[p].astype(F32) * x).astype(BF16) for p, x in zip(pairs, inner)]
        for p, g, q, ds in zip(pairs, grads, queries, dscores):
            vm.dproj_c[:, cols_at(p, 2048)] = dot_tn(vm.raised_c[p], g)[:144].astype(BF16)
            dq = one_row(dot(ds, vm.proj_c[:, cols_at(p, 1024)]))
            vm.dproj_c[:, cols_at(p, 0)] = (dq * 0.125).astype(BF16)
            vm.dproj_c[:, cols_at(p, 1024)] = dot_tn(ds, q)[:144].astype(BF16)

    loop(4, coarse_attend_grad)

    def coarse_project_grad(t):
        cols = rows_at(t * 512, 512, 512)
        vm.grad_c[:, cols] = dot_nt(vm.dproj_c[...], ld.coarse_qkv[cols, :])

    loop(2, coarse_project_grad)

    def coarse_norm_grad(t):
        at = rows_at(t * 48, 48)
        grad = norm_grad(vm.grad_c[at, :], vm.hat_c[at, :], vm.scale_c[at, :1])
        vm.dmerged[at, :] = (vm.cot[at, :].astype(F32) + grad).astype(BF16)

    loop(3, coarse_norm_grad)

    def merge_project_grad(t):
        cols = rows_at(t * 512, 512, 512)
        vm.grad_m[:, cols] = dot_nt(vm.dmerged[...], ld.merge_weight[cols, :])

    loop(4, merge_project_grad)
    loads.merge_t.wait()

    def third(l, kind, half, sem, q, to):
        at, size, into = kind
        return remote(
            vm.send3.at[l, q, pl.ds(into, size)], vm.part.at[l, half, pl.ds(at, size)], sem, l, device(*to)
        )

    def third_near(l, kind, half, sem, q):
        at, size, into = kind
        return pltpu.make_async_copy(
            vm.send3.at[l, q, pl.ds(into, size)], vm.part.at[l, half, pl.ds(at, size)], near_sem.at[sem, l]
        )

    even_back = [
        (own, 1, 15, 0, (0, -1)), (own, 0, 14, 3, (0, 1)), (before, 1, 19, 0, (-1, -1)),
        (before, 0, 18, 1, (-1, 0)), (before, 1, 20, 2, (-1, 0)), (before, 0, 21, 3, (-1, 1)),
    ]
    even_back_near = [(own, 0, 4, 1), (own, 1, 5, 2)]
    even_back_takes = [
        (next_, 0, 16, 0, side), (next_, 1, 17, 0, side), (before, 0, 18, 0, side), (before, 1, 20, 0, side),
    ]
    odd_back = [(next_, 1, 22, 0, (0, -2)), (next_, 0, 16, 1, (0, -1)), (next_, 1, 17, 2, (0, -1))]
    odd_back_near = [(next_, 0, 4, 3)]
    odd_back_takes = [
        (own, 0, 14, 0, side), (own, 1, 15, 0, side), (next_, 1, 22, 0, side), (before, 0, 21, 0, side),
        (before, 1, 19, 0, side),
    ]

    def scatter(l):
        at = rows_at(l * 72, 72, 8)
        grad = norm_grad(vm.grad_m[at, :], vm.hat_m[at, :], vm.scale_m[at, :1]).astype(BF16)
        total = dot(ld.merge_t[0], grad[:, :512])
        for k in range(1, 4):
            total = total + dot(ld.merge_t[k], grad[:, 512 * k : 512 * k + 512])
        vm.send3[l] = total.astype(BF16).reshape(4, QUARTER, 512)
        by_parity(
            lambda: start_all(third, third_near, even_back, even_back_near, l),
            lambda: start_all(third, third_near, odd_back, odd_back_near, l),
        )

    loop(2, scatter)
    loads.to_part_t.wait()
    loads.to_unit_t.wait()
    loads.to_region_t.wait()

    def fourth(l):
        return [
            remote(
                vm.send4.at[l, pl.ds(at, size)],
                vm.region4.at[l, pl.ds(128 + at, size)],
                23 + n,
                l,
                device(-to[0], -to[1]),
            )
            for n, (at, size, to) in enumerate(pieces)
        ]

    def fine_backward(l):
        base = l * 320
        level = rows_at(base, 320)
        by_parity(
            lambda: take_all(third, third_near, even_back_takes, even_back_near, l),
            lambda: take_all(third, third_near, odd_back_takes, odd_back_near, l),
        )
        vm.dmixed[level, :] = dot(ld.to_part_t[...], vm.part[l].reshape(2 * PART, 512)).astype(BF16)
        grad = dot_nt(vm.dmixed[level, :], ld.fine_out[...]) * vm.recip_f[level, :]
        vm.dheads_f[level, :] = grad.astype(BF16)
        vm.dprod_f[level, :] = (grad * vm.heads_f[level, :].astype(F32)).astype(BF16)

        def fine_attend_grad(m):
            at, wide = rows_at(base + m * UNIT, UNIT), rows_at(base + m * UNIT, 128)
            pairs = [slice(128 * p, 128 * p + 128) for p in range(4)]
            minus = jnp.full((128, 128), -1.0, BF16)
            grads = [two_heads(vm.dheads_f[at, pair], vm.heads2) for pair in pairs]
            prods = [two_heads(vm.dprod_f[at, pair], vm.heads2) for pair in pairs]
            queries = [two_heads(vm.proj[at, pair], vm.heads2) for pair in pairs]
            inner = [
                dot_nt(
                    jnp.concatenate([g, d], axis=1),
                    jnp.concatenate([vm.proj[wide, 1024 + pair.start : 1024 + pair.stop], minus], axis=1),
                )
                for pair, g, d in zip(pairs, grads, prods)
            ]
            raised = [vm.raised_f[l * 4 + m, p] for p in range(4)]
            dscores = [(e.astype(F32) * x).astype(BF16) for e, x in zip(raised, inner)]
            dvalues = [dot_tn(e, g) for e, g in zip(raised, grads)]
            dkeys = [dot_tn(ds, q) for ds, q in zip(dscores, queries)]
            dqueries = [
                dot(ds, vm.proj[wide, 512 + pair.start : 512 + pair.stop]) for pair, ds in zip(pairs, dscores)
            ]
            for p, pair in enumerate(pairs):
                vm.dproj_f[at, pair] = (one_row(dqueries[p]) * 0.125).astype(BF16)
                vm.dproj_f[at, 512 + pair.start : 512 + pair.stop] = dkeys[p][:UNIT].astype(BF16)
                vm.dproj_f[at, 1024 + pair.start : 1024 + pair.stop] = dvalues[p][:UNIT].astype(BF16)

        loop(4, fine_attend_grad)
        grad = dot_nt(vm.dproj_f[level, :], ld.fine_qkv[...])
        grad = norm_grad(grad, vm.hat_f[level, :], vm.scale_f[level, :1])
        dunit = (vm.dmixed[level, :].astype(F32) + grad).astype(BF16)
        ordered = dot(ld.to_unit_t[...], dunit).astype(BF16)
        vm.region4[l, :128, :] = ordered[:128]
        vm.send4[l] = ordered[128:]
        for copy in fourth(l):
            copy.start()

    loop(2, fine_backward)
    result_near.wait()
    result_far.wait()

    def grid_back(l):
        for copy in fourth(l):
            copy.wait()
        rows = dot(ld.to_region_t[...], vm.region4[l]).astype(BF16)
        grad_ref[l] = rows.reshape(24, 16, 512)[:, :12]
        by_parity(
            lambda: (sent_all(second, even_sends, l), sent_all(third, even_back, l)),
            lambda: (sent_all(second, odd_sends, l), sent_all(third, odd_back, l)),
        )

    loop(2, grid_back)


def per_device(n_lat, n_lon, *args):
    operands = list(args) + [jnp.asarray(m) for m in row_orders()]
    shapes = dict(zip(ARGS, [(x.shape, x.dtype) for x in operands]))
    loaded = [
        pltpu.VMEM(shapes[name][0][1:] if paired else shapes[name][0], shapes[name][1])
        for name, paired in LOADED.items()
    ]
    return pl.pallas_call(
        functools.partial(kernel, n_lat, n_lon),
        out_shape=(
            jax.ShapeDtypeStruct((2, 12, 6, 1024), BF16),
            jax.ShapeDtypeStruct((2, 24, 12, 512), BF16),
        ),
        in_specs=[
            pl.BlockSpec(memory_space=pltpu.VMEM if placed == 1 else pl.ANY) for placed in ARGS.values()
        ],
        out_specs=(pl.BlockSpec(memory_space=pltpu.VMEM), pl.BlockSpec(memory_space=pltpu.VMEM)),
        scratch_shapes=[pltpu.VMEM(*spec) for spec in SCRATCH.values()]
        + loaded
        + [
            pltpu.SemaphoreType.DMA((len(LOADED),)),
            pltpu.SemaphoreType.DMA((26, 2)),
            pltpu.SemaphoreType.DMA((26, 2)),
            pltpu.SemaphoreType.DMA((6, 2)),
        ],
        compiler_params=pltpu.CompilerParams(
            collective_id=0, has_side_effects=True, vmem_limit_bytes=60 * 2**20
        ),
    )(*operands)


def solution(mesh):
    grid = P(None, "lat", "lon", None)
    placed = (grid, P(None, "lat", "lon"), P(), P(), P(), P(), P(), P(), P(), grid)
    return jax.shard_map(
        functools.partial(per_device, mesh.shape["lat"], mesh.shape["lon"]),
        mesh=mesh,
        in_specs=placed,
        out_specs=(grid, grid),
        check_vma=False,
    )
```

```python
import functools

import jax
import jax.numpy as jnp
import numpy as np
from jax import lax
from jax.experimental import pallas as pl
from jax.experimental.pallas import tpu as pltpu
from jax.sharding import PartitionSpec as P

F32 = jnp.float32
BF16 = jnp.bfloat16
EPSILON = 1e-05
MASKED = -1e30
MESH = pl.DeviceIdType.MESH

UNIT = 80
PART = 176
QUARTER = 96
NEIGHBOURS = [(a, b) for a in (-1, 0, 1) for b in (-1, 0, 1) if (a, b) != (0, 0)] + [(0, 2), (0, -2)]


def one_hot(pairs, rows, columns):
    out = np.zeros((rows, columns), np.float32)
    for r, c in pairs:
        out[r, c] = 1.0
    return out


def region_of(row, col):
    if row >= 3:
        return (row - 3) * 6 + col - 6 if col >= 6 else 128 + (row - 3) * 6 + col
    return 256 + row * 6 + col - 6 if col >= 6 else 288 + row * 6 + col


def part_of(s, o):
    half, c = divmod(o, 6)
    if s < 9:
        at = s * 6 + c
    elif s < 21:
        at = 64 + (s - 9) * 6 + c
    else:
        at = 144 + (s - 21) * 6 + c
    return half * PART + at


@functools.cache
def row_orders():
    to_region = one_hot([(region_of(r, c), c * 24 + r) for r in range(24) for c in range(12)], 320, 288)
    unit_pairs, part_pairs = [], []
    for s in range(24):
        for o in range(12):
            unit = UNIT * (s // 6) + 12 * (s % 6) + o
            unit_pairs.append((unit, region_of((s + 3) % 24, (o + 6) % 12)))
            part_pairs.append((part_of(s, o), unit))
    to_unit = one_hot(unit_pairs, 320, 320)
    to_part = one_hot(part_pairs, 2 * PART, 320)
    merge = np.zeros((2, 4, 72, 4 * QUARTER), np.float32)
    for u in range(2):
        for k, (dr, dc) in enumerate([(0, 0), (1, 0), (0, 1), (1, 1)]):
            for r in range(6):
                for c in range(12):
                    quarter, col = divmod(2 * c + dc, 6)
                    s = 12 * u + 2 * r + dr - 3
                    if u == 1:
                        at = (s - 9) * 6 + col
                    else:
                        at = 64 + (s + 3) * 6 + col if s < 0 else s * 6 + col
                    merge[u, k, r * 12 + c, quarter * QUARTER + at] = 1.0
    coarse = one_hot(
        [
            (l * 72 + r * 12 + c, (((c // 6) * 6 + r) * 6 + c % 6) * 2 + l)
            for l in range(2)
            for r in range(6)
            for c in range(12)
        ],
        144,
        144,
    )
    id_row = one_hot([(t, t // 12 + 18) for t in range(72)], UNIT, 24)
    id_col = one_hot([(t, t % 12) for t in range(72)], UNIT, 12)
    both = lambda m: [m, np.swapaxes(m, -1, -2)]
    orders = both(to_region) + both(to_unit) + both(to_part) + both(merge) + both(coarse)
    return [np.ascontiguousarray(m).astype(jnp.bfloat16) for m in orders] + [id_row, id_col]


def dot(a, b):
    return lax.dot_general(a, b, (((1,), (0,)), ((), ())), preferred_element_type=F32)


def dot_nt(a, b):
    return lax.dot_general(a, b, (((1,), (1,)), ((), ())), preferred_element_type=F32)


def dot_tn(a, b):
    return lax.dot_general(a, b, (((0,), (0,)), ((), ())), preferred_element_type=F32)


def normed_rows(x):
    center = x - jnp.mean(x, axis=-1, keepdims=True)
    scale = lax.rsqrt(jnp.mean(center * center, axis=-1, keepdims=True) + EPSILON)
    return center * scale, scale


def norm_grad(grad, hat, scale):
    inner = jnp.mean(grad * hat, axis=-1, keepdims=True)
    return scale * (grad - jnp.mean(grad, axis=-1, keepdims=True) - hat * inner)


def one_row(x):
    span = x.shape[0] // 2
    low = lax.broadcasted_iota(jnp.int32, (span, 128), 1) < 64
    return jnp.where(low, x[:span], x[span:])


def rows_at(start, size, unit=16):
    return pl.ds(pl.multiple_of(start, unit), size)


def loop(count, body):
    lax.fori_loop(0, count, lambda t, c: (body(t), c)[1], 0)


class Box:
    def __init__(self, **fields):
        self.__dict__.update(fields)


ARGS = dict(
    tokens=0, mask_ids=1, fine_bias=0, fine_qkv=0, fine_out=0, merge_weight=0, coarse_bias=0, coarse_qkv=0,
    coarse_out=0, cotangent=2, to_region=0, to_region_t=0, to_unit=0, to_unit_t=0, to_part=0, to_part_t=0,
    merge=0, merge_t=0, coarse=0, coarse_t=0, id_row=1, id_col=1,
)
LOADED = dict(
    tokens=0, to_region=0, fine_bias=0, coarse=0, coarse_bias=0, coarse_out=0, to_unit=0, fine_qkv=0, fine_out=0,
    to_part=0, merge=1, merge_weight=0, coarse_qkv=0, coarse_t=0, merge_t=1, to_part_t=0, to_unit_t=0,
    to_region_t=0,
)
SCRATCH = dict(
    heads2=((160, 128), BF16),
    heads2_c=((288, 128), BF16),
    send1=((2, 192, 512), BF16),
    region=((2, 320, 512), BF16),
    unit_x=((640, 512), BF16),
    unit_n=((640, 512), BF16),
    hat_f=((640, 512), F32),
    scale_f=((640, 128), F32),
    proj=((704, 1536), BF16),
    bias_f=((2, 2, 4, 160, 128), F32),
    raised_f=((8, 4, 160, 128), BF16),
    recip_f=((640, 512), F32),
    heads_f=((640, 512), BF16),
    send2=((2, 2, PART, 512), BF16),
    quarters=((2, 4, QUARTER, 512), BF16),
    hat_m=((144, 2048), F32),
    scale_m=((144, 128), F32),
    normed_m=((144, 2048), BF16),
    merged=((144, 1024), BF16),
    hat_c=((144, 1024), F32),
    scale_c=((144, 128), F32),
    normed_c=((144, 1024), BF16),
    proj_c=((256, 3072), BF16),
    bias_c=((16, 144, 256), F32),
    raised_c=((8, 288, 256), BF16),
    recip_c=((144, 1024), F32),
    heads_c=((144, 1024), BF16),
    result=((144, 1024), BF16),
    result2=((2, 6, 6, 2, 1024), BF16),
    cot2=((2, 6, 6, 2, 1024), BF16),
    cot=((144, 1024), BF16),
    dheads_c=((144, 1024), BF16),
    dprod_c=((144, 1024), BF16),
    dproj_c=((144, 3072), BF16),
    grad_c=((144, 1024), F32),
    dmerged=((144, 1024), BF16),
    grad_m=((144, 2048), F32),
    send3=((2, 4, QUARTER, 512), BF16),
    part=((2, 2, PART, 512), BF16),
    dmixed=((640, 512), BF16),
    dheads_f=((640, 512), BF16),
    dprod_f=((640, 512), BF16),
    dproj_f=((640, 1536), BF16),
    send4=((2, 192, 512), BF16),
    region4=((2, 320, 512), BF16),
)
def kernel(n_lat, n_lon, *refs):
    rest = list(refs)
    hbm = Box(**{name: rest.pop(0) for name in ARGS})
    result_ref, grad_ref = rest.pop(0), rest.pop(0)
    vm = Box(**{name: rest.pop(0) for name in SCRATCH})
    ld = Box(**{name: rest.pop(0) for name in LOADED})
    load_sem, send_sem, recv_sem, near_sem = rest

    i, j = lax.axis_index("lat"), lax.axis_index("lon")
    odd = lax.rem(j, 2)
    even = odd == 0

    def device(di, dj):
        return (lax.rem(i + di + n_lat, n_lat), lax.rem(j + dj + n_lon, n_lon))

    def remote(src, dst, sem, l, target):
        return pltpu.make_async_remote_copy(
            src_ref=src,
            dst_ref=dst,
            send_sem=send_sem.at[sem, l],
            recv_sem=recv_sem.at[sem, l],
            device_id=target,
            device_id_type=MESH,
        )

    vm.quarters[:, :, 80:, :] = jnp.zeros((2, 4, QUARTER - 80, 512), BF16)
    barrier = pltpu.get_barrier_semaphore()
    for di, dj in NEIGHBOURS:
        pl.semaphore_signal(barrier, inc=1, device_id=device(di, dj), device_id_type=MESH)

    loads = Box()
    for at, (name, paired) in enumerate(LOADED.items()):
        src = getattr(hbm, name)
        if paired:
            src = src.at[odd]
        copy = pltpu.make_async_copy(src, getattr(ld, name), load_sem.at[at])
        copy.start()
        setattr(loads, name, copy)
    own_cot = pltpu.make_async_copy(
        hbm.cotangent.at[pl.ds(6 * odd, 6)], vm.cot2.at[odd], near_sem.at[0, 0]
    )
    own_cot.start()

    for end in (320, 640):
        vm.proj[end : end + 64, :] = jnp.zeros((64, 1536), BF16)
    vm.proj_c[144:, :] = jnp.zeros((112, 3072), BF16)
    for ref in (vm.heads2, vm.heads2_c):
        low = lax.broadcasted_iota(jnp.int32, ref.shape, 1) < 64
        first = lax.broadcasted_iota(jnp.int32, ref.shape, 0) < ref.shape[0] // 2
        ref[...] = jnp.where(low == first, 1.0, 0.0).astype(BF16)

    def two_heads(x, mask):
        return jnp.concatenate([x, x], axis=0) * mask[...]

    loads.tokens.wait()
    loads.to_region.wait()
    pl.semaphore_wait(barrier, len(NEIGHBOURS))
    pieces = [(0, 128, (0, -1)), (128, 32, (-1, 0)), (160, 32, (-1, -1))]

    def first(l):
        return [
            remote(
                vm.send1.at[l, pl.ds(at, size)], vm.region.at[l, pl.ds(128 + at, size)], n, l, device(*to)
            )
            for n, (at, size, to) in enumerate(pieces)
        ]

    def regions(l):
        ordered = dot(ld.to_region[...], ld.tokens[l]).astype(BF16)
        vm.region[l, :128, :] = ordered[:128]
        vm.send1[l] = ordered[128:]
        for copy in first(l):
            copy.start()

    loop(2, regions)
    partner_cot = remote(
        hbm.cotangent.at[pl.ds(6 - 6 * odd, 6)], vm.cot2.at[odd], 3, 0, device(0, 1 - 2 * odd)
    )
    partner_cot.start()

    loads.fine_bias.wait()
    lanes = lax.broadcasted_iota(jnp.int32, (UNIT, 128), 1)
    subs = lax.broadcasted_iota(jnp.int32, (UNIT, 128), 0)
    past = jnp.where(lanes >= 72, MASKED, 0.0).astype(F32)
    for level in range(2):
        spread = dot(hbm.id_col[...], hbm.mask_ids[:, level, :].astype(F32))
        id_of = jnp.sum(spread * hbm.id_row[...], axis=-1, keepdims=True)
        id_at = dot(jnp.ones((8, UNIT), F32), jnp.where(lanes == subs, id_of, 0.0))[:1]
        apart = jnp.where(id_of == id_at, past, MASKED)
        for head in range(8):
            span = slice(72 * level, 72 * level + 72)
            block = ld.fine_bias[head, span, span]
            block = jnp.concatenate([block, jnp.zeros((72, 56), F32)], axis=1)
            block = jnp.concatenate([block, jnp.zeros((8, 128), F32)], axis=0)
            at = slice(UNIT * (head % 2), UNIT * (head % 2) + UNIT)
            vm.bias_f[0, level, head // 2, at, :] = block + past
            vm.bias_f[1, level, head // 2, at, :] = block + apart

    loads.coarse_bias.wait()

    def coarse_pad(h):
        vm.bias_c[h] = jnp.concatenate([ld.coarse_bias[h], jnp.full((144, 112), MASKED, F32)], axis=1)

    loop(16, coarse_pad)
    own_cot.wait()
    partner_cot.wait()
    loads.coarse.wait()
    vm.cot[...] = dot(ld.coarse[...], vm.cot2[...].reshape(144, 1024)).astype(BF16)
    loads.coarse_out.wait()

    def coarse_cot(t):
        cols = rows_at(t * 512, 512, 512)
        vm.grad_c[:, cols] = dot_nt(vm.cot[...], ld.coarse_out[cols, :])

    loop(2, coarse_cot)
    loads.to_unit.wait()
    loads.fine_qkv.wait()
    loads.fine_out.wait()
    loads.to_part.wait()

    own, next_, before = (0, 64, 0), (64, 80, 0), (144, 32, 64)

    def second(l, kind, half, sem, q, to):
        at, size, into = kind
        return remote(
            vm.send2.at[l, half, pl.ds(at, size)], vm.quarters.at[l, q, pl.ds(into, size)], sem, l, device(*to)
        )

    def second_near(l, kind, half, sem, q):
        at, size, into = kind
        return pltpu.make_async_copy(
            vm.send2.at[l, half, pl.ds(at, size)], vm.quarters.at[l, q, pl.ds(into, size)], near_sem.at[sem, l]
        )

    side = (0, 1)
    even_sends = [
        (next_, 0, 5, 1, (0, 1)), (next_, 1, 6, 2, (0, 1)), (before, 0, 9, 1, (1, 0)), (before, 1, 10, 2, (1, 0)),
    ]
    even_near = [(own, 0, 1, 1), (own, 1, 2, 2)]
    even_takes = [
        (own, 0, 4, 0, side), (own, 0, 7, 3, side), (before, 0, 8, 0, side), (before, 0, 9, 1, side),
        (before, 0, 10, 2, side), (before, 0, 11, 3, side),
    ]
    odd_sends = [
        (own, 1, 4, 0, (0, 1)), (next_, 1, 12, 0, (0, 2)), (before, 1, 8, 0, (1, 1)), (own, 0, 7, 3, (0, -1)),
        (before, 0, 11, 3, (1, -1)),
    ]
    odd_near = [(next_, 0, 1, 3)]
    odd_takes = [(next_, 0, 12, 0, side), (next_, 0, 5, 1, side), (next_, 0, 6, 2, side)]

    def by_parity(of_even, of_odd):
        @pl.when(even)
        def _():
            of_even()

        @pl.when(odd == 1)
        def _():
            of_odd()

    def start_all(far, near, far_list, near_list, l):
        for args in far_list:
            far(l, *args).start()
        for args in near_list:
            near(l, *args).start()

    def take_all(far, near, take_list, near_list, l):
        for args in near_list:
            near(l, *args).wait()
        for args in take_list:
            far(l, *args).wait_recv()

    def sent_all(far, far_list, l):
        for args in far_list:
            far(l, *args).wait_send()

    def fine_forward(l):
        base = l * 320
        level = rows_at(base, 320)
        for copy in first(l):
            copy.wait()
        vm.unit_x[level, :] = dot(ld.to_unit[...], vm.region[l]).astype(BF16)

        def fine_norm(t):
            at = rows_at(base + t * 80, 80)
            hat, scale = normed_rows(vm.unit_x[at, :].astype(F32))
            vm.hat_f[at, :] = hat
            vm.scale_f[at, :] = jnp.broadcast_to(scale, (80, 128))
            vm.unit_n[at, :] = hat.astype(BF16)

        loop(4, fine_norm)

        def fine_project(t):
            cols = rows_at(t * 512, 512, 512)
            scale = jnp.where(t < 1, 0.125, 1.0).astype(F32)
            vm.proj[level, cols] = (dot(vm.unit_n[level, :], ld.fine_qkv[:, cols]) * scale).astype(BF16)

        loop(3, fine_project)

        def fine_attend(m):
            last = lax.div(m, 3)
            at, wide = rows_at(base + m * UNIT, UNIT), rows_at(base + m * UNIT, 128)
            pairs = [slice(128 * p, 128 * p + 128) for p in range(4)]
            ones = jnp.ones((128, 128), BF16)
            scores = [
                dot_nt(two_heads(vm.proj[at, pair], vm.heads2), vm.proj[wide, 512 + pair.start : 512 + pair.stop])
                + vm.bias_f[last, 1 - l, p]
                for p, pair in enumerate(pairs)
            ]
            tops = [jnp.max(s, axis=-1, keepdims=True) for s in scores]
            raised = [jnp.exp(s - t).astype(BF16) for s, t in zip(scores, tops)]
            sums = [
                dot(e, jnp.concatenate([vm.proj[wide, 1024 + pair.start : 1024 + pair.stop], ones], axis=1))
                for e, pair in zip(raised, pairs)
            ]
            for p, pair in enumerate(pairs):
                recip = 1.0 / one_row(sums[p][:, 128:])
                vm.raised_f[l * 4 + m, p] = raised[p]
                vm.recip_f[at, pair] = recip
                vm.heads_f[at, pair] = (one_row(sums[p][:, :128]) * recip).astype(BF16)

        loop(4, fine_attend)
        mixed = vm.unit_x[level, :].astype(F32) + dot(vm.heads_f[level, :], ld.fine_out[...])
        ordered = dot(ld.to_part[...], mixed.astype(BF16))
        vm.send2[l] = ordered.astype(BF16).reshape(2, PART, 512)
        by_parity(
            lambda: start_all(second, second_near, even_sends, even_near, l),
            lambda: start_all(second, second_near, odd_sends, odd_near, l),
        )

    loop(2, fine_forward)

    loads.merge.wait()
    loads.merge_weight.wait()
    loads.coarse_qkv.wait()
    loads.coarse_t.wait()

    def gather(l):
        by_parity(
            lambda: take_all(second, second_near, even_takes, even_near, l),
            lambda: take_all(second, second_near, odd_takes, odd_near, l),
        )
        source = vm.quarters[l].reshape(4 * QUARTER, 512)
        for k in range(4):
            vm.hat_m[rows_at(l * 72, 72, 8), 512 * k : 512 * k + 512] = dot(ld.merge[k], source)

    loop(2, gather)

    def merge_norm(t):
        at = rows_at(t * 48, 48)
        hat, scale = normed_rows(vm.hat_m[at, :])
        vm.hat_m[at, :] = hat
        vm.scale_m[at, :] = jnp.broadcast_to(scale, (48, 128))
        vm.normed_m[at, :] = hat.astype(BF16)

    loop(3, merge_norm)

    def merge_project(t):
        cols = rows_at(t * 512, 512, 512)
        vm.merged[:, cols] = dot(vm.normed_m[...], ld.merge_weight[:, cols]).astype(BF16)

    loop(2, merge_project)

    def coarse_norm(t):
        at = rows_at(t * 48, 48)
        hat, scale = normed_rows(vm.merged[at, :].astype(F32))
        vm.hat_c[at, :] = hat
        vm.scale_c[at, :] = jnp.broadcast_to(scale, (48, 128))
        vm.normed_c[at, :] = hat.astype(BF16)

    loop(3, coarse_norm)

    def coarse_project(t):
        cols = rows_at(t * 512, 512, 512)
        scale = jnp.where(t < 2, 0.125, 1.0).astype(F32)
        vm.proj_c[:144, cols] = (dot(vm.normed_c[...], ld.coarse_qkv[:, cols]) * scale).astype(BF16)

    loop(6, coarse_project)

    def cols_at(p, base):
        return rows_at(p * 128 + base, 128, 128)

    def coarse_attend(t):
        pairs = [2 * t, 2 * t + 1]
        ones = jnp.ones((256, 128), BF16)
        scores = [
            dot_nt(two_heads(vm.proj_c[:144, cols_at(p, 0)], vm.heads2_c), vm.proj_c[:, cols_at(p, 1024)])
            + vm.bias_c[pl.ds(2 * p, 2)].reshape(288, 256)
            for p in pairs
        ]
        tops = [jnp.max(s, axis=-1, keepdims=True) for s in scores]
        raised = [jnp.exp(s - top).astype(BF16) for s, top in zip(scores, tops)]
        sums = [
            dot(e, jnp.concatenate([vm.proj_c[:, cols_at(p, 2048)], ones], axis=1))
            for e, p in zip(raised, pairs)
        ]
        for p, e, total in zip(pairs, raised, sums):
            recip = 1.0 / one_row(total[:, 128:])
            vm.raised_c[p] = e
            vm.recip_c[:, cols_at(p, 0)] = recip
            vm.heads_c[:, cols_at(p, 0)] = (one_row(total[:, :128]) * recip).astype(BF16)

    loop(4, coarse_attend)

    def coarse_mix(t):
        cols = rows_at(t * 512, 512, 512)
        mixed = dot(vm.heads_c[...], ld.coarse_out[:, cols])
        vm.result[:, cols] = (vm.merged[:, cols].astype(F32) + mixed).astype(BF16)
        grad = vm.grad_c[:, cols] * vm.recip_c[:, cols]
        vm.dheads_c[:, cols] = grad.astype(BF16)
        vm.dprod_c[:, cols] = (grad * vm.heads_c[:, cols].astype(F32)).astype(BF16)

    loop(2, coarse_mix)

    vm.result2[...] = dot(ld.coarse_t[...], vm.result[...]).astype(BF16).reshape(2, 6, 6, 2, 1024)
    into = result_ref.at[pl.ds(6 * odd, 6)]
    result_near = pltpu.make_async_copy(vm.result2.at[odd], into, near_sem.at[3, 0])
    result_far = remote(vm.result2.at[1 - odd], into, 13, 0, device(0, 1 - 2 * odd))
    result_near.start()
    result_far.start()

    def coarse_attend_grad(t):
        pairs = [2 * t, 2 * t + 1]
        minus = jnp.full((256, 128), -1.0, BF16)
        grads = [two_heads(vm.dheads_c[:, cols_at(p, 0)], vm.heads2_c) for p in pairs]
        prods = [two_heads(vm.dprod_c[:, cols_at(p, 0)], vm.heads2_c) for p in pairs]
        queries = [two_heads(vm.proj_c[:144, cols_at(p, 0)], vm.heads2_c) for p in pairs]
        inner = [
            dot_nt(
                jnp.concatenate([g, d], axis=1), jnp.concatenate([vm.proj_c[:, cols_at(p, 2048)], minus], axis=1)
            )
            for p, g, d in zip(pairs, grads, prods)
        ]
        dscores = [(vm.raised_c[p].astype(F32) * x).astype(BF16) for p, x in zip(pairs, inner)]
        for p, g, q, ds in zip(pairs, grads, queries, dscores):
            vm.dproj_c[:, cols_at(p, 2048)] = dot_tn(vm.raised_c[p], g)[:144].astype(BF16)
            dq = one_row(dot(ds, vm.proj_c[:, cols_at(p, 1024)]))
            vm.dproj_c[:, cols_at(p, 0)] = (dq * 0.125).astype(BF16)
            vm.dproj_c[:, cols_at(p, 1024)] = dot_tn(ds, q)[:144].astype(BF16)

    loop(4, coarse_attend_grad)

    def coarse_project_grad(t):
        cols = rows_at(t * 512, 512, 512)
        vm.grad_c[:, cols] = dot_nt(vm.dproj_c[...], ld.coarse_qkv[cols, :])

    loop(2, coarse_project_grad)

    def coarse_norm_grad(t):
        at = rows_at(t * 48, 48)
        grad = norm_grad(vm.grad_c[at, :], vm.hat_c[at, :], vm.scale_c[at, :1])
        vm.dmerged[at, :] = (vm.cot[at, :].astype(F32) + grad).astype(BF16)

    loop(3, coarse_norm_grad)

    def merge_project_grad(t):
        cols = rows_at(t * 512, 512, 512)
        vm.grad_m[:, cols] = dot_nt(vm.dmerged[...], ld.merge_weight[cols, :])

    loop(4, merge_project_grad)
    loads.merge_t.wait()

    def third(l, kind, half, sem, q, to):
        at, size, into = kind
        return remote(
            vm.send3.at[l, q, pl.ds(into, size)], vm.part.at[l, half, pl.ds(at, size)], sem, l, device(*to)
        )

    def third_near(l, kind, half, sem, q):
        at, size, into = kind
        return pltpu.make_async_copy(
            vm.send3.at[l, q, pl.ds(into, size)], vm.part.at[l, half, pl.ds(at, size)], near_sem.at[sem, l]
        )

    even_back = [
        (own, 1, 15, 0, (0, -1)), (own, 0, 14, 3, (0, 1)), (before, 1, 19, 0, (-1, -1)),
        (before, 0, 18, 1, (-1, 0)), (before, 1, 20, 2, (-1, 0)), (before, 0, 21, 3, (-1, 1)),
    ]
    even_back_near = [(own, 0, 4, 1), (own, 1, 5, 2)]
    even_back_takes = [
        (next_, 0, 16, 0, side), (next_, 1, 17, 0, side), (before, 0, 18, 0, side), (before, 1, 20, 0, side),
    ]
    odd_back = [(next_, 1, 22, 0, (0, -2)), (next_, 0, 16, 1, (0, -1)), (next_, 1, 17, 2, (0, -1))]
    odd_back_near = [(next_, 0, 4, 3)]
    odd_back_takes = [
        (own, 0, 14, 0, side), (own, 1, 15, 0, side), (next_, 1, 22, 0, side), (before, 0, 21, 0, side),
        (before, 1, 19, 0, side),
    ]

    def scatter(l):
        at = rows_at(l * 72, 72, 8)
        grad = norm_grad(vm.grad_m[at, :], vm.hat_m[at, :], vm.scale_m[at, :1]).astype(BF16)
        total = dot(ld.merge_t[0], grad[:, :512])
        for k in range(1, 4):
            total = total + dot(ld.merge_t[k], grad[:, 512 * k : 512 * k + 512])
        vm.send3[l] = total.astype(BF16).reshape(4, QUARTER, 512)
        by_parity(
            lambda: start_all(third, third_near, even_back, even_back_near, l),
            lambda: start_all(third, third_near, odd_back, odd_back_near, l),
        )

    loop(2, scatter)
    loads.to_part_t.wait()
    loads.to_unit_t.wait()
    loads.to_region_t.wait()

    def fourth(l):
        return [
            remote(
                vm.send4.at[l, pl.ds(at, size)],
                vm.region4.at[l, pl.ds(128 + at, size)],
                23 + n,
                l,
                device(-to[0], -to[1]),
            )
            for n, (at, size, to) in enumerate(pieces)
        ]

    def fine_backward(l):
        base = l * 320
        level = rows_at(base, 320)
        by_parity(
            lambda: take_all(third, third_near, even_back_takes, even_back_near, l),
            lambda: take_all(third, third_near, odd_back_takes, odd_back_near, l),
        )
        vm.dmixed[level, :] = dot(ld.to_part_t[...], vm.part[l].reshape(2 * PART, 512)).astype(BF16)
        grad = dot_nt(vm.dmixed[level, :], ld.fine_out[...]) * vm.recip_f[level, :]
        vm.dheads_f[level, :] = grad.astype(BF16)
        vm.dprod_f[level, :] = (grad * vm.heads_f[level, :].astype(F32)).astype(BF16)

        def fine_attend_grad(m):
            at, wide = rows_at(base + m * UNIT, UNIT), rows_at(base + m * UNIT, 128)
            pairs = [slice(128 * p, 128 * p + 128) for p in range(4)]
            minus = jnp.full((128, 128), -1.0, BF16)
            grads = [two_heads(vm.dheads_f[at, pair], vm.heads2) for pair in pairs]
            prods = [two_heads(vm.dprod_f[at, pair], vm.heads2) for pair in pairs]
            queries = [two_heads(vm.proj[at, pair], vm.heads2) for pair in pairs]
            inner = [
                dot_nt(
                    jnp.concatenate([g, d], axis=1),
                    jnp.concatenate([vm.proj[wide, 1024 + pair.start : 1024 + pair.stop], minus], axis=1),
                )
                for pair, g, d in zip(pairs, grads, prods)
            ]
            raised = [vm.raised_f[l * 4 + m, p] for p in range(4)]
            dscores = [(e.astype(F32) * x).astype(BF16) for e, x in zip(raised, inner)]
            dvalues = [dot_tn(e, g) for e, g in zip(raised, grads)]
            dkeys = [dot_tn(ds, q) for ds, q in zip(dscores, queries)]
            dqueries = [
                dot(ds, vm.proj[wide, 512 + pair.start : 512 + pair.stop]) for pair, ds in zip(pairs, dscores)
            ]
            for p, pair in enumerate(pairs):
                vm.dproj_f[at, pair] = (one_row(dqueries[p]) * 0.125).astype(BF16)
                vm.dproj_f[at, 512 + pair.start : 512 + pair.stop] = dkeys[p][:UNIT].astype(BF16)
                vm.dproj_f[at, 1024 + pair.start : 1024 + pair.stop] = dvalues[p][:UNIT].astype(BF16)

        loop(4, fine_attend_grad)
        grad = dot_nt(vm.dproj_f[level, :], ld.fine_qkv[...])
        grad = norm_grad(grad, vm.hat_f[level, :], vm.scale_f[level, :1])
        dunit = (vm.dmixed[level, :].astype(F32) + grad).astype(BF16)
        ordered = dot(ld.to_unit_t[...], dunit).astype(BF16)
        vm.region4[l, :128, :] = ordered[:128]
        vm.send4[l] = ordered[128:]
        for copy in fourth(l):
            copy.start()

    loop(2, fine_backward)
    result_near.wait()
    result_far.wait()

    def grid_back(l):
        for copy in fourth(l):
            copy.wait()
        grad_ref[l] = dot(ld.to_region_t[...], vm.region4[l]).astype(BF16)
        by_parity(
            lambda: (sent_all(second, even_sends, l), sent_all(third, even_back, l)),
            lambda: (sent_all(second, odd_sends, l), sent_all(third, odd_back, l)),
        )

    loop(2, grid_back)


def per_device(n_lat, n_lon, *args):
    tokens, mask_ids, *middle, cotangent = args
    tokens = tokens.transpose(0, 2, 1, 3).reshape(2, 288, 512)
    operands = [tokens, mask_ids.transpose(2, 0, 1), *middle, cotangent.transpose(1, 2, 0, 3)]
    operands += [jnp.asarray(m) for m in row_orders()]
    shapes = dict(zip(ARGS, [(x.shape, x.dtype) for x in operands]))
    loaded = [
        pltpu.VMEM(shapes[name][0][1:] if paired else shapes[name][0], shapes[name][1])
        for name, paired in LOADED.items()
    ]
    result, grad = pl.pallas_call(
        functools.partial(kernel, n_lat, n_lon),
        out_shape=(
            jax.ShapeDtypeStruct((12, 6, 2, 1024), BF16),
            jax.ShapeDtypeStruct((2, 288, 512), BF16),
        ),
        in_specs=[
            pl.BlockSpec(memory_space=pltpu.VMEM if placed == 1 else pl.ANY) for placed in ARGS.values()
        ],
        out_specs=(pl.BlockSpec(memory_space=pltpu.VMEM), pl.BlockSpec(memory_space=pltpu.VMEM)),
        scratch_shapes=[pltpu.VMEM(*spec) for spec in SCRATCH.values()]
        + loaded
        + [
            pltpu.SemaphoreType.DMA((len(LOADED),)),
            pltpu.SemaphoreType.DMA((26, 2)),
            pltpu.SemaphoreType.DMA((26, 2)),
            pltpu.SemaphoreType.DMA((6, 2)),
        ],
        compiler_params=pltpu.CompilerParams(
            collective_id=0, has_side_effects=True, vmem_limit_bytes=60 * 2**20
        ),
    )(*operands)
    return result.transpose(2, 0, 1, 3), grad.reshape(2, 12, 24, 512).transpose(0, 2, 1, 3)


def solution(mesh):
    grid = P(None, "lat", "lon", None)
    placed = (grid, P(None, "lat", "lon"), P(), P(), P(), P(), P(), P(), P(), grid)
    return jax.shard_map(
        functools.partial(per_device, mesh.shape["lat"], mesh.shape["lon"]),
        mesh=mesh,
        in_specs=placed,
        out_specs=(grid, grid),
        check_vma=False,
    )
```

```python
import functools

import jax
import jax.numpy as jnp
import numpy as np
from jax import lax
from jax.experimental import pallas as pl
from jax.experimental.pallas import tpu as pltpu
from jax.sharding import PartitionSpec as P

F32 = jnp.float32
BF16 = jnp.bfloat16
EPSILON = 1e-05
MASKED = -1e30
MESH = pl.DeviceIdType.MESH

UNIT = 80
QUARTER = 96
NEIGHBOURS = [(a, b) for a in (-1, 0, 1) for b in (-1, 0, 1) if (a, b) != (0, 0)] + [(0, 2), (0, -2)]


def one_hot(pairs, rows, columns):
    out = np.zeros((rows, columns), np.float32)
    for r, c in pairs:
        out[r, c] = 1.0
    return out


def in_quarter(row, col):
    return row * 6 + col if row < 9 else 64 + (row - 9) * 6 + col


@functools.cache
def row_orders():
    to_region = np.zeros((2, 4 * QUARTER, 288), np.float32)
    for odd in range(2):
        for half in range(2):
            for c in range(6):
                for a in range(12):
                    col = 24 * (6 * half + c)
                    upper = a + 3
                    lower = a + 15 if a < 9 else a - 9
                    kept, sent = (lower, upper) if odd else (upper, lower)
                    to_region[odd, half * QUARTER + in_quarter(a, c), col + kept] = 1.0
                    to_region[odd, (2 + half) * QUARTER + in_quarter(a, c), col + sent] = 1.0
    to_unit = one_hot(
        [
            (UNIT * (a // 6) + 12 * (a % 6) + o, (o // 6) * QUARTER + in_quarter(a, o % 6))
            for a in range(12)
            for o in range(12)
        ],
        2 * UNIT,
        2 * QUARTER,
    )
    merge = np.zeros((4, 72, 4 * QUARTER), np.float32)
    for k, (dr, dc) in enumerate([(0, 0), (1, 0), (0, 1), (1, 1)]):
        for r in range(6):
            for c in range(12):
                quarter, col = divmod(2 * c + dc, 6)
                a = 2 * r + dr
                at = 64 + a * 6 + col if a < 3 else (a - 3) * 6 + col
                merge[k, r * 12 + c, quarter * QUARTER + at] = 1.0
    coarse = one_hot(
        [
            (l * 72 + r * 12 + c, (((c // 6) * 6 + r) * 6 + c % 6) * 2 + l)
            for l in range(2)
            for r in range(6)
            for c in range(12)
        ],
        144,
        144,
    )
    id_row = one_hot([(t, t // 12 + 18) for t in range(72)], UNIT, 24)
    id_col = one_hot([(t, t % 12) for t in range(72)], UNIT, 12)
    both = lambda m: [m, np.swapaxes(m, -1, -2)]
    orders = both(to_region) + both(to_unit) + both(merge) + both(coarse)
    return [np.ascontiguousarray(m).astype(jnp.bfloat16) for m in orders] + [id_row, id_col]


def dot(a, b):
    return lax.dot_general(a, b, (((1,), (0,)), ((), ())), preferred_element_type=F32)


def dot_nt(a, b):
    return lax.dot_general(a, b, (((1,), (1,)), ((), ())), preferred_element_type=F32)


def dot_tn(a, b):
    return lax.dot_general(a, b, (((0,), (0,)), ((), ())), preferred_element_type=F32)


def normed_rows(x):
    center = x - jnp.mean(x, axis=-1, keepdims=True)
    scale = lax.rsqrt(jnp.mean(center * center, axis=-1, keepdims=True) + EPSILON)
    return center * scale, scale


def norm_grad(grad, hat, scale):
    inner = jnp.mean(grad * hat, axis=-1, keepdims=True)
    return scale * (grad - jnp.mean(grad, axis=-1, keepdims=True) - hat * inner)


def one_row(x):
    span = x.shape[0] // 2
    low = lax.broadcasted_iota(jnp.int32, (span, 128), 1) < 64
    return jnp.where(low, x[:span], x[span:])


def rows_at(start, size, unit=16):
    return pl.ds(pl.multiple_of(start, unit), size)


def loop(count, body):
    lax.fori_loop(0, count, lambda t, c: (body(t), c)[1], 0)


class Box:
    def __init__(self, **fields):
        self.__dict__.update(fields)


ARGS = dict(
    tokens=0, mask_ids=1, fine_bias=0, fine_qkv=0, fine_out=0, merge_weight=0, coarse_bias=0, coarse_qkv=0,
    coarse_out=0, cotangent=2, to_region=0, to_region_t=0, to_unit=0, to_unit_t=0,
    merge=0, merge_t=0, coarse=0, coarse_t=0, id_row=1, id_col=1,
)
LOADED = dict(
    tokens=0, to_region=1, fine_bias=0, coarse=0, coarse_bias=0, coarse_out=0, to_unit=0, fine_qkv=0, fine_out=0,
    to_unit_t=0, merge=0, merge_weight=0, coarse_qkv=0, coarse_t=0, merge_t=0, to_region_t=1,
)
SCRATCH = dict(
    heads2=((160, 128), BF16),
    heads2_c=((288, 128), BF16),
    send1=((2, 4, QUARTER, 512), BF16),
    region=((2, 4, QUARTER, 512), BF16),
    unit_x=((640, 512), BF16),
    unit_n=((640, 512), BF16),
    hat_f=((640, 512), F32),
    scale_f=((640, 128), F32),
    proj=((704, 1536), BF16),
    mask_left=((12, 2, 24), jnp.int32),
    bias_f=((3, 2, 4, 160, 128), F32),
    raised_f=((8, 4, 160, 128), BF16),
    recip_f=((640, 512), F32),
    heads_f=((640, 512), BF16),
    send2=((2, 4, QUARTER, 512), BF16),
    quarters=((2, 4, QUARTER, 512), BF16),
    hat_m=((144, 2048), F32),
    scale_m=((144, 128), F32),
    normed_m=((144, 2048), BF16),
    merged=((144, 1024), BF16),
    hat_c=((144, 1024), F32),
    scale_c=((144, 128), F32),
    normed_c=((144, 1024), BF16),
    proj_c=((256, 3072), BF16),
    bias_c=((16, 144, 256), F32),
    raised_c=((8, 288, 256), BF16),
    recip_c=((144, 1024), F32),
    heads_c=((144, 1024), BF16),
    result=((144, 1024), BF16),
    result2=((2, 6, 6, 2, 1024), BF16),
    cot2=((2, 6, 6, 2, 1024), BF16),
    cot=((144, 1024), BF16),
    dheads_c=((144, 1024), BF16),
    dprod_c=((144, 1024), BF16),
    dproj_c=((144, 3072), BF16),
    grad_c=((144, 1024), F32),
    dmerged=((144, 1024), BF16),
    grad_m=((144, 2048), F32),
    send3=((2, 4, QUARTER, 512), BF16),
    part=((2, 4, QUARTER, 512), BF16),
    dmixed=((640, 512), BF16),
    dheads_f=((640, 512), BF16),
    dprod_f=((640, 512), BF16),
    dproj_f=((640, 1536), BF16),
    send4=((2, 4, QUARTER, 512), BF16),
    region4=((2, 4, QUARTER, 512), BF16),
)
def kernel(n_lat, n_lon, *refs):
    rest = list(refs)
    hbm = Box(**{name: rest.pop(0) for name in ARGS})
    result_ref, grad_ref = rest.pop(0), rest.pop(0)
    vm = Box(**{name: rest.pop(0) for name in SCRATCH})
    ld = Box(**{name: rest.pop(0) for name in LOADED})
    load_sem, send_sem, recv_sem, near_sem = rest

    i, j = lax.axis_index("lat"), lax.axis_index("lon")
    odd = lax.rem(j, 2)
    even = odd == 0

    def device(di, dj):
        return (lax.rem(i + di + n_lat, n_lat), lax.rem(j + dj + n_lon, n_lon))

    def remote(src, dst, sem, l, target):
        return pltpu.make_async_remote_copy(
            src_ref=src,
            dst_ref=dst,
            send_sem=send_sem.at[sem, l],
            recv_sem=recv_sem.at[sem, l],
            device_id=target,
            device_id_type=MESH,
        )

    vm.mask_left[...] = jnp.zeros((12, 2, 24), jnp.int32)
    barrier = pltpu.get_barrier_semaphore()
    for di, dj in NEIGHBOURS:
        pl.semaphore_signal(barrier, inc=1, device_id=device(di, dj), device_id_type=MESH)

    loads = Box()
    for at, (name, paired) in enumerate(LOADED.items()):
        src = getattr(hbm, name)
        if paired:
            src = src.at[odd]
        copy = pltpu.make_async_copy(src, getattr(ld, name), load_sem.at[at])
        copy.start()
        setattr(loads, name, copy)
    own_cot = pltpu.make_async_copy(
        hbm.cotangent.at[pl.ds(6 * odd, 6)], vm.cot2.at[odd], near_sem.at[16, 0]
    )
    own_cot.start()

    for end in (320, 640):
        vm.proj[end : end + 64, :] = jnp.zeros((64, 1536), BF16)
    vm.proj_c[144:, :] = jnp.zeros((112, 3072), BF16)
    for ref in (vm.heads2, vm.heads2_c):
        low = lax.broadcasted_iota(jnp.int32, ref.shape, 1) < 64
        first = lax.broadcasted_iota(jnp.int32, ref.shape, 0) < ref.shape[0] // 2
        ref[...] = jnp.where(low == first, 1.0, 0.0).astype(BF16)

    def two_heads(x, mask):
        return jnp.concatenate([x, x], axis=0) * mask[...]

    loads.tokens.wait()
    loads.to_region.wait()
    pl.semaphore_wait(barrier, len(NEIGHBOURS))

    whole, top, low = (0, 96), (0, 64), (64, 32)
    left, right, far_left, far_right = (0, -1), (0, 1), (0, -2), (0, 2)
    plans = [
        (
            vm.send1,
            vm.region,
            [
                (2, 3, low, (-1, -1)), (3, 0, low, (-1, 1)), (2, 3, top, left), (3, 0, top, right),
                (0, 1, whole, None), (1, 2, whole, None),
            ],
            [
                (0, 1, low, (-1, 0)), (1, 2, low, (-1, 0)), (2, 3, whole, left), (3, 0, whole, right),
                (0, 1, top, None), (1, 2, top, None),
            ],
        ),
        (
            vm.send2,
            vm.quarters,
            [
                (0, 3, top, far_left), (0, 3, low, left), (1, 0, low, right), (2, 1, low, right),
                (3, 2, low, right), (1, 0, top, None), (2, 1, top, None), (3, 2, top, None),
            ],
            [
                (3, 0, top, far_right), (3, 0, low, (1, 1)), (0, 1, low, (1, -1)), (1, 2, low, (1, -1)),
                (2, 3, low, (1, -1)), (0, 1, top, None), (1, 2, top, None), (2, 3, top, None),
            ],
        ),
    ]
    for (_, _, of_even, of_odd), src, dst in ((plans[1], vm.send3, vm.part), (plans[0], vm.send4, vm.region4)):
        back_even, back_odd = [], []
        for mine, ours in ((of_even, 0), (of_odd, 1)):
            for at, into, rows, to in mine:
                if to is None:
                    target = ours
                    way = None
                else:
                    target = (ours + to[1]) % 2
                    way = (-to[0], -to[1])
                (back_odd if target else back_even).append((into, at, rows, way))
        plans.append((src, dst, back_even, back_odd))

    def transfer(phase, l, plan):
        at, into, (start, size), to = plan
        src, dst = plans[phase][:2]
        src, dst = src.at[l, at, pl.ds(start, size)], dst.at[l, into, pl.ds(start, size)]
        sem = phase * 8 + into * 2 + (start > 0)
        if to is None:
            return pltpu.make_async_copy(src, dst, near_sem.at[phase * 4 + into, l])
        return remote(src, dst, sem, l, device(*to))

    def by_parity(of_even, of_odd):
        @pl.when(even)
        def _():
            of_even()

        @pl.when(odd == 1)
        def _():
            of_odd()

    def send(phase, l, keep=None):
        def start(mine):
            for plan in mine:
                if keep is None or plan[0] in keep:
                    transfer(phase, l, plan).start()

        by_parity(lambda: start(plans[phase][2]), lambda: start(plans[phase][3]))

    def arrivals(phase, parity):
        got = []
        for ours in range(2):
            for plan in plans[phase][2 + ours]:
                to = plan[3]
                if (ours if to is None else (ours + to[1]) % 2) == parity:
                    got.append(plan)
        return got

    def take(phase, l, keep=None):
        def wait(parity):
            for plan in arrivals(phase, parity):
                if keep is None or plan[1] in keep:
                    copy = transfer(phase, l, plan)
                    copy.wait() if plan[3] is None else copy.wait_recv()

        by_parity(lambda: wait(0), lambda: wait(1))

    def sent(phase, l):
        def wait(mine):
            for plan in mine:
                if plan[3] is not None:
                    transfer(phase, l, plan).wait_send()

        by_parity(lambda: wait(plans[phase][2]), lambda: wait(plans[phase][3]))

    def at_strip(strip, of_strip):
        @pl.when(strip == 0)
        def _():
            of_strip((0, 1))

        @pl.when(strip == 1)
        def _():
            of_strip((2, 3))

    def regions(l):
        vm.send1[l] = dot(ld.to_region[...], ld.tokens[l]).astype(BF16).reshape(4, QUARTER, 512)
        send(0, l)

    loop(2, regions)
    partner_cot = remote(
        hbm.cotangent.at[pl.ds(6 - 6 * odd, 6)], vm.cot2.at[odd], 32, 0, device(0, 1 - 2 * odd)
    )
    partner_cot.start()
    left_mask = remote(hbm.mask_ids, vm.mask_left, 34, 0, device(0, 1))
    by_parity(left_mask.start, lambda: None)

    loads.fine_bias.wait()
    by_parity(lambda: None, left_mask.wait_recv)
    lanes = lax.broadcasted_iota(jnp.int32, (UNIT, 128), 1)
    subs = lax.broadcasted_iota(jnp.int32, (UNIT, 128), 0)
    past = jnp.where(lanes >= 72, MASKED, 0.0).astype(F32)
    for level in range(2):
        masks = [past]
        for ids in (vm.mask_left, hbm.mask_ids):
            spread = dot(hbm.id_col[...], ids[:, level, :].astype(F32))
            id_of = jnp.sum(spread * hbm.id_row[...], axis=-1, keepdims=True)
            id_at = dot(jnp.ones((8, UNIT), F32), jnp.where(lanes == subs, id_of, 0.0))[:1]
            masks.append(jnp.where(id_of == id_at, past, MASKED))
        for head in range(8):
            span = slice(72 * level, 72 * level + 72)
            block = ld.fine_bias[head, span, span]
            block = jnp.concatenate([block, jnp.zeros((72, 56), F32)], axis=1)
            block = jnp.concatenate([block, jnp.zeros((8, 128), F32)], axis=0)
            at = slice(UNIT * (head % 2), UNIT * (head % 2) + UNIT)
            for kind, mask in enumerate(masks):
                vm.bias_f[kind, level, head // 2, at, :] = block + mask

    loads.coarse_bias.wait()

    def coarse_pad(h):
        vm.bias_c[h] = jnp.concatenate([ld.coarse_bias[h], jnp.full((144, 112), MASKED, F32)], axis=1)

    loop(16, coarse_pad)
    own_cot.wait()
    partner_cot.wait()
    loads.coarse.wait()
    vm.cot[...] = dot(ld.coarse[...], vm.cot2[...].reshape(144, 1024)).astype(BF16)
    loads.coarse_out.wait()

    def coarse_cot(t):
        cols = rows_at(t * 512, 512, 512)
        vm.grad_c[:, cols] = dot_nt(vm.cot[...], ld.coarse_out[cols, :])

    loop(2, coarse_cot)
    loads.to_unit.wait()
    loads.fine_qkv.wait()
    loads.fine_out.wait()
    loads.to_unit_t.wait()

    def fine_forward(turn):
        strip = lax.rem(1 - odd + turn, 2)
        base = strip * 320
        level_at = lambda l: rows_at(base + l * 160, 160)
        both_levels = rows_at(base, 320)
        at_strip(strip, lambda keep: [take(0, l, keep) for l in range(2)])

        def fine_norm(l):
            source = vm.region[l, pl.ds(2 * strip, 2)].reshape(2 * QUARTER, 512)
            x = dot(ld.to_unit[...], source)
            hat, scale = normed_rows(x)
            vm.unit_x[level_at(l), :] = x.astype(BF16)
            vm.hat_f[level_at(l), :] = hat
            vm.scale_f[level_at(l), :] = jnp.broadcast_to(scale, (160, 128))
            vm.unit_n[level_at(l), :] = hat.astype(BF16)

        loop(2, fine_norm)

        def fine_project(t):
            cols = rows_at(t * 512, 512, 512)
            scale = jnp.where(t < 1, 0.125, 1.0).astype(F32)
            vm.proj[both_levels, cols] = (
                dot(vm.unit_n[both_levels, :], ld.fine_qkv[:, cols]) * scale
            ).astype(BF16)

        loop(3, fine_project)

        def fine_level(l):
            def fine_attend(m):
                last = odd * m * (1 + strip)
                start = base + l * 160 + m * UNIT
                at, wide = rows_at(start, UNIT), rows_at(start, 128)
                pairs = [slice(128 * p, 128 * p + 128) for p in range(4)]
                ones = jnp.ones((128, 128), BF16)
                scores = [
                    dot_nt(
                        two_heads(vm.proj[at, pair], vm.heads2), vm.proj[wide, 512 + pair.start : 512 + pair.stop]
                    )
                    + vm.bias_f[last, 1 - l, p]
                    for p, pair in enumerate(pairs)
                ]
                tops = [jnp.max(s, axis=-1, keepdims=True) for s in scores]
                raised = [jnp.exp(s - t).astype(BF16) for s, t in zip(scores, tops)]
                sums = [
                    dot(e, jnp.concatenate([vm.proj[wide, 1024 + pair.start : 1024 + pair.stop], ones], axis=1))
                    for e, pair in zip(raised, pairs)
                ]
                for p, pair in enumerate(pairs):
                    recip = 1.0 / one_row(sums[p][:, 128:])
                    vm.raised_f[strip * 4 + l * 2 + m, p] = raised[p]
                    vm.recip_f[at, pair] = recip
                    vm.heads_f[at, pair] = (one_row(sums[p][:, :128]) * recip).astype(BF16)

            loop(2, fine_attend)
            mixed = vm.unit_x[level_at(l), :].astype(F32) + dot(vm.heads_f[level_at(l), :], ld.fine_out[...])
            ordered = dot(ld.to_unit_t[...], mixed.astype(BF16)).astype(BF16)
            vm.send2[l, pl.ds(2 * strip, 2)] = ordered.reshape(2, QUARTER, 512)
            at_strip(strip, lambda keep: send(1, l, keep))

        loop(2, fine_level)

    loop(2, fine_forward)
    loads.merge.wait()
    loads.merge_weight.wait()
    loads.coarse_qkv.wait()
    loads.coarse_t.wait()

    def gather(l):
        take(1, l)
        source = vm.quarters[l].reshape(4 * QUARTER, 512)
        for k in range(4):
            vm.hat_m[rows_at(l * 72, 72, 8), 512 * k : 512 * k + 512] = dot(ld.merge[k], source)

    loop(2, gather)

    def merge_norm(t):
        at = rows_at(t * 48, 48)
        hat, scale = normed_rows(vm.hat_m[at, :])
        vm.hat_m[at, :] = hat
        vm.scale_m[at, :] = jnp.broadcast_to(scale, (48, 128))
        vm.normed_m[at, :] = hat.astype(BF16)

    loop(3, merge_norm)

    def merge_project(t):
        cols = rows_at(t * 512, 512, 512)
        vm.merged[:, cols] = dot(vm.normed_m[...], ld.merge_weight[:, cols]).astype(BF16)

    loop(2, merge_project)

    def coarse_norm(t):
        at = rows_at(t * 48, 48)
        hat, scale = normed_rows(vm.merged[at, :].astype(F32))
        vm.hat_c[at, :] = hat
        vm.scale_c[at, :] = jnp.broadcast_to(scale, (48, 128))
        vm.normed_c[at, :] = hat.astype(BF16)

    loop(3, coarse_norm)

    def coarse_project(t):
        cols = rows_at(t * 512, 512, 512)
        scale = jnp.where(t < 2, 0.125, 1.0).astype(F32)
        vm.proj_c[:144, cols] = (dot(vm.normed_c[...], ld.coarse_qkv[:, cols]) * scale).astype(BF16)

    loop(6, coarse_project)

    def cols_at(p, base):
        return rows_at(p * 128 + base, 128, 128)

    def coarse_attend(t):
        pairs = [2 * t, 2 * t + 1]
        ones = jnp.ones((256, 128), BF16)
        scores = [
            dot_nt(two_heads(vm.proj_c[:144, cols_at(p, 0)], vm.heads2_c), vm.proj_c[:, cols_at(p, 1024)])
            + vm.bias_c[pl.ds(2 * p, 2)].reshape(288, 256)
            for p in pairs
        ]
        tops = [jnp.max(s, axis=-1, keepdims=True) for s in scores]
        raised = [jnp.exp(s - top).astype(BF16) for s, top in zip(scores, tops)]
        sums = [
            dot(e, jnp.concatenate([vm.proj_c[:, cols_at(p, 2048)], ones], axis=1))
            for e, p in zip(raised, pairs)
        ]
        for p, e, total in zip(pairs, raised, sums):
            recip = 1.0 / one_row(total[:, 128:])
            vm.raised_c[p] = e
            vm.recip_c[:, cols_at(p, 0)] = recip
            vm.heads_c[:, cols_at(p, 0)] = (one_row(total[:, :128]) * recip).astype(BF16)

    loop(4, coarse_attend)

    def coarse_mix(t):
        cols = rows_at(t * 512, 512, 512)
        mixed = dot(vm.heads_c[...], ld.coarse_out[:, cols])
        vm.result[:, cols] = (vm.merged[:, cols].astype(F32) + mixed).astype(BF16)
        grad = vm.grad_c[:, cols] * vm.recip_c[:, cols]
        vm.dheads_c[:, cols] = grad.astype(BF16)
        vm.dprod_c[:, cols] = (grad * vm.heads_c[:, cols].astype(F32)).astype(BF16)

    loop(2, coarse_mix)

    vm.result2[...] = dot(ld.coarse_t[...], vm.result[...]).astype(BF16).reshape(2, 6, 6, 2, 1024)
    into = result_ref.at[pl.ds(6 * odd, 6)]
    result_near = pltpu.make_async_copy(vm.result2.at[odd], into, near_sem.at[17, 0])
    result_far = remote(vm.result2.at[1 - odd], into, 33, 0, device(0, 1 - 2 * odd))
    result_near.start()
    result_far.start()

    def coarse_attend_grad(t):
        pairs = [2 * t, 2 * t + 1]
        minus = jnp.full((256, 128), -1.0, BF16)
        grads = [two_heads(vm.dheads_c[:, cols_at(p, 0)], vm.heads2_c) for p in pairs]
        prods = [two_heads(vm.dprod_c[:, cols_at(p, 0)], vm.heads2_c) for p in pairs]
        queries = [two_heads(vm.proj_c[:144, cols_at(p, 0)], vm.heads2_c) for p in pairs]
        inner = [
            dot_nt(
                jnp.concatenate([g, d], axis=1), jnp.concatenate([vm.proj_c[:, cols_at(p, 2048)], minus], axis=1)
            )
            for p, g, d in zip(pairs, grads, prods)
        ]
        dscores = [(vm.raised_c[p].astype(F32) * x).astype(BF16) for p, x in zip(pairs, inner)]
        for p, g, q, ds in zip(pairs, grads, queries, dscores):
            vm.dproj_c[:, cols_at(p, 2048)] = dot_tn(vm.raised_c[p], g)[:144].astype(BF16)
            dq = one_row(dot(ds, vm.proj_c[:, cols_at(p, 1024)]))
            vm.dproj_c[:, cols_at(p, 0)] = (dq * 0.125).astype(BF16)
            vm.dproj_c[:, cols_at(p, 1024)] = dot_tn(ds, q)[:144].astype(BF16)

    loop(4, coarse_attend_grad)

    def coarse_project_grad(t):
        cols = rows_at(t * 512, 512, 512)
        vm.grad_c[:, cols] = dot_nt(vm.dproj_c[...], ld.coarse_qkv[cols, :])

    loop(2, coarse_project_grad)

    def coarse_norm_grad(t):
        at = rows_at(t * 48, 48)
        grad = norm_grad(vm.grad_c[at, :], vm.hat_c[at, :], vm.scale_c[at, :1])
        vm.dmerged[at, :] = (vm.cot[at, :].astype(F32) + grad).astype(BF16)

    loop(3, coarse_norm_grad)

    def merge_project_grad(t):
        cols = rows_at(t * 512, 512, 512)
        vm.grad_m[:, cols] = dot_nt(vm.dmerged[...], ld.merge_weight[cols, :])

    loop(4, merge_project_grad)
    loads.merge_t.wait()

    def scatter(l):
        at = rows_at(l * 72, 72, 8)
        grad = norm_grad(vm.grad_m[at, :], vm.hat_m[at, :], vm.scale_m[at, :1]).astype(BF16)
        total = dot(ld.merge_t[0], grad[:, :512])
        for k in range(1, 4):
            total = total + dot(ld.merge_t[k], grad[:, 512 * k : 512 * k + 512])
        vm.send3[l] = total.astype(BF16).reshape(4, QUARTER, 512)
        send(2, l)

    loop(2, scatter)
    loads.to_region_t.wait()

    def fine_backward(turn):
        strip = lax.rem(1 - odd + turn, 2)
        base = strip * 320
        level_at = lambda l: rows_at(base + l * 160, 160)
        both_levels = rows_at(base, 320)
        at_strip(strip, lambda keep: [take(2, l, keep) for l in range(2)])

        def fine_units(l):
            source = vm.part[l, pl.ds(2 * strip, 2)].reshape(2 * QUARTER, 512)
            vm.dmixed[level_at(l), :] = dot(ld.to_unit[...], source).astype(BF16)

        loop(2, fine_units)
        grad = dot_nt(vm.dmixed[both_levels, :], ld.fine_out[...]) * vm.recip_f[both_levels, :]
        vm.dheads_f[both_levels, :] = grad.astype(BF16)
        vm.dprod_f[both_levels, :] = (grad * vm.heads_f[both_levels, :].astype(F32)).astype(BF16)

        def fine_level_back(l):
            def fine_attend_grad(m):
                start = base + l * 160 + m * UNIT
                at, wide = rows_at(start, UNIT), rows_at(start, 128)
                pairs = [slice(128 * p, 128 * p + 128) for p in range(4)]
                minus = jnp.full((128, 128), -1.0, BF16)
                grads = [two_heads(vm.dheads_f[at, pair], vm.heads2) for pair in pairs]
                prods = [two_heads(vm.dprod_f[at, pair], vm.heads2) for pair in pairs]
                queries = [two_heads(vm.proj[at, pair], vm.heads2) for pair in pairs]
                inner = [
                    dot_nt(
                        jnp.concatenate([g, d], axis=1),
                        jnp.concatenate([vm.proj[wide, 1024 + pair.start : 1024 + pair.stop], minus], axis=1),
                    )
                    for pair, g, d in zip(pairs, grads, prods)
                ]
                raised = [vm.raised_f[strip * 4 + l * 2 + m, p] for p in range(4)]
                dscores = [(e.astype(F32) * x).astype(BF16) for e, x in zip(raised, inner)]
                dvalues = [dot_tn(e, g) for e, g in zip(raised, grads)]
                dkeys = [dot_tn(ds, q) for ds, q in zip(dscores, queries)]
                dqueries = [
                    dot(ds, vm.proj[wide, 512 + pair.start : 512 + pair.stop]) for pair, ds in zip(pairs, dscores)
                ]
                for p, pair in enumerate(pairs):
                    vm.dproj_f[at, pair] = (one_row(dqueries[p]) * 0.125).astype(BF16)
                    vm.dproj_f[at, 512 + pair.start : 512 + pair.stop] = dkeys[p][:UNIT].astype(BF16)
                    vm.dproj_f[at, 1024 + pair.start : 1024 + pair.stop] = dvalues[p][:UNIT].astype(BF16)

            loop(2, fine_attend_grad)
            grad = dot_nt(vm.dproj_f[level_at(l), :], ld.fine_qkv[...])
            grad = norm_grad(grad, vm.hat_f[level_at(l), :], vm.scale_f[level_at(l), :1])
            dunit = (vm.dmixed[level_at(l), :].astype(F32) + grad).astype(BF16)
            ordered = dot(ld.to_unit_t[...], dunit).astype(BF16)
            vm.send4[l, pl.ds(2 * strip, 2)] = ordered.reshape(2, QUARTER, 512)
            at_strip(strip, lambda keep: send(3, l, keep))

        loop(2, fine_level_back)

    loop(2, fine_backward)
    by_parity(left_mask.wait_send, lambda: None)
    result_near.wait()
    result_far.wait()

    def grid_back(l):
        take(3, l)
        grad_ref[l] = dot(ld.to_region_t[...], vm.region4[l].reshape(4 * QUARTER, 512)).astype(BF16)
        for phase in range(4):
            sent(phase, l)

    loop(2, grid_back)


def per_device(n_lat, n_lon, *args):
    tokens, mask_ids, *middle, cotangent = args
    tokens = tokens.transpose(0, 2, 1, 3).reshape(2, 288, 512)
    operands = [tokens, mask_ids.transpose(2, 0, 1), *middle, cotangent.transpose(1, 2, 0, 3)]
    operands += [jnp.asarray(m) for m in row_orders()]
    shapes = dict(zip(ARGS, [(x.shape, x.dtype) for x in operands]))
    loaded = [
        pltpu.VMEM(shapes[name][0][1:] if paired else shapes[name][0], shapes[name][1])
        for name, paired in LOADED.items()
    ]
    result, grad = pl.pallas_call(
        functools.partial(kernel, n_lat, n_lon),
        out_shape=(
            jax.ShapeDtypeStruct((12, 6, 2, 1024), BF16),
            jax.ShapeDtypeStruct((2, 288, 512), BF16),
        ),
        in_specs=[
            pl.BlockSpec(memory_space=pltpu.VMEM if placed == 1 else pl.ANY) for placed in ARGS.values()
        ],
        out_specs=(pl.BlockSpec(memory_space=pltpu.VMEM), pl.BlockSpec(memory_space=pltpu.VMEM)),
        scratch_shapes=[pltpu.VMEM(*spec) for spec in SCRATCH.values()]
        + loaded
        + [
            pltpu.SemaphoreType.DMA((len(LOADED),)),
            pltpu.SemaphoreType.DMA((35, 2)),
            pltpu.SemaphoreType.DMA((35, 2)),
            pltpu.SemaphoreType.DMA((18, 2)),
        ],
        compiler_params=pltpu.CompilerParams(
            collective_id=0, has_side_effects=True, vmem_limit_bytes=60 * 2**20
        ),
    )(*operands)
    return result.transpose(2, 0, 1, 3), grad.reshape(2, 12, 24, 512).transpose(0, 2, 1, 3)


def solution(mesh):
    grid = P(None, "lat", "lon", None)
    placed = (grid, P(None, "lat", "lon"), P(), P(), P(), P(), P(), P(), P(), grid)
    return jax.shard_map(
        functools.partial(per_device, mesh.shape["lat"], mesh.shape["lon"]),
        mesh=mesh,
        in_specs=placed,
        out_specs=(grid, grid),
        check_vma=False,
    )
```

```python
import functools

import jax
import jax.numpy as jnp
import numpy as np
from jax import lax
from jax.experimental import pallas as pl
from jax.experimental.pallas import tpu as pltpu
from jax.sharding import PartitionSpec as P

F32 = jnp.float32
BF16 = jnp.bfloat16
EPSILON = 1e-05
MASKED = -1e30
MESH = pl.DeviceIdType.MESH

UNIT = 80
QUARTER = 96
NEIGHBOURS = [(a, b) for a in (-1, 0, 1) for b in (-1, 0, 1) if (a, b) != (0, 0)] + [(0, 2), (0, -2)]


def one_hot(pairs, rows, columns):
    out = np.zeros((rows, columns), np.float32)
    for r, c in pairs:
        out[r, c] = 1.0
    return out


def in_quarter(row, col):
    return row * 6 + col if row < 9 else 64 + (row - 9) * 6 + col


@functools.cache
def row_orders():
    to_region = np.zeros((2, 4 * QUARTER, 288), np.float32)
    for odd in range(2):
        for half in range(2):
            for c in range(6):
                for a in range(12):
                    col = 24 * (6 * half + c)
                    upper = a + 3
                    lower = a + 15 if a < 9 else a - 9
                    kept, sent = (lower, upper) if odd else (upper, lower)
                    to_region[odd, half * QUARTER + in_quarter(a, c), col + kept] = 1.0
                    to_region[odd, (2 + half) * QUARTER + in_quarter(a, c), col + sent] = 1.0
    to_unit = one_hot(
        [
            (UNIT * (a // 6) + 12 * (a % 6) + o, (o // 6) * QUARTER + in_quarter(a, o % 6))
            for a in range(12)
            for o in range(12)
        ],
        2 * UNIT,
        2 * QUARTER,
    )
    merge = np.zeros((4, 72, 4 * QUARTER), np.float32)
    for k, (dr, dc) in enumerate([(0, 0), (1, 0), (0, 1), (1, 1)]):
        for r in range(6):
            for c in range(12):
                quarter, col = divmod(2 * c + dc, 6)
                a = 2 * r + dr
                at = 64 + a * 6 + col if a < 3 else (a - 3) * 6 + col
                merge[k, r * 12 + c, quarter * QUARTER + at] = 1.0
    coarse = one_hot(
        [
            (l * 72 + r * 12 + c, (((c // 6) * 6 + r) * 6 + c % 6) * 2 + l)
            for l in range(2)
            for r in range(6)
            for c in range(12)
        ],
        144,
        144,
    )
    id_row = one_hot([(t, t // 12 + 18) for t in range(72)], UNIT, 24)
    id_col = one_hot([(t, t % 12) for t in range(72)], UNIT, 12)
    both = lambda m: [m, np.swapaxes(m, -1, -2)]
    orders = both(to_region) + both(to_unit) + both(merge) + both(coarse)
    return [np.ascontiguousarray(m).astype(jnp.bfloat16) for m in orders] + [id_row, id_col]


def dot(a, b):
    return lax.dot_general(a, b, (((1,), (0,)), ((), ())), preferred_element_type=F32)


def dot_nt(a, b):
    return lax.dot_general(a, b, (((1,), (1,)), ((), ())), preferred_element_type=F32)


def dot_tn(a, b):
    return lax.dot_general(a, b, (((0,), (0,)), ((), ())), preferred_element_type=F32)


def normed_rows(x):
    center = x - jnp.mean(x, axis=-1, keepdims=True)
    scale = lax.rsqrt(jnp.mean(center * center, axis=-1, keepdims=True) + EPSILON)
    return center * scale, scale


def norm_grad(grad, hat, scale):
    inner = jnp.mean(grad * hat, axis=-1, keepdims=True)
    return scale * (grad - jnp.mean(grad, axis=-1, keepdims=True) - hat * inner)


def one_row(x):
    span = x.shape[0] // 2
    low = lax.broadcasted_iota(jnp.int32, (span, 128), 1) < 64
    return jnp.where(low, x[:span], x[span:])


def rows_at(start, size, unit=16):
    return pl.ds(pl.multiple_of(start, unit), size)


def loop(count, body):
    lax.fori_loop(0, count, lambda t, c: (body(t), c)[1], 0)


class Box:
    def __init__(self, **fields):
        self.__dict__.update(fields)


ARGS = dict(
    tokens=0, mask_ids=1, fine_bias=0, fine_qkv=0, fine_out=0, merge_weight=0, coarse_bias=0, coarse_qkv=0,
    coarse_out=0, cotangent=2, to_region=0, to_region_t=0, to_unit=0, to_unit_t=0,
    merge=0, merge_t=0, coarse=0, coarse_t=0, id_row=1, id_col=1,
)
LOADED = dict(
    tokens=0, to_region=1, fine_bias=0, to_unit=0, fine_qkv=0, fine_out=0, to_unit_t=0, coarse=0, coarse_bias=0,
    coarse_out=0, merge=0, merge_weight=0, coarse_qkv=0, coarse_t=0, merge_t=0, to_region_t=1,
)
SCRATCH = dict(
    heads2=((160, 128), BF16),
    heads2_c=((288, 128), BF16),
    send1=((2, 4, QUARTER, 512), BF16),
    region=((2, 4, QUARTER, 512), BF16),
    unit_x=((640, 512), BF16),
    unit_n=((640, 512), BF16),
    hat_f=((640, 512), F32),
    scale_f=((640, 128), F32),
    proj=((704, 1536), BF16),
    mask_left=((12, 2, 24), jnp.int32),
    bias_f=((3, 2, 4, 160, 128), F32),
    raised_f=((8, 4, 160, 128), BF16),
    recip_f=((640, 512), F32),
    heads_f=((640, 512), BF16),
    send2=((2, 4, QUARTER, 512), BF16),
    quarters=((2, 4, QUARTER, 512), BF16),
    hat_m=((144, 2048), F32),
    scale_m=((144, 128), F32),
    normed_m=((144, 2048), BF16),
    merged=((144, 1024), BF16),
    hat_c=((144, 1024), F32),
    scale_c=((144, 128), F32),
    normed_c=((144, 1024), BF16),
    proj_c=((256, 3072), BF16),
    bias_c=((16, 144, 256), F32),
    raised_c=((8, 288, 256), BF16),
    recip_c=((144, 1024), F32),
    heads_c=((144, 1024), BF16),
    result=((144, 1024), BF16),
    result2=((2, 6, 6, 2, 1024), BF16),
    cot2=((2, 6, 6, 2, 1024), BF16),
    cot=((144, 1024), BF16),
    dheads_c=((144, 1024), BF16),
    dprod_c=((144, 1024), BF16),
    dproj_c=((144, 3072), BF16),
    grad_c=((144, 1024), F32),
    dmerged=((144, 1024), BF16),
    grad_m=((144, 2048), F32),
    send3=((2, 4, QUARTER, 512), BF16),
    part=((2, 4, QUARTER, 512), BF16),
    dmixed=((640, 512), BF16),
    dheads_f=((640, 512), BF16),
    dprod_f=((640, 512), BF16),
    dproj_f=((640, 1536), BF16),
    send4=((2, 4, QUARTER, 512), BF16),
    region4=((2, 4, QUARTER, 512), BF16),
)
def kernel(n_lat, n_lon, *refs):
    rest = list(refs)
    hbm = Box(**{name: rest.pop(0) for name in ARGS})
    result_ref, grad_ref = rest.pop(0), rest.pop(0)
    vm = Box(**{name: rest.pop(0) for name in SCRATCH})
    ld = Box(**{name: rest.pop(0) for name in LOADED})
    load_sem, send_sem, recv_sem, near_sem = rest

    i, j = lax.axis_index("lat"), lax.axis_index("lon")
    odd = lax.rem(j, 2)
    even = odd == 0

    def device(di, dj):
        return (lax.rem(i + di + n_lat, n_lat), lax.rem(j + dj + n_lon, n_lon))

    def remote(src, dst, sem, l, target):
        return pltpu.make_async_remote_copy(
            src_ref=src,
            dst_ref=dst,
            send_sem=send_sem.at[sem, l],
            recv_sem=recv_sem.at[sem, l],
            device_id=target,
            device_id_type=MESH,
        )

    vm.mask_left[...] = jnp.zeros((12, 2, 24), jnp.int32)
    barrier = pltpu.get_barrier_semaphore()
    for di, dj in NEIGHBOURS:
        pl.semaphore_signal(barrier, inc=1, device_id=device(di, dj), device_id_type=MESH)

    loads = Box()
    for at, (name, paired) in enumerate(LOADED.items()):
        src = getattr(hbm, name)
        if paired:
            src = src.at[odd]
        copy = pltpu.make_async_copy(src, getattr(ld, name), load_sem.at[at])
        copy.start()
        setattr(loads, name, copy)
    own_cot = pltpu.make_async_copy(
        hbm.cotangent.at[pl.ds(6 * odd, 6)], vm.cot2.at[odd], near_sem.at[16, 0]
    )
    own_cot.start()

    for end in (320, 640):
        vm.proj[end : end + 64, :] = jnp.zeros((64, 1536), BF16)
    vm.proj_c[144:, :] = jnp.zeros((112, 3072), BF16)
    for ref in (vm.heads2, vm.heads2_c):
        low = lax.broadcasted_iota(jnp.int32, ref.shape, 1) < 64
        first = lax.broadcasted_iota(jnp.int32, ref.shape, 0) < ref.shape[0] // 2
        ref[...] = jnp.where(low == first, 1.0, 0.0).astype(BF16)

    def two_heads(x, mask):
        return jnp.concatenate([x, x], axis=0) * mask[...]

    loads.tokens.wait()
    loads.to_region.wait()
    pl.semaphore_wait(barrier, len(NEIGHBOURS))

    whole, top, low = (0, 96), (0, 64), (64, 32)
    left, right, far_left, far_right = (0, -1), (0, 1), (0, -2), (0, 2)
    plans = [
        (
            vm.send1,
            vm.region,
            [
                (2, 3, low, (-1, -1)), (3, 0, low, (-1, 1)), (2, 3, top, left), (3, 0, top, right),
                (0, 1, whole, None), (1, 2, whole, None),
            ],
            [
                (0, 1, low, (-1, 0)), (1, 2, low, (-1, 0)), (2, 3, whole, left), (3, 0, whole, right),
                (0, 1, top, None), (1, 2, top, None),
            ],
        ),
        (
            vm.send2,
            vm.quarters,
            [
                (0, 3, top, far_left), (0, 3, low, left), (1, 0, low, right), (2, 1, low, right),
                (3, 2, low, right), (1, 0, top, None), (2, 1, top, None), (3, 2, top, None),
            ],
            [
                (3, 0, top, far_right), (3, 0, low, (1, 1)), (0, 1, low, (1, -1)), (1, 2, low, (1, -1)),
                (2, 3, low, (1, -1)), (0, 1, top, None), (1, 2, top, None), (2, 3, top, None),
            ],
        ),
    ]
    for (_, _, of_even, of_odd), src, dst in ((plans[1], vm.send3, vm.part), (plans[0], vm.send4, vm.region4)):
        back_even, back_odd = [], []
        for mine, ours in ((of_even, 0), (of_odd, 1)):
            for at, into, rows, to in mine:
                if to is None:
                    target = ours
                    way = None
                else:
                    target = (ours + to[1]) % 2
                    way = (-to[0], -to[1])
                (back_odd if target else back_even).append((into, at, rows, way))
        plans.append((src, dst, back_even, back_odd))

    def transfer(phase, l, plan):
        at, into, (start, size), to = plan
        src, dst = plans[phase][:2]
        src, dst = src.at[l, at, pl.ds(start, size)], dst.at[l, into, pl.ds(start, size)]
        sem = phase * 8 + into * 2 + (start > 0)
        if to is None:
            return pltpu.make_async_copy(src, dst, near_sem.at[phase * 4 + into, l])
        return remote(src, dst, sem, l, device(*to))

    def by_parity(of_even, of_odd):
        @pl.when(even)
        def _():
            of_even()

        @pl.when(odd == 1)
        def _():
            of_odd()

    def send(phase, l, keep=None):
        def start(mine):
            for plan in mine:
                if keep is None or plan[0] in keep:
                    transfer(phase, l, plan).start()

        by_parity(lambda: start(plans[phase][2]), lambda: start(plans[phase][3]))

    def arrivals(phase, parity):
        got = []
        for ours in range(2):
            for plan in plans[phase][2 + ours]:
                to = plan[3]
                if (ours if to is None else (ours + to[1]) % 2) == parity:
                    got.append(plan)
        return got

    def take(phase, l, keep=None):
        def wait(parity):
            for plan in arrivals(phase, parity):
                if keep is None or plan[1] in keep:
                    copy = transfer(phase, l, plan)
                    copy.wait() if plan[3] is None else copy.wait_recv()

        by_parity(lambda: wait(0), lambda: wait(1))

    def sent(phase, l):
        def wait(mine):
            for plan in mine:
                if plan[3] is not None:
                    transfer(phase, l, plan).wait_send()

        by_parity(lambda: wait(plans[phase][2]), lambda: wait(plans[phase][3]))

    def at_strip(strip, of_strip):
        @pl.when(strip == 0)
        def _():
            of_strip((0, 1))

        @pl.when(strip == 1)
        def _():
            of_strip((2, 3))

    def regions(l):
        vm.send1[l] = dot(ld.to_region[...], ld.tokens[l]).astype(BF16).reshape(4, QUARTER, 512)
        send(0, l)

    loop(2, regions)
    partner_cot = remote(
        hbm.cotangent.at[pl.ds(6 - 6 * odd, 6)], vm.cot2.at[odd], 32, 0, device(0, 1 - 2 * odd)
    )
    partner_cot.start()
    left_mask = remote(hbm.mask_ids, vm.mask_left, 34, 0, device(0, 1))
    by_parity(left_mask.start, lambda: None)

    loads.fine_bias.wait()
    by_parity(lambda: None, left_mask.wait_recv)
    lanes = lax.broadcasted_iota(jnp.int32, (UNIT, 128), 1)
    subs = lax.broadcasted_iota(jnp.int32, (UNIT, 128), 0)
    past = jnp.where(lanes >= 72, MASKED, 0.0).astype(F32)
    for level in range(2):
        masks = [past]
        for ids in (vm.mask_left, hbm.mask_ids):
            spread = dot(hbm.id_col[...], ids[:, level, :].astype(F32))
            id_of = jnp.sum(spread * hbm.id_row[...], axis=-1, keepdims=True)
            id_at = dot(jnp.ones((8, UNIT), F32), jnp.where(lanes == subs, id_of, 0.0))[:1]
            masks.append(jnp.where(id_of == id_at, past, MASKED))
        for head in range(8):
            span = slice(72 * level, 72 * level + 72)
            block = ld.fine_bias[head, span, span]
            block = jnp.concatenate([block, jnp.zeros((72, 56), F32)], axis=1)
            block = jnp.concatenate([block, jnp.zeros((8, 128), F32)], axis=0)
            at = slice(UNIT * (head % 2), UNIT * (head % 2) + UNIT)
            for kind, mask in enumerate(masks):
                vm.bias_f[kind, level, head // 2, at, :] = block + mask

    loads.to_unit.wait()
    loads.fine_qkv.wait()
    loads.fine_out.wait()
    loads.to_unit_t.wait()

    def fine_forward(turn):
        strip = lax.rem(1 - odd + turn, 2)
        base = strip * 320
        level_at = lambda l: rows_at(base + l * 160, 160)
        both_levels = rows_at(base, 320)
        at_strip(strip, lambda keep: [take(0, l, keep) for l in range(2)])

        def fine_norm(l):
            source = vm.region[l, pl.ds(2 * strip, 2)].reshape(2 * QUARTER, 512)
            x = dot(ld.to_unit[...], source)
            hat, scale = normed_rows(x)
            vm.unit_x[level_at(l), :] = x.astype(BF16)
            vm.hat_f[level_at(l), :] = hat
            vm.scale_f[level_at(l), :] = jnp.broadcast_to(scale, (160, 128))
            vm.unit_n[level_at(l), :] = hat.astype(BF16)

        loop(2, fine_norm)

        def fine_project(t):
            cols = rows_at(t * 512, 512, 512)
            scale = jnp.where(t < 1, 0.125, 1.0).astype(F32)
            vm.proj[both_levels, cols] = (
                dot(vm.unit_n[both_levels, :], ld.fine_qkv[:, cols]) * scale
            ).astype(BF16)

        loop(3, fine_project)

        def fine_level(l):
            def fine_attend(m):
                last = odd * m * (1 + strip)
                start = base + l * 160 + m * UNIT
                at, wide = rows_at(start, UNIT), rows_at(start, 128)
                pairs = [slice(128 * p, 128 * p + 128) for p in range(4)]
                ones = jnp.ones((128, 128), BF16)
                scores = [
                    dot_nt(
                        two_heads(vm.proj[at, pair], vm.heads2), vm.proj[wide, 512 + pair.start : 512 + pair.stop]
                    )
                    + vm.bias_f[last, 1 - l, p]
                    for p, pair in enumerate(pairs)
                ]
                tops = [jnp.max(s, axis=-1, keepdims=True) for s in scores]
                raised = [jnp.exp(s - t).astype(BF16) for s, t in zip(scores, tops)]
                sums = [
                    dot(e, jnp.concatenate([vm.proj[wide, 1024 + pair.start : 1024 + pair.stop], ones], axis=1))
                    for e, pair in zip(raised, pairs)
                ]
                for p, pair in enumerate(pairs):
                    recip = 1.0 / one_row(sums[p][:, 128:])
                    vm.raised_f[strip * 4 + l * 2 + m, p] = raised[p]
                    vm.recip_f[at, pair] = recip
                    vm.heads_f[at, pair] = (one_row(sums[p][:, :128]) * recip).astype(BF16)

            loop(2, fine_attend)
            mixed = vm.unit_x[level_at(l), :].astype(F32) + dot(vm.heads_f[level_at(l), :], ld.fine_out[...])
            ordered = dot(ld.to_unit_t[...], mixed.astype(BF16)).astype(BF16)
            vm.send2[l, pl.ds(2 * strip, 2)] = ordered.reshape(2, QUARTER, 512)
            at_strip(strip, lambda keep: send(1, l, keep))

        loop(2, fine_level)

    loop(2, fine_forward)
    loads.coarse_bias.wait()

    def coarse_pad(h):
        vm.bias_c[h] = jnp.concatenate([ld.coarse_bias[h], jnp.full((144, 112), MASKED, F32)], axis=1)

    loop(16, coarse_pad)
    own_cot.wait()
    partner_cot.wait()
    loads.coarse.wait()
    vm.cot[...] = dot(ld.coarse[...], vm.cot2[...].reshape(144, 1024)).astype(BF16)
    loads.coarse_out.wait()

    def coarse_cot(t):
        cols = rows_at(t * 512, 512, 512)
        vm.grad_c[:, cols] = dot_nt(vm.cot[...], ld.coarse_out[cols, :])

    loop(2, coarse_cot)
    loads.merge.wait()
    loads.merge_weight.wait()
    loads.coarse_qkv.wait()
    loads.coarse_t.wait()

    def gather(l):
        take(1, l)
        source = vm.quarters[l].reshape(4 * QUARTER, 512)
        for k in range(4):
            vm.hat_m[rows_at(l * 72, 72, 8), 512 * k : 512 * k + 512] = dot(ld.merge[k], source)

    loop(2, gather)

    def merge_norm(t):
        at = rows_at(t * 48, 48)
        hat, scale = normed_rows(vm.hat_m[at, :])
        vm.hat_m[at, :] = hat
        vm.scale_m[at, :] = jnp.broadcast_to(scale, (48, 128))
        vm.normed_m[at, :] = hat.astype(BF16)

    loop(3, merge_norm)

    def merge_project(t):
        cols = rows_at(t * 512, 512, 512)
        vm.merged[:, cols] = dot(vm.normed_m[...], ld.merge_weight[:, cols]).astype(BF16)

    loop(2, merge_project)

    def coarse_norm(t):
        at = rows_at(t * 48, 48)
        hat, scale = normed_rows(vm.merged[at, :].astype(F32))
        vm.hat_c[at, :] = hat
        vm.scale_c[at, :] = jnp.broadcast_to(scale, (48, 128))
        vm.normed_c[at, :] = hat.astype(BF16)

    loop(3, coarse_norm)

    def coarse_project(t):
        cols = rows_at(t * 512, 512, 512)
        scale = jnp.where(t < 2, 0.125, 1.0).astype(F32)
        vm.proj_c[:144, cols] = (dot(vm.normed_c[...], ld.coarse_qkv[:, cols]) * scale).astype(BF16)

    loop(6, coarse_project)

    def cols_at(p, base):
        return rows_at(p * 128 + base, 128, 128)

    def coarse_attend(t):
        pairs = [2 * t, 2 * t + 1]
        ones = jnp.ones((256, 128), BF16)
        scores = [
            dot_nt(two_heads(vm.proj_c[:144, cols_at(p, 0)], vm.heads2_c), vm.proj_c[:, cols_at(p, 1024)])
            + vm.bias_c[pl.ds(2 * p, 2)].reshape(288, 256)
            for p in pairs
        ]
        tops = [jnp.max(s, axis=-1, keepdims=True) for s in scores]
        raised = [jnp.exp(s - top).astype(BF16) for s, top in zip(scores, tops)]
        sums = [
            dot(e, jnp.concatenate([vm.proj_c[:, cols_at(p, 2048)], ones], axis=1))
            for e, p in zip(raised, pairs)
        ]
        for p, e, total in zip(pairs, raised, sums):
            recip = 1.0 / one_row(total[:, 128:])
            vm.raised_c[p] = e
            vm.recip_c[:, cols_at(p, 0)] = recip
            vm.heads_c[:, cols_at(p, 0)] = (one_row(total[:, :128]) * recip).astype(BF16)

    loop(4, coarse_attend)

    def coarse_mix(t):
        cols = rows_at(t * 512, 512, 512)
        mixed = dot(vm.heads_c[...], ld.coarse_out[:, cols])
        vm.result[:, cols] = (vm.merged[:, cols].astype(F32) + mixed).astype(BF16)
        grad = vm.grad_c[:, cols] * vm.recip_c[:, cols]
        vm.dheads_c[:, cols] = grad.astype(BF16)
        vm.dprod_c[:, cols] = (grad * vm.heads_c[:, cols].astype(F32)).astype(BF16)

    loop(2, coarse_mix)

    vm.result2[...] = dot(ld.coarse_t[...], vm.result[...]).astype(BF16).reshape(2, 6, 6, 2, 1024)
    into = result_ref.at[pl.ds(6 * odd, 6)]
    result_near = pltpu.make_async_copy(vm.result2.at[odd], into, near_sem.at[17, 0])
    result_far = remote(vm.result2.at[1 - odd], into, 33, 0, device(0, 1 - 2 * odd))
    result_near.start()
    result_far.start()

    def coarse_attend_grad(t):
        pairs = [2 * t, 2 * t + 1]
        minus = jnp.full((256, 128), -1.0, BF16)
        grads = [two_heads(vm.dheads_c[:, cols_at(p, 0)], vm.heads2_c) for p in pairs]
        prods = [two_heads(vm.dprod_c[:, cols_at(p, 0)], vm.heads2_c) for p in pairs]
        queries = [two_heads(vm.proj_c[:144, cols_at(p, 0)], vm.heads2_c) for p in pairs]
        inner = [
            dot_nt(
                jnp.concatenate([g, d], axis=1), jnp.concatenate([vm.proj_c[:, cols_at(p, 2048)], minus], axis=1)
            )
            for p, g, d in zip(pairs, grads, prods)
        ]
        dscores = [(vm.raised_c[p].astype(F32) * x).astype(BF16) for p, x in zip(pairs, inner)]
        for p, g, q, ds in zip(pairs, grads, queries, dscores):
            vm.dproj_c[:, cols_at(p, 2048)] = dot_tn(vm.raised_c[p], g)[:144].astype(BF16)
            dq = one_row(dot(ds, vm.proj_c[:, cols_at(p, 1024)]))
            vm.dproj_c[:, cols_at(p, 0)] = (dq * 0.125).astype(BF16)
            vm.dproj_c[:, cols_at(p, 1024)] = dot_tn(ds, q)[:144].astype(BF16)

    loop(4, coarse_attend_grad)

    def coarse_project_grad(t):
        cols = rows_at(t * 512, 512, 512)
        vm.grad_c[:, cols] = dot_nt(vm.dproj_c[...], ld.coarse_qkv[cols, :])

    loop(2, coarse_project_grad)

    def coarse_norm_grad(t):
        at = rows_at(t * 48, 48)
        grad = norm_grad(vm.grad_c[at, :], vm.hat_c[at, :], vm.scale_c[at, :1])
        vm.dmerged[at, :] = (vm.cot[at, :].astype(F32) + grad).astype(BF16)

    loop(3, coarse_norm_grad)

    def merge_project_grad(t):
        cols = rows_at(t * 512, 512, 512)
        vm.grad_m[:, cols] = dot_nt(vm.dmerged[...], ld.merge_weight[cols, :])

    loop(4, merge_project_grad)
    loads.merge_t.wait()

    def scatter(l):
        at = rows_at(l * 72, 72, 8)
        grad = norm_grad(vm.grad_m[at, :], vm.hat_m[at, :], vm.scale_m[at, :1]).astype(BF16)
        total = dot(ld.merge_t[0], grad[:, :512])
        for k in range(1, 4):
            total = total + dot(ld.merge_t[k], grad[:, 512 * k : 512 * k + 512])
        vm.send3[l] = total.astype(BF16).reshape(4, QUARTER, 512)
        send(2, l)

    loop(2, scatter)
    loads.to_region_t.wait()

    def fine_backward(turn):
        strip = lax.rem(1 - odd + turn, 2)
        base = strip * 320
        level_at = lambda l: rows_at(base + l * 160, 160)
        both_levels = rows_at(base, 320)
        at_strip(strip, lambda keep: [take(2, l, keep) for l in range(2)])

        def fine_units(l):
            source = vm.part[l, pl.ds(2 * strip, 2)].reshape(2 * QUARTER, 512)
            vm.dmixed[level_at(l), :] = dot(ld.to_unit[...], source).astype(BF16)

        loop(2, fine_units)
        grad = dot_nt(vm.dmixed[both_levels, :], ld.fine_out[...]) * vm.recip_f[both_levels, :]
        vm.dheads_f[both_levels, :] = grad.astype(BF16)
        vm.dprod_f[both_levels, :] = (grad * vm.heads_f[both_levels, :].astype(F32)).astype(BF16)

        def fine_level_back(l):
            def fine_attend_grad(m):
                start = base + l * 160 + m * UNIT
                at, wide = rows_at(start, UNIT), rows_at(start, 128)
                pairs = [slice(128 * p, 128 * p + 128) for p in range(4)]
                minus = jnp.full((128, 128), -1.0, BF16)
                grads = [two_heads(vm.dheads_f[at, pair], vm.heads2) for pair in pairs]
                prods = [two_heads(vm.dprod_f[at, pair], vm.heads2) for pair in pairs]
                queries = [two_heads(vm.proj[at, pair], vm.heads2) for pair in pairs]
                inner = [
                    dot_nt(
                        jnp.concatenate([g, d], axis=1),
                        jnp.concatenate([vm.proj[wide, 1024 + pair.start : 1024 + pair.stop], minus], axis=1),
                    )
                    for pair, g, d in zip(pairs, grads, prods)
                ]
                raised = [vm.raised_f[strip * 4 + l * 2 + m, p] for p in range(4)]
                dscores = [(e.astype(F32) * x).astype(BF16) for e, x in zip(raised, inner)]
                dvalues = [dot_tn(e, g) for e, g in zip(raised, grads)]
                dkeys = [dot_tn(ds, q) for ds, q in zip(dscores, queries)]
                dqueries = [
                    dot(ds, vm.proj[wide, 512 + pair.start : 512 + pair.stop]) for pair, ds in zip(pairs, dscores)
                ]
                for p, pair in enumerate(pairs):
                    vm.dproj_f[at, pair] = (one_row(dqueries[p]) * 0.125).astype(BF16)
                    vm.dproj_f[at, 512 + pair.start : 512 + pair.stop] = dkeys[p][:UNIT].astype(BF16)
                    vm.dproj_f[at, 1024 + pair.start : 1024 + pair.stop] = dvalues[p][:UNIT].astype(BF16)

            loop(2, fine_attend_grad)
            grad = dot_nt(vm.dproj_f[level_at(l), :], ld.fine_qkv[...])
            grad = norm_grad(grad, vm.hat_f[level_at(l), :], vm.scale_f[level_at(l), :1])
            dunit = (vm.dmixed[level_at(l), :].astype(F32) + grad).astype(BF16)
            ordered = dot(ld.to_unit_t[...], dunit).astype(BF16)
            vm.send4[l, pl.ds(2 * strip, 2)] = ordered.reshape(2, QUARTER, 512)
            at_strip(strip, lambda keep: send(3, l, keep))

        loop(2, fine_level_back)

    loop(2, fine_backward)
    by_parity(left_mask.wait_send, lambda: None)
    result_near.wait()
    result_far.wait()

    def grid_back(l):
        take(3, l)
        grad_ref[l] = dot(ld.to_region_t[...], vm.region4[l].reshape(4 * QUARTER, 512)).astype(BF16)
        for phase in range(4):
            sent(phase, l)

    loop(2, grid_back)


PIECES = 2


def hand_over(*refs):
    ins, outs = [], []
    for n in range(2):
        src, dst, held = refs[n], refs[2 + n], refs[4 + n]
        size = src.shape[0] // PIECES
        for piece in range(PIECES):
            at = pl.ds(piece * size, size)
            ins.append(pltpu.make_async_copy(src.at[at], held.at[at], refs[6].at[n, piece]))
            outs.append(pltpu.make_async_copy(held.at[at], dst.at[at], refs[7].at[n, piece]))
    for copy in ins:
        copy.start()
    for before, after in zip(ins, outs):
        before.wait()
        after.start()
    for copy in outs:
        copy.wait()


def per_device(n_lat, n_lon, *args):
    tokens, mask_ids, *middle, cotangent = args
    tokens = tokens.transpose(0, 2, 1, 3).reshape(2, 288, 512)
    operands = [tokens, mask_ids.transpose(2, 0, 1), *middle, cotangent.transpose(1, 2, 0, 3)]
    operands += [jnp.asarray(m) for m in row_orders()]
    shapes = dict(zip(ARGS, [(x.shape, x.dtype) for x in operands]))
    loaded = [
        pltpu.VMEM(shapes[name][0][1:] if paired else shapes[name][0], shapes[name][1])
        for name, paired in LOADED.items()
    ]
    result, grad = pl.pallas_call(
        functools.partial(kernel, n_lat, n_lon),
        out_shape=(
            jax.ShapeDtypeStruct((12, 6, 2, 1024), BF16),
            jax.ShapeDtypeStruct((2, 288, 512), BF16),
        ),
        in_specs=[
            pl.BlockSpec(memory_space=pltpu.VMEM if placed == 1 else pl.ANY) for placed in ARGS.values()
        ],
        out_specs=(pl.BlockSpec(memory_space=pltpu.VMEM), pl.BlockSpec(memory_space=pltpu.VMEM)),
        scratch_shapes=[pltpu.VMEM(*spec) for spec in SCRATCH.values()]
        + loaded
        + [
            pltpu.SemaphoreType.DMA((len(LOADED),)),
            pltpu.SemaphoreType.DMA((35, 2)),
            pltpu.SemaphoreType.DMA((35, 2)),
            pltpu.SemaphoreType.DMA((18, 2)),
        ],
        compiler_params=pltpu.CompilerParams(
            collective_id=0, has_side_effects=True, vmem_limit_bytes=60 * 2**20
        ),
    )(*operands)
    anywhere = pl.BlockSpec(memory_space=pl.ANY)
    result, grad = pl.pallas_call(
        hand_over,
        out_shape=(
            jax.ShapeDtypeStruct((12, 6, 2, 1024), BF16),
            jax.ShapeDtypeStruct((8, 72, 512), BF16),
        ),
        in_specs=[anywhere, anywhere],
        out_specs=(anywhere, anywhere),
        scratch_shapes=[
            pltpu.VMEM((12, 6, 2, 1024), BF16),
            pltpu.VMEM((8, 72, 512), BF16),
            pltpu.SemaphoreType.DMA((2, PIECES)),
            pltpu.SemaphoreType.DMA((2, PIECES)),
        ],
        compiler_params=pltpu.CompilerParams(vmem_limit_bytes=60 * 2**20),
    )(result, grad.reshape(8, 72, 512))
    return result.transpose(2, 0, 1, 3), grad.reshape(2, 12, 24, 512).transpose(0, 2, 1, 3)


def solution(mesh):
    grid = P(None, "lat", "lon", None)
    placed = (grid, P(None, "lat", "lon"), P(), P(), P(), P(), P(), P(), P(), grid)
    return jax.shard_map(
        functools.partial(per_device, mesh.shape["lat"], mesh.shape["lon"]),
        mesh=mesh,
        in_specs=placed,
        out_specs=(grid, grid),
        check_vma=False,
    )
```

```python
import functools

import jax
import jax.numpy as jnp
import numpy as np
from jax import lax
from jax.experimental import pallas as pl
from jax.experimental.pallas import tpu as pltpu
from jax.sharding import PartitionSpec as P

F32 = jnp.float32
BF16 = jnp.bfloat16
EPSILON = 1e-05
MASKED = -1e30
MESH = pl.DeviceIdType.MESH

UNIT = 80
QUARTER = 96
NEIGHBOURS = [(a, b) for a in (-1, 0, 1) for b in (-1, 0, 1) if (a, b) != (0, 0)] + [(0, 2), (0, -2)]


def one_hot(pairs, rows, columns):
    out = np.zeros((rows, columns), np.float32)
    for r, c in pairs:
        out[r, c] = 1.0
    return out


def in_quarter(row, col):
    return row * 6 + col if row < 9 else 64 + (row - 9) * 6 + col


@functools.cache
def row_orders():
    to_region = np.zeros((2, 4 * QUARTER, 288), np.float32)
    for odd in range(2):
        for half in range(2):
            for c in range(6):
                for a in range(12):
                    col = 24 * (6 * half + c)
                    upper = a + 3
                    lower = a + 15 if a < 9 else a - 9
                    kept, sent = (lower, upper) if odd else (upper, lower)
                    to_region[odd, half * QUARTER + in_quarter(a, c), col + kept] = 1.0
                    to_region[odd, (2 + half) * QUARTER + in_quarter(a, c), col + sent] = 1.0
    to_unit = one_hot(
        [
            (UNIT * (a // 6) + 12 * (a % 6) + o, (o // 6) * QUARTER + in_quarter(a, o % 6))
            for a in range(12)
            for o in range(12)
        ],
        2 * UNIT,
        2 * QUARTER,
    )
    merge = np.zeros((4 * 72, 4 * QUARTER), np.float32)
    for k, (dr, dc) in enumerate([(0, 0), (1, 0), (0, 1), (1, 1)]):
        for r in range(6):
            for c in range(12):
                quarter, col = divmod(2 * c + dc, 6)
                a = 2 * r + dr
                at = 64 + a * 6 + col if a < 3 else (a - 3) * 6 + col
                merge[k * 72 + r * 12 + c, quarter * QUARTER + at] = 1.0
    coarse = one_hot(
        [
            (l * 72 + r * 12 + c, (((c // 6) * 6 + r) * 6 + c % 6) * 2 + l)
            for l in range(2)
            for r in range(6)
            for c in range(12)
        ],
        144,
        144,
    )
    id_row = one_hot([(t, t // 12 + 18) for t in range(72)], UNIT, 24)
    id_col = one_hot([(t, t % 12) for t in range(72)], UNIT, 12)
    both = lambda m: [m, np.swapaxes(m, -1, -2)]
    orders = both(to_region) + both(to_unit) + both(merge) + both(coarse)
    return [np.ascontiguousarray(m).astype(jnp.bfloat16) for m in orders] + [id_row, id_col]


def dot(a, b):
    return lax.dot_general(a, b, (((1,), (0,)), ((), ())), preferred_element_type=F32)


def dot_nt(a, b):
    return lax.dot_general(a, b, (((1,), (1,)), ((), ())), preferred_element_type=F32)


def dot_tn(a, b):
    return lax.dot_general(a, b, (((0,), (0,)), ((), ())), preferred_element_type=F32)


def normed_rows(x):
    center = x - jnp.mean(x, axis=-1, keepdims=True)
    scale = lax.rsqrt(jnp.mean(center * center, axis=-1, keepdims=True) + EPSILON)
    return center * scale, scale


def norm_grad(grad, hat, scale):
    inner = jnp.mean(grad * hat, axis=-1, keepdims=True)
    return scale * (grad - jnp.mean(grad, axis=-1, keepdims=True) - hat * inner)


def one_row(x):
    span = x.shape[0] // 2
    low = lax.broadcasted_iota(jnp.int32, (span, 128), 1) < 64
    return jnp.where(low, x[:span], x[span:])


def rows_at(start, size, unit=16):
    return pl.ds(pl.multiple_of(start, unit), size)


def loop(count, body):
    lax.fori_loop(0, count, lambda t, c: (body(t), c)[1], 0)


class Box:
    def __init__(self, **fields):
        self.__dict__.update(fields)


ARGS = dict(
    tokens=0, mask_ids=1, fine_bias=0, fine_qkv=0, fine_out=0, merge_weight=0, coarse_bias=0, coarse_qkv=0,
    coarse_out=0, cotangent=2, to_region=0, to_region_t=0, to_unit=0, to_unit_t=0,
    merge=0, merge_t=0, coarse=0, coarse_t=0, id_row=1, id_col=1,
)
LOADED = dict(
    tokens=0, to_region=1, fine_bias=0, to_unit=0, fine_qkv=0, fine_out=0, to_unit_t=0, coarse=0, coarse_bias=0,
    coarse_out=0, merge=0, merge_weight=0, coarse_qkv=0, coarse_t=0, merge_t=0, to_region_t=1,
)
SCRATCH = dict(
    heads2=((160, 128), BF16),
    heads2_c=((288, 128), BF16),
    send1=((2, 4, QUARTER, 512), BF16),
    region=((2, 4, QUARTER, 512), BF16),
    unit_x=((640, 512), BF16),
    unit_n=((640, 512), BF16),
    hat_f=((640, 512), F32),
    scale_f=((640, 128), F32),
    proj=((704, 1536), BF16),
    mask_left=((12, 2, 24), jnp.int32),
    bias_f=((3, 2, 4, 160, 128), F32),
    raised_f=((8, 4, 160, 128), BF16),
    recip_f=((640, 512), F32),
    heads_f=((640, 512), BF16),
    send2=((2, 4, QUARTER, 512), BF16),
    quarters=((2, 4, QUARTER, 512), BF16),
    hat_m=((144, 2048), F32),
    scale_m=((144, 128), F32),
    normed_m=((144, 2048), BF16),
    merged=((144, 1024), BF16),
    hat_c=((144, 1024), F32),
    scale_c=((144, 128), F32),
    normed_c=((144, 1024), BF16),
    proj_c=((256, 3072), BF16),
    bias_c=((16, 144, 256), F32),
    raised_c=((8, 288, 256), BF16),
    recip_c=((144, 1024), F32),
    heads_c=((144, 1024), BF16),
    result=((144, 1024), BF16),
    result2=((2, 6, 6, 2, 1024), BF16),
    cot2=((2, 6, 6, 2, 1024), BF16),
    cot=((144, 1024), BF16),
    dheads_c=((144, 1024), BF16),
    dprod_c=((144, 1024), BF16),
    dproj_c=((144, 3072), BF16),
    grad_c=((144, 1024), F32),
    dmerged=((144, 1024), BF16),
    grad_m=((144, 2048), F32),
    send3=((2, 4, QUARTER, 512), BF16),
    part=((2, 4, QUARTER, 512), BF16),
    dmixed=((640, 512), BF16),
    dheads_f=((640, 512), BF16),
    dprod_f=((640, 512), BF16),
    dproj_f=((640, 1536), BF16),
    send4=((2, 4, QUARTER, 512), BF16),
    region4=((2, 4, QUARTER, 512), BF16),
)
def kernel(n_lat, n_lon, *refs):
    rest = list(refs)
    hbm = Box(**{name: rest.pop(0) for name in ARGS})
    result_ref, grad_ref = rest.pop(0), rest.pop(0)
    vm = Box(**{name: rest.pop(0) for name in SCRATCH})
    ld = Box(**{name: rest.pop(0) for name in LOADED})
    load_sem, send_sem, recv_sem, near_sem = rest

    i, j = lax.axis_index("lat"), lax.axis_index("lon")
    odd = lax.rem(j, 2)
    even = odd == 0

    def device(di, dj):
        return (lax.rem(i + di + n_lat, n_lat), lax.rem(j + dj + n_lon, n_lon))

    def remote(src, dst, sem, l, target):
        return pltpu.make_async_remote_copy(
            src_ref=src,
            dst_ref=dst,
            send_sem=send_sem.at[sem, l],
            recv_sem=recv_sem.at[sem, l],
            device_id=target,
            device_id_type=MESH,
        )

    vm.mask_left[...] = jnp.zeros((12, 2, 24), jnp.int32)
    barrier = pltpu.get_barrier_semaphore()
    for di, dj in NEIGHBOURS:
        pl.semaphore_signal(barrier, inc=1, device_id=device(di, dj), device_id_type=MESH)

    loads = Box()
    for at, (name, paired) in enumerate(LOADED.items()):
        src = getattr(hbm, name)
        if paired:
            src = src.at[odd]
        copy = pltpu.make_async_copy(src, getattr(ld, name), load_sem.at[at])
        copy.start()
        setattr(loads, name, copy)
    own_cot = pltpu.make_async_copy(
        hbm.cotangent.at[pl.ds(6 * odd, 6)], vm.cot2.at[odd], near_sem.at[16, 0]
    )
    own_cot.start()

    for end in (320, 640):
        vm.proj[end : end + 64, :] = jnp.zeros((64, 1536), BF16)
    vm.proj_c[144:, :] = jnp.zeros((112, 3072), BF16)
    for ref in (vm.heads2, vm.heads2_c):
        low = lax.broadcasted_iota(jnp.int32, ref.shape, 1) < 64
        first = lax.broadcasted_iota(jnp.int32, ref.shape, 0) < ref.shape[0] // 2
        ref[...] = jnp.where(low == first, 1.0, 0.0).astype(BF16)

    def two_heads(x, mask):
        return jnp.concatenate([x, x], axis=0) * mask[...]

    loads.tokens.wait()
    loads.to_region.wait()
    pl.semaphore_wait(barrier, len(NEIGHBOURS))

    whole, top, low = (0, 96), (0, 64), (64, 32)
    left, right, far_left, far_right = (0, -1), (0, 1), (0, -2), (0, 2)
    plans = [
        (
            vm.send1,
            vm.region,
            [
                (2, 3, low, (-1, -1)), (3, 0, low, (-1, 1)), (2, 3, top, left), (3, 0, top, right),
                (0, 1, whole, None), (1, 2, whole, None),
            ],
            [
                (0, 1, low, (-1, 0)), (1, 2, low, (-1, 0)), (2, 3, whole, left), (3, 0, whole, right),
                (0, 1, top, None), (1, 2, top, None),
            ],
        ),
        (
            vm.send2,
            vm.quarters,
            [
                (0, 3, top, far_left), (0, 3, low, left), (1, 0, low, right), (2, 1, low, right),
                (3, 2, low, right), (1, 0, top, None), (2, 1, top, None), (3, 2, top, None),
            ],
            [
                (3, 0, top, far_right), (3, 0, low, (1, 1)), (0, 1, low, (1, -1)), (1, 2, low, (1, -1)),
                (2, 3, low, (1, -1)), (0, 1, top, None), (1, 2, top, None), (2, 3, top, None),
            ],
        ),
    ]
    for (_, _, of_even, of_odd), src, dst in ((plans[1], vm.send3, vm.part), (plans[0], vm.send4, vm.region4)):
        back_even, back_odd = [], []
        for mine, ours in ((of_even, 0), (of_odd, 1)):
            for at, into, rows, to in mine:
                if to is None:
                    target = ours
                    way = None
                else:
                    target = (ours + to[1]) % 2
                    way = (-to[0], -to[1])
                (back_odd if target else back_even).append((into, at, rows, way))
        plans.append((src, dst, back_even, back_odd))

    def transfer(phase, l, plan):
        at, into, (start, size), to = plan
        src, dst = plans[phase][:2]
        src, dst = src.at[l, at, pl.ds(start, size)], dst.at[l, into, pl.ds(start, size)]
        sem = phase * 8 + into * 2 + (start > 0)
        if to is None:
            return pltpu.make_async_copy(src, dst, near_sem.at[phase * 4 + into, l])
        return remote(src, dst, sem, l, device(*to))

    def by_parity(of_even, of_odd):
        @pl.when(even)
        def _():
            of_even()

        @pl.when(odd == 1)
        def _():
            of_odd()

    def send(phase, l, keep=None):
        def start(mine):
            for plan in mine:
                if keep is None or plan[0] in keep:
                    transfer(phase, l, plan).start()

        by_parity(lambda: start(plans[phase][2]), lambda: start(plans[phase][3]))

    def arrivals(phase, parity):
        got = []
        for ours in range(2):
            for plan in plans[phase][2 + ours]:
                to = plan[3]
                if (ours if to is None else (ours + to[1]) % 2) == parity:
                    got.append(plan)
        return got

    def take(phase, l, keep=None):
        def wait(parity):
            for plan in arrivals(phase, parity):
                if keep is None or plan[1] in keep:
                    copy = transfer(phase, l, plan)
                    copy.wait() if plan[3] is None else copy.wait_recv()

        by_parity(lambda: wait(0), lambda: wait(1))

    def sent(phase, l):
        def wait(mine):
            for plan in mine:
                if plan[3] is not None:
                    transfer(phase, l, plan).wait_send()

        by_parity(lambda: wait(plans[phase][2]), lambda: wait(plans[phase][3]))

    def at_strip(strip, of_strip):
        @pl.when(strip == 0)
        def _():
            of_strip((0, 1))

        @pl.when(strip == 1)
        def _():
            of_strip((2, 3))

    def regions(l):
        vm.send1[l] = dot(ld.to_region[...], ld.tokens[l]).astype(BF16).reshape(4, QUARTER, 512)
        send(0, l)

    loop(2, regions)
    partner_cot = remote(
        hbm.cotangent.at[pl.ds(6 - 6 * odd, 6)], vm.cot2.at[odd], 32, 0, device(0, 1 - 2 * odd)
    )
    partner_cot.start()
    left_mask = remote(hbm.mask_ids, vm.mask_left, 34, 0, device(0, 1))
    by_parity(left_mask.start, lambda: None)

    loads.fine_bias.wait()
    by_parity(lambda: None, left_mask.wait_recv)
    lanes = lax.broadcasted_iota(jnp.int32, (UNIT, 128), 1)
    subs = lax.broadcasted_iota(jnp.int32, (UNIT, 128), 0)
    past = jnp.where(lanes >= 72, MASKED, 0.0).astype(F32)
    for level in range(2):
        masks = [past]
        for ids in (vm.mask_left, hbm.mask_ids):
            spread = dot(hbm.id_col[...], ids[:, level, :].astype(F32))
            id_of = jnp.sum(spread * hbm.id_row[...], axis=-1, keepdims=True)
            id_at = dot(jnp.ones((8, UNIT), F32), jnp.where(lanes == subs, id_of, 0.0))[:1]
            masks.append(jnp.where(id_of == id_at, past, MASKED))
        for head in range(8):
            span = slice(72 * level, 72 * level + 72)
            block = ld.fine_bias[head, span, span]
            block = jnp.concatenate([block, jnp.zeros((72, 56), F32)], axis=1)
            block = jnp.concatenate([block, jnp.zeros((8, 128), F32)], axis=0)
            at = slice(UNIT * (head % 2), UNIT * (head % 2) + UNIT)
            for kind, mask in enumerate(masks):
                vm.bias_f[kind, level, head // 2, at, :] = block + mask

    loads.to_unit.wait()
    loads.fine_qkv.wait()
    loads.fine_out.wait()
    loads.to_unit_t.wait()

    def fine_forward(turn):
        strip = lax.rem(1 - odd + turn, 2)
        base = strip * 320
        level_at = lambda l: rows_at(base + l * 160, 160)
        both_levels = rows_at(base, 320)
        at_strip(strip, lambda keep: [take(0, l, keep) for l in range(2)])

        for l in range(2):
            source = vm.region[l, pl.ds(2 * strip, 2)].reshape(2 * QUARTER, 512)
            x = dot(ld.to_unit[...], source)
            hat, scale = normed_rows(x)
            vm.unit_x[level_at(l), :] = x.astype(BF16)
            vm.hat_f[level_at(l), :] = hat
            vm.scale_f[level_at(l), :] = jnp.broadcast_to(scale, (160, 128))
            vm.unit_n[level_at(l), :] = hat.astype(BF16)

        projected = dot(vm.unit_n[both_levels, :], ld.fine_qkv[...])
        vm.proj[both_levels, :512] = (projected[:, :512] * 0.125).astype(BF16)
        vm.proj[both_levels, 512:] = projected[:, 512:].astype(BF16)

        def fine_attend(n):
            l, m = lax.div(n, 2), lax.rem(n, 2)
            last = odd * m * (1 + strip)
            start = base + n * UNIT
            at, wide = rows_at(start, UNIT), rows_at(start, 128)
            pairs = [slice(128 * p, 128 * p + 128) for p in range(4)]
            ones = jnp.ones((128, 128), BF16)
            scores = [
                dot_nt(
                    two_heads(vm.proj[at, pair], vm.heads2), vm.proj[wide, 512 + pair.start : 512 + pair.stop]
                )
                + vm.bias_f[last, 1 - l, p]
                for p, pair in enumerate(pairs)
            ]
            tops = [jnp.max(s, axis=-1, keepdims=True) for s in scores]
            raised = [jnp.exp(s - t).astype(BF16) for s, t in zip(scores, tops)]
            sums = [
                dot(e, jnp.concatenate([vm.proj[wide, 1024 + pair.start : 1024 + pair.stop], ones], axis=1))
                for e, pair in zip(raised, pairs)
            ]
            for p, pair in enumerate(pairs):
                recip = 1.0 / one_row(sums[p][:, 128:])
                vm.raised_f[strip * 4 + n, p] = raised[p]
                vm.recip_f[at, pair] = recip
                vm.heads_f[at, pair] = (one_row(sums[p][:, :128]) * recip).astype(BF16)

        loop(4, fine_attend)
        mixed = vm.unit_x[both_levels, :].astype(F32) + dot(vm.heads_f[both_levels, :], ld.fine_out[...])
        mixed = mixed.astype(BF16)
        for l in range(2):
            ordered = dot(ld.to_unit_t[...], mixed[160 * l : 160 * l + 160]).astype(BF16)
            vm.send2[l, pl.ds(2 * strip, 2)] = ordered.reshape(2, QUARTER, 512)
            at_strip(strip, lambda keep: send(1, l, keep))

    loop(2, fine_forward)
    loads.coarse_bias.wait()

    def coarse_pad(h):
        vm.bias_c[h] = jnp.concatenate([ld.coarse_bias[h], jnp.full((144, 112), MASKED, F32)], axis=1)

    loop(16, coarse_pad)
    own_cot.wait()
    partner_cot.wait()
    loads.coarse.wait()
    vm.cot[...] = dot(ld.coarse[...], vm.cot2[...].reshape(144, 1024)).astype(BF16)
    loads.coarse_out.wait()

    vm.grad_c[...] = dot_nt(vm.cot[...], ld.coarse_out[...])
    loads.merge.wait()
    loads.merge_weight.wait()
    loads.coarse_qkv.wait()
    loads.coarse_t.wait()

    for l in range(2):
        take(1, l)
    for l in range(2):
        gathered = dot(ld.merge[...], vm.quarters[l].reshape(4 * QUARTER, 512))
        for k in range(4):
            vm.hat_m[72 * l : 72 * l + 72, 512 * k : 512 * k + 512] = gathered[72 * k : 72 * k + 72]

    def merge_norm(t):
        at = rows_at(t * 48, 48)
        hat, scale = normed_rows(vm.hat_m[at, :])
        vm.hat_m[at, :] = hat
        vm.scale_m[at, :] = jnp.broadcast_to(scale, (48, 128))
        vm.normed_m[at, :] = hat.astype(BF16)

    loop(3, merge_norm)

    vm.merged[...] = dot(vm.normed_m[...], ld.merge_weight[...]).astype(BF16)

    def coarse_norm(t):
        at = rows_at(t * 48, 48)
        hat, scale = normed_rows(vm.merged[at, :].astype(F32))
        vm.hat_c[at, :] = hat
        vm.scale_c[at, :] = jnp.broadcast_to(scale, (48, 128))
        vm.normed_c[at, :] = hat.astype(BF16)

    loop(3, coarse_norm)

    projected = dot(vm.normed_c[...], ld.coarse_qkv[...])
    vm.proj_c[:144, :1024] = (projected[:, :1024] * 0.125).astype(BF16)
    vm.proj_c[:144, 1024:] = projected[:, 1024:].astype(BF16)

    def cols_at(p, base):
        return rows_at(p * 128 + base, 128, 128)

    def coarse_attend(t):
        pairs = [2 * t, 2 * t + 1]
        ones = jnp.ones((256, 128), BF16)
        scores = [
            dot_nt(two_heads(vm.proj_c[:144, cols_at(p, 0)], vm.heads2_c), vm.proj_c[:, cols_at(p, 1024)])
            + vm.bias_c[pl.ds(2 * p, 2)].reshape(288, 256)
            for p in pairs
        ]
        tops = [jnp.max(s, axis=-1, keepdims=True) for s in scores]
        raised = [jnp.exp(s - top).astype(BF16) for s, top in zip(scores, tops)]
        sums = [
            dot(e, jnp.concatenate([vm.proj_c[:, cols_at(p, 2048)], ones], axis=1))
            for e, p in zip(raised, pairs)
        ]
        for p, e, total in zip(pairs, raised, sums):
            recip = 1.0 / one_row(total[:, 128:])
            vm.raised_c[p] = e
            vm.recip_c[:, cols_at(p, 0)] = recip
            vm.heads_c[:, cols_at(p, 0)] = (one_row(total[:, :128]) * recip).astype(BF16)

    loop(4, coarse_attend)

    mixed = dot(vm.heads_c[...], ld.coarse_out[...])
    vm.result[...] = (vm.merged[...].astype(F32) + mixed).astype(BF16)
    grad = vm.grad_c[...] * vm.recip_c[...]
    vm.dheads_c[...] = grad.astype(BF16)
    vm.dprod_c[...] = (grad * vm.heads_c[...].astype(F32)).astype(BF16)
    vm.result2[...] = dot(ld.coarse_t[...], vm.result[...]).astype(BF16).reshape(2, 6, 6, 2, 1024)
    into = result_ref.at[pl.ds(6 * odd, 6)]
    result_near = pltpu.make_async_copy(vm.result2.at[odd], into, near_sem.at[17, 0])
    result_far = remote(vm.result2.at[1 - odd], into, 33, 0, device(0, 1 - 2 * odd))
    result_near.start()
    result_far.start()

    def coarse_attend_grad(t):
        pairs = [2 * t, 2 * t + 1]
        minus = jnp.full((256, 128), -1.0, BF16)
        grads = [two_heads(vm.dheads_c[:, cols_at(p, 0)], vm.heads2_c) for p in pairs]
        prods = [two_heads(vm.dprod_c[:, cols_at(p, 0)], vm.heads2_c) for p in pairs]
        queries = [two_heads(vm.proj_c[:144, cols_at(p, 0)], vm.heads2_c) for p in pairs]
        inner = [
            dot_nt(
                jnp.concatenate([g, d], axis=1), jnp.concatenate([vm.proj_c[:, cols_at(p, 2048)], minus], axis=1)
            )
            for p, g, d in zip(pairs, grads, prods)
        ]
        dscores = [(vm.raised_c[p].astype(F32) * x).astype(BF16) for p, x in zip(pairs, inner)]
        for p, g, q, ds in zip(pairs, grads, queries, dscores):
            vm.dproj_c[:, cols_at(p, 2048)] = dot_tn(vm.raised_c[p], g)[:144].astype(BF16)
            dq = one_row(dot(ds, vm.proj_c[:, cols_at(p, 1024)]))
            vm.dproj_c[:, cols_at(p, 0)] = (dq * 0.125).astype(BF16)
            vm.dproj_c[:, cols_at(p, 1024)] = dot_tn(ds, q)[:144].astype(BF16)

    loop(4, coarse_attend_grad)

    vm.grad_c[...] = dot_nt(vm.dproj_c[...], ld.coarse_qkv[...])

    def coarse_norm_grad(t):
        at = rows_at(t * 48, 48)
        grad = norm_grad(vm.grad_c[at, :], vm.hat_c[at, :], vm.scale_c[at, :1])
        vm.dmerged[at, :] = (vm.cot[at, :].astype(F32) + grad).astype(BF16)

    loop(3, coarse_norm_grad)

    vm.grad_m[...] = dot_nt(vm.dmerged[...], ld.merge_weight[...])
    loads.merge_t.wait()

    for l in range(2):
        at = slice(72 * l, 72 * l + 72)
        grad = norm_grad(vm.grad_m[at, :], vm.hat_m[at, :], vm.scale_m[at, :1])
        grad = jnp.concatenate([grad[:, 512 * k : 512 * k + 512] for k in range(4)], axis=0)
        vm.send3[l] = dot(ld.merge_t[...], grad.astype(BF16)).astype(BF16).reshape(4, QUARTER, 512)
        send(2, l)
    loads.to_region_t.wait()

    def fine_backward(turn):
        strip = lax.rem(1 - odd + turn, 2)
        base = strip * 320
        level_at = lambda l: rows_at(base + l * 160, 160)
        both_levels = rows_at(base, 320)
        at_strip(strip, lambda keep: [take(2, l, keep) for l in range(2)])

        for l in range(2):
            source = vm.part[l, pl.ds(2 * strip, 2)].reshape(2 * QUARTER, 512)
            vm.dmixed[level_at(l), :] = dot(ld.to_unit[...], source).astype(BF16)

        grad = dot_nt(vm.dmixed[both_levels, :], ld.fine_out[...]) * vm.recip_f[both_levels, :]
        vm.dheads_f[both_levels, :] = grad.astype(BF16)
        vm.dprod_f[both_levels, :] = (grad * vm.heads_f[both_levels, :].astype(F32)).astype(BF16)

        def fine_attend_grad(n):
            start = base + n * UNIT
            at, wide = rows_at(start, UNIT), rows_at(start, 128)
            pairs = [slice(128 * p, 128 * p + 128) for p in range(4)]
            minus = jnp.full((128, 128), -1.0, BF16)
            grads = [two_heads(vm.dheads_f[at, pair], vm.heads2) for pair in pairs]
            prods = [two_heads(vm.dprod_f[at, pair], vm.heads2) for pair in pairs]
            queries = [two_heads(vm.proj[at, pair], vm.heads2) for pair in pairs]
            inner = [
                dot_nt(
                    jnp.concatenate([g, d], axis=1),
                    jnp.concatenate([vm.proj[wide, 1024 + pair.start : 1024 + pair.stop], minus], axis=1),
                )
                for pair, g, d in zip(pairs, grads, prods)
            ]
            raised = [vm.raised_f[strip * 4 + n, p] for p in range(4)]
            dscores = [(e.astype(F32) * x).astype(BF16) for e, x in zip(raised, inner)]
            dvalues = [dot_tn(e, g) for e, g in zip(raised, grads)]
            dkeys = [dot_tn(ds, q) for ds, q in zip(dscores, queries)]
            dqueries = [
                dot(ds, vm.proj[wide, 512 + pair.start : 512 + pair.stop]) for pair, ds in zip(pairs, dscores)
            ]
            for p, pair in enumerate(pairs):
                vm.dproj_f[at, pair] = (one_row(dqueries[p]) * 0.125).astype(BF16)
                vm.dproj_f[at, 512 + pair.start : 512 + pair.stop] = dkeys[p][:UNIT].astype(BF16)
                vm.dproj_f[at, 1024 + pair.start : 1024 + pair.stop] = dvalues[p][:UNIT].astype(BF16)

        loop(4, fine_attend_grad)
        grad = dot_nt(vm.dproj_f[both_levels, :], ld.fine_qkv[...])
        grad = norm_grad(grad, vm.hat_f[both_levels, :], vm.scale_f[both_levels, :1])
        dunit = (vm.dmixed[both_levels, :].astype(F32) + grad).astype(BF16)
        for l in range(2):
            ordered = dot(ld.to_unit_t[...], dunit[160 * l : 160 * l + 160]).astype(BF16)
            vm.send4[l, pl.ds(2 * strip, 2)] = ordered.reshape(2, QUARTER, 512)
            at_strip(strip, lambda keep: send(3, l, keep))

    loop(2, fine_backward)
    by_parity(left_mask.wait_send, lambda: None)
    result_near.wait()
    result_far.wait()

    def grid_back(l):
        take(3, l)
        grad_ref[l] = dot(ld.to_region_t[...], vm.region4[l].reshape(4 * QUARTER, 512)).astype(BF16)
        for phase in range(4):
            sent(phase, l)

    loop(2, grid_back)


PIECES = 2


def hand_over(*refs):
    ins, outs = [], []
    for n in range(2):
        src, dst, held = refs[n], refs[2 + n], refs[4 + n]
        size = src.shape[0] // PIECES
        for piece in range(PIECES):
            at = pl.ds(piece * size, size)
            ins.append(pltpu.make_async_copy(src.at[at], held.at[at], refs[6].at[n, piece]))
            outs.append(pltpu.make_async_copy(held.at[at], dst.at[at], refs[7].at[n, piece]))
    for copy in ins:
        copy.start()
    for before, after in zip(ins, outs):
        before.wait()
        after.start()
    for copy in outs:
        copy.wait()


def per_device(n_lat, n_lon, *args):
    tokens, mask_ids, *middle, cotangent = args
    tokens = tokens.transpose(0, 2, 1, 3).reshape(2, 288, 512)
    operands = [tokens, mask_ids.transpose(2, 0, 1), *middle, cotangent.transpose(1, 2, 0, 3)]
    operands += [jnp.asarray(m) for m in row_orders()]
    shapes = dict(zip(ARGS, [(x.shape, x.dtype) for x in operands]))
    loaded = [
        pltpu.VMEM(shapes[name][0][1:] if paired else shapes[name][0], shapes[name][1])
        for name, paired in LOADED.items()
    ]
    result, grad = pl.pallas_call(
        functools.partial(kernel, n_lat, n_lon),
        out_shape=(
            jax.ShapeDtypeStruct((12, 6, 2, 1024), BF16),
            jax.ShapeDtypeStruct((2, 288, 512), BF16),
        ),
        in_specs=[
            pl.BlockSpec(memory_space=pltpu.VMEM if placed == 1 else pl.ANY) for placed in ARGS.values()
        ],
        out_specs=(pl.BlockSpec(memory_space=pltpu.VMEM), pl.BlockSpec(memory_space=pltpu.VMEM)),
        scratch_shapes=[pltpu.VMEM(*spec) for spec in SCRATCH.values()]
        + loaded
        + [
            pltpu.SemaphoreType.DMA((len(LOADED),)),
            pltpu.SemaphoreType.DMA((35, 2)),
            pltpu.SemaphoreType.DMA((35, 2)),
            pltpu.SemaphoreType.DMA((18, 2)),
        ],
        compiler_params=pltpu.CompilerParams(
            collective_id=0, has_side_effects=True, vmem_limit_bytes=60 * 2**20
        ),
    )(*operands)
    anywhere = pl.BlockSpec(memory_space=pl.ANY)
    result, grad = pl.pallas_call(
        hand_over,
        out_shape=(
            jax.ShapeDtypeStruct((12, 6, 2, 1024), BF16),
            jax.ShapeDtypeStruct((8, 72, 512), BF16),
        ),
        in_specs=[anywhere, anywhere],
        out_specs=(anywhere, anywhere),
        scratch_shapes=[
            pltpu.VMEM((12, 6, 2, 1024), BF16),
            pltpu.VMEM((8, 72, 512), BF16),
            pltpu.SemaphoreType.DMA((2, PIECES)),
            pltpu.SemaphoreType.DMA((2, PIECES)),
        ],
        compiler_params=pltpu.CompilerParams(vmem_limit_bytes=60 * 2**20),
    )(result, grad.reshape(8, 72, 512))
    return result.transpose(2, 0, 1, 3), grad.reshape(2, 12, 24, 512).transpose(0, 2, 1, 3)


def solution(mesh):
    grid = P(None, "lat", "lon", None)
    placed = (grid, P(None, "lat", "lon"), P(), P(), P(), P(), P(), P(), P(), grid)
    return jax.shard_map(
        functools.partial(per_device, mesh.shape["lat"], mesh.shape["lon"]),
        mesh=mesh,
        in_specs=placed,
        out_specs=(grid, grid),
        check_vma=False,
    )
```

```python
import functools

import jax
import jax.numpy as jnp
import numpy as np
from jax import lax
from jax.experimental import pallas as pl
from jax.experimental.pallas import tpu as pltpu
from jax.sharding import PartitionSpec as P

F32 = jnp.float32
BF16 = jnp.bfloat16
EPSILON = 1e-05
MASKED = -1e30
MESH = pl.DeviceIdType.MESH

UNIT = 80
QUARTER = 96
NEIGHBOURS = [(a, b) for a in (-1, 0, 1) for b in (-1, 0, 1) if (a, b) != (0, 0)] + [(0, 2), (0, -2)]


def one_hot(pairs, rows, columns):
    out = np.zeros((rows, columns), np.float32)
    for r, c in pairs:
        out[r, c] = 1.0
    return out


def in_quarter(row, col):
    return row * 6 + col if row < 9 else 64 + (row - 9) * 6 + col


@functools.cache
def row_orders():
    to_region = np.zeros((2, 4 * QUARTER, 288), np.float32)
    for odd in range(2):
        for half in range(2):
            for c in range(6):
                for a in range(12):
                    col = 24 * (6 * half + c)
                    upper = a + 3
                    lower = a + 15 if a < 9 else a - 9
                    kept, sent = (lower, upper) if odd else (upper, lower)
                    to_region[odd, half * QUARTER + in_quarter(a, c), col + kept] = 1.0
                    to_region[odd, (2 + half) * QUARTER + in_quarter(a, c), col + sent] = 1.0
    to_unit = one_hot(
        [
            (UNIT * (a // 6) + 12 * (a % 6) + o, (o // 6) * QUARTER + in_quarter(a, o % 6))
            for a in range(12)
            for o in range(12)
        ],
        2 * UNIT,
        2 * QUARTER,
    )
    merge = np.zeros((4 * 72, 4 * QUARTER), np.float32)
    for k, (dr, dc) in enumerate([(0, 0), (1, 0), (0, 1), (1, 1)]):
        for r in range(6):
            for c in range(12):
                quarter, col = divmod(2 * c + dc, 6)
                a = 2 * r + dr
                at = 64 + a * 6 + col if a < 3 else (a - 3) * 6 + col
                merge[k * 72 + r * 12 + c, quarter * QUARTER + at] = 1.0
    coarse = one_hot(
        [
            (l * 72 + r * 12 + c, (((c // 6) * 6 + r) * 6 + c % 6) * 2 + l)
            for l in range(2)
            for r in range(6)
            for c in range(12)
        ],
        144,
        144,
    )
    id_row = one_hot([(t, t // 12 + 18) for t in range(72)], UNIT, 24)
    id_col = one_hot([(t, t % 12) for t in range(72)], UNIT, 12)
    both = lambda m: [m, np.swapaxes(m, -1, -2)]
    orders = both(to_region) + both(to_unit) + both(merge) + both(coarse)
    return [np.ascontiguousarray(m).astype(jnp.bfloat16) for m in orders] + [id_row, id_col]


def dot(a, b):
    return lax.dot_general(a, b, (((1,), (0,)), ((), ())), preferred_element_type=F32)


def dot_nt(a, b):
    return lax.dot_general(a, b, (((1,), (1,)), ((), ())), preferred_element_type=F32)


def dot_tn(a, b):
    return lax.dot_general(a, b, (((0,), (0,)), ((), ())), preferred_element_type=F32)


def normed_rows(x):
    center = x - jnp.mean(x, axis=-1, keepdims=True)
    scale = lax.rsqrt(jnp.mean(center * center, axis=-1, keepdims=True) + EPSILON)
    return center * scale, scale


def norm_grad(grad, hat, scale):
    inner = jnp.mean(grad * hat, axis=-1, keepdims=True)
    return scale * (grad - jnp.mean(grad, axis=-1, keepdims=True) - hat * inner)


def one_row(x):
    span = x.shape[0] // 2
    low = lax.broadcasted_iota(jnp.int32, (span, 128), 1) < 64
    return jnp.where(low, x[:span], x[span:])


def rows_at(start, size, unit=16):
    return pl.ds(start if isinstance(start, int) else pl.multiple_of(start, unit), size)


def loop(count, body, together=1):
    def step(t, carry):
        for n in range(together):
            body(together * t + n)
        return carry

    lax.fori_loop(0, count // together, step, 0)


class Box:
    def __init__(self, **fields):
        self.__dict__.update(fields)


ARGS = dict(
    tokens=0, mask_ids=1, fine_bias=0, fine_qkv=0, fine_out=0, merge_weight=0, coarse_bias=0, coarse_qkv=0,
    coarse_out=0, cotangent=2, to_region=0, to_region_t=0, to_unit=0, to_unit_t=0,
    merge=0, merge_t=0, coarse=0, coarse_t=0, id_row=1, id_col=1,
)
LOADED = dict(
    tokens=0, to_region=1, fine_bias=0, to_unit=0, fine_qkv=0, fine_out=0, to_unit_t=0, coarse=0, coarse_bias=0,
    coarse_out=0, merge=0, merge_weight=0, coarse_qkv=0, coarse_t=0, merge_t=0, to_region_t=1,
)
SCRATCH = dict(
    heads2=((160, 128), BF16),
    heads2_c=((288, 128), BF16),
    send1=((2, 4, QUARTER, 512), BF16),
    region=((2, 4, QUARTER, 512), BF16),
    unit_x=((640, 512), BF16),
    unit_n=((640, 512), BF16),
    hat_f=((640, 512), F32),
    scale_f=((640, 128), F32),
    proj=((704, 1536), BF16),
    mask_left=((12, 2, 24), jnp.int32),
    bias_f=((3, 2, 4, 160, 128), F32),
    raised_f=((8, 4, 160, 128), BF16),
    recip_f=((640, 512), F32),
    heads_f=((640, 512), BF16),
    send2=((2, 4, QUARTER, 512), BF16),
    quarters=((2, 4, QUARTER, 512), BF16),
    hat_m=((144, 2048), F32),
    scale_m=((144, 128), F32),
    normed_m=((144, 2048), BF16),
    merged=((144, 1024), BF16),
    hat_c=((144, 1024), F32),
    scale_c=((144, 128), F32),
    normed_c=((144, 1024), BF16),
    proj_c=((256, 3072), BF16),
    bias_c=((16, 144, 256), F32),
    raised_c=((8, 288, 256), BF16),
    recip_c=((144, 1024), F32),
    heads_c=((144, 1024), BF16),
    result=((144, 1024), BF16),
    result2=((2, 6, 6, 2, 1024), BF16),
    cot2=((2, 6, 6, 2, 1024), BF16),
    cot=((144, 1024), BF16),
    dheads_c=((144, 1024), BF16),
    dprod_c=((144, 1024), BF16),
    dproj_c=((144, 3072), BF16),
    grad_c=((144, 1024), F32),
    dmerged=((144, 1024), BF16),
    grad_m=((144, 2048), F32),
    send3=((2, 4, QUARTER, 512), BF16),
    part=((2, 4, QUARTER, 512), BF16),
    dmixed=((640, 512), BF16),
    dheads_f=((640, 512), BF16),
    dprod_f=((640, 512), BF16),
    dproj_f=((640, 1536), BF16),
    send4=((2, 4, QUARTER, 512), BF16),
    region4=((2, 4, QUARTER, 512), BF16),
)
def kernel(n_lat, n_lon, *refs):
    rest = list(refs)
    hbm = Box(**{name: rest.pop(0) for name in ARGS})
    result_ref, grad_ref = rest.pop(0), rest.pop(0)
    vm = Box(**{name: rest.pop(0) for name in SCRATCH})
    ld = Box(**{name: rest.pop(0) for name in LOADED})
    load_sem, send_sem, recv_sem, near_sem = rest

    i, j = lax.axis_index("lat"), lax.axis_index("lon")
    odd = lax.rem(j, 2)
    even = odd == 0

    def device(di, dj):
        return (lax.rem(i + di + n_lat, n_lat), lax.rem(j + dj + n_lon, n_lon))

    def remote(src, dst, sem, l, target):
        return pltpu.make_async_remote_copy(
            src_ref=src,
            dst_ref=dst,
            send_sem=send_sem.at[sem, l],
            recv_sem=recv_sem.at[sem, l],
            device_id=target,
            device_id_type=MESH,
        )

    vm.mask_left[...] = jnp.zeros((12, 2, 24), jnp.int32)
    barrier = pltpu.get_barrier_semaphore()
    for di, dj in NEIGHBOURS:
        pl.semaphore_signal(barrier, inc=1, device_id=device(di, dj), device_id_type=MESH)

    loads = Box()
    for at, (name, paired) in enumerate(LOADED.items()):
        src = getattr(hbm, name)
        if paired:
            src = src.at[odd]
        copy = pltpu.make_async_copy(src, getattr(ld, name), load_sem.at[at])
        copy.start()
        setattr(loads, name, copy)
    own_cot = pltpu.make_async_copy(
        hbm.cotangent.at[pl.ds(6 * odd, 6)], vm.cot2.at[odd], near_sem.at[16, 0]
    )
    own_cot.start()

    for end in (320, 640):
        vm.proj[end : end + 64, :] = jnp.zeros((64, 1536), BF16)
    vm.proj_c[144:, :] = jnp.zeros((112, 3072), BF16)
    for ref in (vm.heads2, vm.heads2_c):
        low = lax.broadcasted_iota(jnp.int32, ref.shape, 1) < 64
        first = lax.broadcasted_iota(jnp.int32, ref.shape, 0) < ref.shape[0] // 2
        ref[...] = jnp.where(low == first, 1.0, 0.0).astype(BF16)

    def two_heads(x, mask):
        return jnp.concatenate([x, x], axis=0) * mask[...]

    loads.tokens.wait()
    loads.to_region.wait()
    pl.semaphore_wait(barrier, len(NEIGHBOURS))

    whole, top, low = (0, 96), (0, 64), (64, 32)
    left, right, far_left, far_right = (0, -1), (0, 1), (0, -2), (0, 2)
    plans = [
        (
            vm.send1,
            vm.region,
            [
                (2, 3, low, (-1, -1)), (3, 0, low, (-1, 1)), (2, 3, top, left), (3, 0, top, right),
                (0, 1, whole, None), (1, 2, whole, None),
            ],
            [
                (0, 1, low, (-1, 0)), (1, 2, low, (-1, 0)), (2, 3, whole, left), (3, 0, whole, right),
                (0, 1, top, None), (1, 2, top, None),
            ],
        ),
        (
            vm.send2,
            vm.quarters,
            [
                (0, 3, top, far_left), (0, 3, low, left), (1, 0, low, right), (2, 1, low, right),
                (3, 2, low, right), (1, 0, top, None), (2, 1, top, None), (3, 2, top, None),
            ],
            [
                (3, 0, top, far_right), (3, 0, low, (1, 1)), (0, 1, low, (1, -1)), (1, 2, low, (1, -1)),
                (2, 3, low, (1, -1)), (0, 1, top, None), (1, 2, top, None), (2, 3, top, None),
            ],
        ),
    ]
    for (_, _, of_even, of_odd), src, dst in ((plans[1], vm.send3, vm.part), (plans[0], vm.send4, vm.region4)):
        back_even, back_odd = [], []
        for mine, ours in ((of_even, 0), (of_odd, 1)):
            for at, into, rows, to in mine:
                if to is None:
                    target = ours
                    way = None
                else:
                    target = (ours + to[1]) % 2
                    way = (-to[0], -to[1])
                (back_odd if target else back_even).append((into, at, rows, way))
        plans.append((src, dst, back_even, back_odd))

    def transfer(phase, l, plan):
        at, into, (start, size), to = plan
        src, dst = plans[phase][:2]
        src, dst = src.at[l, at, pl.ds(start, size)], dst.at[l, into, pl.ds(start, size)]
        sem = phase * 8 + into * 2 + (start > 0)
        if to is None:
            return pltpu.make_async_copy(src, dst, near_sem.at[phase * 4 + into, l])
        return remote(src, dst, sem, l, device(*to))

    def by_parity(of_even, of_odd):
        @pl.when(even)
        def _():
            of_even()

        @pl.when(odd == 1)
        def _():
            of_odd()

    def send(phase, l, keep=None):
        def start(mine):
            for plan in mine:
                if keep is None or plan[0] in keep:
                    transfer(phase, l, plan).start()

        by_parity(lambda: start(plans[phase][2]), lambda: start(plans[phase][3]))

    def arrivals(phase, parity):
        got = []
        for ours in range(2):
            for plan in plans[phase][2 + ours]:
                to = plan[3]
                if (ours if to is None else (ours + to[1]) % 2) == parity:
                    got.append(plan)
        return got

    def take(phase, l, keep=None):
        def wait(parity):
            for plan in arrivals(phase, parity):
                if keep is None or plan[1] in keep:
                    copy = transfer(phase, l, plan)
                    copy.wait() if plan[3] is None else copy.wait_recv()

        by_parity(lambda: wait(0), lambda: wait(1))

    def sent(phase, l):
        def wait(mine):
            for plan in mine:
                if plan[3] is not None:
                    transfer(phase, l, plan).wait_send()

        by_parity(lambda: wait(plans[phase][2]), lambda: wait(plans[phase][3]))

    def at_strip(strip, of_strip):
        @pl.when(strip == 0)
        def _():
            of_strip((0, 1))

        @pl.when(strip == 1)
        def _():
            of_strip((2, 3))

    def regions(l):
        vm.send1[l] = dot(ld.to_region[...], ld.tokens[l]).astype(BF16).reshape(4, QUARTER, 512)
        send(0, l)

    for l in range(2):
        regions(l)
    partner_cot = remote(
        hbm.cotangent.at[pl.ds(6 - 6 * odd, 6)], vm.cot2.at[odd], 32, 0, device(0, 1 - 2 * odd)
    )
    partner_cot.start()
    left_mask = remote(hbm.mask_ids, vm.mask_left, 34, 0, device(0, 1))
    by_parity(left_mask.start, lambda: None)

    loads.fine_bias.wait()
    by_parity(lambda: None, left_mask.wait_recv)
    lanes = lax.broadcasted_iota(jnp.int32, (UNIT, 128), 1)
    subs = lax.broadcasted_iota(jnp.int32, (UNIT, 128), 0)
    past = jnp.where(lanes >= 72, MASKED, 0.0).astype(F32)
    for level in range(2):
        masks = [past]
        for ids in (vm.mask_left, hbm.mask_ids):
            spread = dot(hbm.id_col[...], ids[:, level, :].astype(F32))
            id_of = jnp.sum(spread * hbm.id_row[...], axis=-1, keepdims=True)
            id_at = dot(jnp.ones((8, UNIT), F32), jnp.where(lanes == subs, id_of, 0.0))[:1]
            masks.append(jnp.where(id_of == id_at, past, MASKED))
        for head in range(8):
            span = slice(72 * level, 72 * level + 72)
            block = ld.fine_bias[head, span, span]
            block = jnp.concatenate([block, jnp.zeros((72, 56), F32)], axis=1)
            block = jnp.concatenate([block, jnp.zeros((8, 128), F32)], axis=0)
            at = slice(UNIT * (head % 2), UNIT * (head % 2) + UNIT)
            for kind, mask in enumerate(masks):
                vm.bias_f[kind, level, head // 2, at, :] = block + mask

    loads.to_unit.wait()
    loads.fine_qkv.wait()
    loads.fine_out.wait()
    loads.to_unit_t.wait()

    def fine_forward(turn):
        strip = lax.rem(1 - odd + turn, 2)
        base = strip * 320
        level_at = lambda l: rows_at(base + l * 160, 160)
        both_levels = rows_at(base, 320)
        at_strip(strip, lambda keep: [take(0, l, keep) for l in range(2)])

        for l in range(2):
            source = vm.region[l, pl.ds(2 * strip, 2)].reshape(2 * QUARTER, 512)
            x = dot(ld.to_unit[...], source)
            hat, scale = normed_rows(x)
            vm.unit_x[level_at(l), :] = x.astype(BF16)
            vm.hat_f[level_at(l), :] = hat
            vm.scale_f[level_at(l), :] = jnp.broadcast_to(scale, (160, 128))
            vm.unit_n[level_at(l), :] = hat.astype(BF16)

        projected = dot(vm.unit_n[both_levels, :], ld.fine_qkv[...])
        vm.proj[both_levels, :512] = (projected[:, :512] * 0.125).astype(BF16)
        vm.proj[both_levels, 512:] = projected[:, 512:].astype(BF16)

        def fine_attend(n):
            l, m = lax.div(n, 2), lax.rem(n, 2)
            last = odd * m * (1 + strip)
            start = base + n * UNIT
            at, wide = rows_at(start, UNIT), rows_at(start, 128)
            pairs = [slice(128 * p, 128 * p + 128) for p in range(4)]
            ones = jnp.ones((128, 128), BF16)
            scores = [
                dot_nt(
                    two_heads(vm.proj[at, pair], vm.heads2), vm.proj[wide, 512 + pair.start : 512 + pair.stop]
                )
                + vm.bias_f[last, 1 - l, p]
                for p, pair in enumerate(pairs)
            ]
            tops = [jnp.max(s, axis=-1, keepdims=True) for s in scores]
            raised = [jnp.exp(s - t).astype(BF16) for s, t in zip(scores, tops)]
            sums = [
                dot(e, jnp.concatenate([vm.proj[wide, 1024 + pair.start : 1024 + pair.stop], ones], axis=1))
                for e, pair in zip(raised, pairs)
            ]
            for p, pair in enumerate(pairs):
                recip = 1.0 / one_row(sums[p][:, 128:])
                vm.raised_f[strip * 4 + n, p] = raised[p]
                vm.recip_f[at, pair] = recip
                vm.heads_f[at, pair] = (one_row(sums[p][:, :128]) * recip).astype(BF16)

        loop(4, fine_attend, 2)
        mixed = vm.unit_x[both_levels, :].astype(F32) + dot(vm.heads_f[both_levels, :], ld.fine_out[...])
        mixed = mixed.astype(BF16)
        for l in range(2):
            ordered = dot(ld.to_unit_t[...], mixed[160 * l : 160 * l + 160]).astype(BF16)
            vm.send2[l, pl.ds(2 * strip, 2)] = ordered.reshape(2, QUARTER, 512)
            at_strip(strip, lambda keep: send(1, l, keep))

    loop(2, fine_forward)
    loads.coarse_bias.wait()

    def coarse_pad(h):
        vm.bias_c[h] = jnp.concatenate([ld.coarse_bias[h], jnp.full((144, 112), MASKED, F32)], axis=1)

    loop(16, coarse_pad)
    own_cot.wait()
    partner_cot.wait()
    loads.coarse.wait()
    vm.cot[...] = dot(ld.coarse[...], vm.cot2[...].reshape(144, 1024)).astype(BF16)
    loads.coarse_out.wait()

    vm.grad_c[...] = dot_nt(vm.cot[...], ld.coarse_out[...])
    loads.merge.wait()
    loads.merge_weight.wait()
    loads.coarse_qkv.wait()
    loads.coarse_t.wait()

    for l in range(2):
        take(1, l)
    for l in range(2):
        gathered = dot(ld.merge[...], vm.quarters[l].reshape(4 * QUARTER, 512))
        for k in range(4):
            vm.hat_m[72 * l : 72 * l + 72, 512 * k : 512 * k + 512] = gathered[72 * k : 72 * k + 72]

    def merge_norm(t):
        at = rows_at(t * 48, 48)
        hat, scale = normed_rows(vm.hat_m[at, :])
        vm.hat_m[at, :] = hat
        vm.scale_m[at, :] = jnp.broadcast_to(scale, (48, 128))
        vm.normed_m[at, :] = hat.astype(BF16)

    for t in range(3):
        merge_norm(t)

    vm.merged[...] = dot(vm.normed_m[...], ld.merge_weight[...]).astype(BF16)

    def coarse_norm(t):
        at = rows_at(t * 48, 48)
        hat, scale = normed_rows(vm.merged[at, :].astype(F32))
        vm.hat_c[at, :] = hat
        vm.scale_c[at, :] = jnp.broadcast_to(scale, (48, 128))
        vm.normed_c[at, :] = hat.astype(BF16)

    for t in range(3):
        coarse_norm(t)

    projected = dot(vm.normed_c[...], ld.coarse_qkv[...])
    vm.proj_c[:144, :1024] = (projected[:, :1024] * 0.125).astype(BF16)
    vm.proj_c[:144, 1024:] = projected[:, 1024:].astype(BF16)

    def cols_at(p, base):
        return rows_at(p * 128 + base, 128, 128)

    def coarse_attend(t):
        pairs = [2 * t, 2 * t + 1]
        ones = jnp.ones((256, 128), BF16)
        scores = [
            dot_nt(two_heads(vm.proj_c[:144, cols_at(p, 0)], vm.heads2_c), vm.proj_c[:, cols_at(p, 1024)])
            + vm.bias_c[pl.ds(2 * p, 2)].reshape(288, 256)
            for p in pairs
        ]
        tops = [jnp.max(s, axis=-1, keepdims=True) for s in scores]
        raised = [jnp.exp(s - top).astype(BF16) for s, top in zip(scores, tops)]
        sums = [
            dot(e, jnp.concatenate([vm.proj_c[:, cols_at(p, 2048)], ones], axis=1))
            for e, p in zip(raised, pairs)
        ]
        for p, e, total in zip(pairs, raised, sums):
            recip = 1.0 / one_row(total[:, 128:])
            vm.raised_c[p] = e
            vm.recip_c[:, cols_at(p, 0)] = recip
            vm.heads_c[:, cols_at(p, 0)] = (one_row(total[:, :128]) * recip).astype(BF16)

    loop(4, coarse_attend, 2)

    mixed = dot(vm.heads_c[...], ld.coarse_out[...])
    vm.result[...] = (vm.merged[...].astype(F32) + mixed).astype(BF16)
    grad = vm.grad_c[...] * vm.recip_c[...]
    vm.dheads_c[...] = grad.astype(BF16)
    vm.dprod_c[...] = (grad * vm.heads_c[...].astype(F32)).astype(BF16)
    vm.result2[...] = dot(ld.coarse_t[...], vm.result[...]).astype(BF16).reshape(2, 6, 6, 2, 1024)
    into = result_ref.at[pl.ds(6 * odd, 6)]
    result_near = pltpu.make_async_copy(vm.result2.at[odd], into, near_sem.at[17, 0])
    result_far = remote(vm.result2.at[1 - odd], into, 33, 0, device(0, 1 - 2 * odd))
    result_near.start()
    result_far.start()

    def coarse_attend_grad(t):
        pairs = [2 * t, 2 * t + 1]
        minus = jnp.full((256, 128), -1.0, BF16)
        grads = [two_heads(vm.dheads_c[:, cols_at(p, 0)], vm.heads2_c) for p in pairs]
        prods = [two_heads(vm.dprod_c[:, cols_at(p, 0)], vm.heads2_c) for p in pairs]
        queries = [two_heads(vm.proj_c[:144, cols_at(p, 0)], vm.heads2_c) for p in pairs]
        inner = [
            dot_nt(
                jnp.concatenate([g, d], axis=1), jnp.concatenate([vm.proj_c[:, cols_at(p, 2048)], minus], axis=1)
            )
            for p, g, d in zip(pairs, grads, prods)
        ]
        dscores = [(vm.raised_c[p].astype(F32) * x).astype(BF16) for p, x in zip(pairs, inner)]
        for p, g, q, ds in zip(pairs, grads, queries, dscores):
            vm.dproj_c[:, cols_at(p, 2048)] = dot_tn(vm.raised_c[p], g)[:144].astype(BF16)
            dq = one_row(dot(ds, vm.proj_c[:, cols_at(p, 1024)]))
            vm.dproj_c[:, cols_at(p, 0)] = (dq * 0.125).astype(BF16)
            vm.dproj_c[:, cols_at(p, 1024)] = dot_tn(ds, q)[:144].astype(BF16)

    loop(4, coarse_attend_grad, 2)

    vm.grad_c[...] = dot_nt(vm.dproj_c[...], ld.coarse_qkv[...])

    def coarse_norm_grad(t):
        at = rows_at(t * 48, 48)
        grad = norm_grad(vm.grad_c[at, :], vm.hat_c[at, :], vm.scale_c[at, :1])
        vm.dmerged[at, :] = (vm.cot[at, :].astype(F32) + grad).astype(BF16)

    for t in range(3):
        coarse_norm_grad(t)

    vm.grad_m[...] = dot_nt(vm.dmerged[...], ld.merge_weight[...])
    loads.merge_t.wait()

    for l in range(2):
        at = slice(72 * l, 72 * l + 72)
        grad = norm_grad(vm.grad_m[at, :], vm.hat_m[at, :], vm.scale_m[at, :1])
        grad = jnp.concatenate([grad[:, 512 * k : 512 * k + 512] for k in range(4)], axis=0)
        vm.send3[l] = dot(ld.merge_t[...], grad.astype(BF16)).astype(BF16).reshape(4, QUARTER, 512)
        send(2, l)
    loads.to_region_t.wait()

    def fine_backward(turn):
        strip = lax.rem(1 - odd + turn, 2)
        base = strip * 320
        level_at = lambda l: rows_at(base + l * 160, 160)
        both_levels = rows_at(base, 320)
        at_strip(strip, lambda keep: [take(2, l, keep) for l in range(2)])

        for l in range(2):
            source = vm.part[l, pl.ds(2 * strip, 2)].reshape(2 * QUARTER, 512)
            vm.dmixed[level_at(l), :] = dot(ld.to_unit[...], source).astype(BF16)

        grad = dot_nt(vm.dmixed[both_levels, :], ld.fine_out[...]) * vm.recip_f[both_levels, :]
        vm.dheads_f[both_levels, :] = grad.astype(BF16)
        vm.dprod_f[both_levels, :] = (grad * vm.heads_f[both_levels, :].astype(F32)).astype(BF16)

        def fine_attend_grad(n):
            start = base + n * UNIT
            at, wide = rows_at(start, UNIT), rows_at(start, 128)
            pairs = [slice(128 * p, 128 * p + 128) for p in range(4)]
            minus = jnp.full((128, 128), -1.0, BF16)
            grads = [two_heads(vm.dheads_f[at, pair], vm.heads2) for pair in pairs]
            prods = [two_heads(vm.dprod_f[at, pair], vm.heads2) for pair in pairs]
            queries = [two_heads(vm.proj[at, pair], vm.heads2) for pair in pairs]
            inner = [
                dot_nt(
                    jnp.concatenate([g, d], axis=1),
                    jnp.concatenate([vm.proj[wide, 1024 + pair.start : 1024 + pair.stop], minus], axis=1),
                )
                for pair, g, d in zip(pairs, grads, prods)
            ]
            raised = [vm.raised_f[strip * 4 + n, p] for p in range(4)]
            dscores = [(e.astype(F32) * x).astype(BF16) for e, x in zip(raised, inner)]
            dvalues = [dot_tn(e, g) for e, g in zip(raised, grads)]
            dkeys = [dot_tn(ds, q) for ds, q in zip(dscores, queries)]
            dqueries = [
                dot(ds, vm.proj[wide, 512 + pair.start : 512 + pair.stop]) for pair, ds in zip(pairs, dscores)
            ]
            for p, pair in enumerate(pairs):
                vm.dproj_f[at, pair] = (one_row(dqueries[p]) * 0.125).astype(BF16)
                vm.dproj_f[at, 512 + pair.start : 512 + pair.stop] = dkeys[p][:UNIT].astype(BF16)
                vm.dproj_f[at, 1024 + pair.start : 1024 + pair.stop] = dvalues[p][:UNIT].astype(BF16)

        loop(4, fine_attend_grad, 2)
        grad = dot_nt(vm.dproj_f[both_levels, :], ld.fine_qkv[...])
        grad = norm_grad(grad, vm.hat_f[both_levels, :], vm.scale_f[both_levels, :1])
        dunit = (vm.dmixed[both_levels, :].astype(F32) + grad).astype(BF16)
        for l in range(2):
            ordered = dot(ld.to_unit_t[...], dunit[160 * l : 160 * l + 160]).astype(BF16)
            vm.send4[l, pl.ds(2 * strip, 2)] = ordered.reshape(2, QUARTER, 512)
            at_strip(strip, lambda keep: send(3, l, keep))

    loop(2, fine_backward)
    by_parity(left_mask.wait_send, lambda: None)
    result_near.wait()
    result_far.wait()

    def grid_back(l):
        take(3, l)
        grad_ref[l] = dot(ld.to_region_t[...], vm.region4[l].reshape(4 * QUARTER, 512)).astype(BF16)
        for phase in range(4):
            sent(phase, l)

    loop(2, grid_back)


PIECES = 2


def hand_over(*refs):
    ins, outs = [], []
    for n in range(2):
        src, dst, held = refs[n], refs[2 + n], refs[4 + n]
        size = src.shape[0] // PIECES
        for piece in range(PIECES):
            at = pl.ds(piece * size, size)
            ins.append(pltpu.make_async_copy(src.at[at], held.at[at], refs[6].at[n, piece]))
            outs.append(pltpu.make_async_copy(held.at[at], dst.at[at], refs[7].at[n, piece]))
    for copy in ins:
        copy.start()
    for before, after in zip(ins, outs):
        before.wait()
        after.start()
    for copy in outs:
        copy.wait()


def per_device(n_lat, n_lon, *args):
    tokens, mask_ids, *middle, cotangent = args
    tokens = tokens.transpose(0, 2, 1, 3).reshape(2, 288, 512)
    operands = [tokens, mask_ids.transpose(2, 0, 1), *middle, cotangent.transpose(1, 2, 0, 3)]
    operands += [jnp.asarray(m) for m in row_orders()]
    shapes = dict(zip(ARGS, [(x.shape, x.dtype) for x in operands]))
    loaded = [
        pltpu.VMEM(shapes[name][0][1:] if paired else shapes[name][0], shapes[name][1])
        for name, paired in LOADED.items()
    ]
    result, grad = pl.pallas_call(
        functools.partial(kernel, n_lat, n_lon),
        out_shape=(
            jax.ShapeDtypeStruct((12, 6, 2, 1024), BF16),
            jax.ShapeDtypeStruct((2, 288, 512), BF16),
        ),
        in_specs=[
            pl.BlockSpec(memory_space=pltpu.VMEM if placed == 1 else pl.ANY) for placed in ARGS.values()
        ],
        out_specs=(pl.BlockSpec(memory_space=pltpu.VMEM), pl.BlockSpec(memory_space=pltpu.VMEM)),
        scratch_shapes=[pltpu.VMEM(*spec) for spec in SCRATCH.values()]
        + loaded
        + [
            pltpu.SemaphoreType.DMA((len(LOADED),)),
            pltpu.SemaphoreType.DMA((35, 2)),
            pltpu.SemaphoreType.DMA((35, 2)),
            pltpu.SemaphoreType.DMA((18, 2)),
        ],
        compiler_params=pltpu.CompilerParams(
            collective_id=0, has_side_effects=True, vmem_limit_bytes=60 * 2**20
        ),
    )(*operands)
    anywhere = pl.BlockSpec(memory_space=pl.ANY)
    result, grad = pl.pallas_call(
        hand_over,
        out_shape=(
            jax.ShapeDtypeStruct((12, 6, 2, 1024), BF16),
            jax.ShapeDtypeStruct((8, 72, 512), BF16),
        ),
        in_specs=[anywhere, anywhere],
        out_specs=(anywhere, anywhere),
        scratch_shapes=[
            pltpu.VMEM((12, 6, 2, 1024), BF16),
            pltpu.VMEM((8, 72, 512), BF16),
            pltpu.SemaphoreType.DMA((2, PIECES)),
            pltpu.SemaphoreType.DMA((2, PIECES)),
        ],
        compiler_params=pltpu.CompilerParams(vmem_limit_bytes=60 * 2**20),
    )(result, grad.reshape(8, 72, 512))
    return result.transpose(2, 0, 1, 3), grad.reshape(2, 12, 24, 512).transpose(0, 2, 1, 3)


def solution(mesh):
    grid = P(None, "lat", "lon", None)
    placed = (grid, P(None, "lat", "lon"), P(), P(), P(), P(), P(), P(), P(), grid)
    return jax.shard_map(
        functools.partial(per_device, mesh.shape["lat"], mesh.shape["lon"]),
        mesh=mesh,
        in_specs=placed,
        out_specs=(grid, grid),
        check_vma=False,
    )
```

```python
import functools

import jax
import jax.numpy as jnp
import numpy as np
from jax import lax
from jax.experimental import pallas as pl
from jax.experimental.pallas import tpu as pltpu
from jax.sharding import PartitionSpec as P

F32 = jnp.float32
BF16 = jnp.bfloat16
EPSILON = 1e-05
MASKED = -1e30
MESH = pl.DeviceIdType.MESH

UNIT = 80
QUARTER = 96
NEIGHBOURS = [(a, b) for a in (-1, 0, 1) for b in (-1, 0, 1) if (a, b) != (0, 0)] + [(0, 2), (0, -2)]


def one_hot(pairs, rows, columns):
    out = np.zeros((rows, columns), np.float32)
    for r, c in pairs:
        out[r, c] = 1.0
    return out


def in_quarter(row, col):
    return row * 6 + col if row < 9 else 64 + (row - 9) * 6 + col


@functools.cache
def row_orders():
    to_region = np.zeros((2, 4 * QUARTER, 288), np.float32)
    for odd in range(2):
        for half in range(2):
            for c in range(6):
                for a in range(12):
                    col = 24 * (6 * half + c)
                    upper = a + 3
                    lower = a + 15 if a < 9 else a - 9
                    kept, sent = (lower, upper) if odd else (upper, lower)
                    to_region[odd, half * QUARTER + in_quarter(a, c), col + kept] = 1.0
                    to_region[odd, (2 + half) * QUARTER + in_quarter(a, c), col + sent] = 1.0
    to_unit = one_hot(
        [
            (UNIT * (a // 6) + 12 * (a % 6) + o, (o // 6) * QUARTER + in_quarter(a, o % 6))
            for a in range(12)
            for o in range(12)
        ],
        2 * UNIT,
        2 * QUARTER,
    )
    merge = np.zeros((4 * 72, 4 * QUARTER), np.float32)
    for k, (dr, dc) in enumerate([(0, 0), (1, 0), (0, 1), (1, 1)]):
        for r in range(6):
            for c in range(12):
                quarter, col = divmod(2 * c + dc, 6)
                a = 2 * r + dr
                at = 64 + a * 6 + col if a < 3 else (a - 3) * 6 + col
                merge[k * 72 + r * 12 + c, quarter * QUARTER + at] = 1.0
    coarse = one_hot(
        [
            (l * 72 + r * 12 + c, (((c // 6) * 6 + r) * 6 + c % 6) * 2 + l)
            for l in range(2)
            for r in range(6)
            for c in range(12)
        ],
        144,
        144,
    )
    id_row = one_hot([(t, t // 12 + 18) for t in range(72)], UNIT, 24)
    id_col = one_hot([(t, t % 12) for t in range(72)], UNIT, 12)
    both = lambda m: [m, np.swapaxes(m, -1, -2)]
    orders = both(to_region) + both(to_unit) + both(merge) + both(coarse)
    return [np.ascontiguousarray(m).astype(jnp.bfloat16) for m in orders] + [id_row, id_col]


def dot(a, b):
    return lax.dot_general(a, b, (((1,), (0,)), ((), ())), preferred_element_type=F32)


def dot_nt(a, b):
    return lax.dot_general(a, b, (((1,), (1,)), ((), ())), preferred_element_type=F32)


def dot_tn(a, b):
    return lax.dot_general(a, b, (((0,), (0,)), ((), ())), preferred_element_type=F32)


def normed_rows(x):
    center = x - jnp.mean(x, axis=-1, keepdims=True)
    scale = lax.rsqrt(jnp.mean(center * center, axis=-1, keepdims=True) + EPSILON)
    return center * scale, scale


def norm_grad(grad, hat, scale):
    inner = jnp.mean(grad * hat, axis=-1, keepdims=True)
    return scale * (grad - jnp.mean(grad, axis=-1, keepdims=True) - hat * inner)


def one_row(x):
    span = x.shape[0] // 2
    low = lax.broadcasted_iota(jnp.int32, (span, 128), 1) < 64
    return jnp.where(low, x[:span], x[span:])


def rows_at(start, size, unit=16):
    return pl.ds(start if isinstance(start, int) else pl.multiple_of(start, unit), size)


def loop(count, body, together=1):
    def step(t, carry):
        for n in range(together):
            body(together * t + n)
        return carry

    lax.fori_loop(0, count // together, step, 0)


class Box:
    def __init__(self, **fields):
        self.__dict__.update(fields)


ARGS = dict(
    tokens=0, mask_ids=1, fine_bias=0, fine_qkv=0, fine_out=0, merge_weight=0, coarse_bias=0, coarse_qkv=0,
    coarse_out=0, cotangent=2, to_region=0, to_region_t=0, to_unit=0, to_unit_t=0,
    merge=0, merge_t=0, coarse=0, coarse_t=0, id_row=1, id_col=1,
)
LOADED = dict(
    tokens=0, to_region=1, fine_bias=0, to_unit=0, fine_qkv=0, fine_out=0, to_unit_t=0, coarse=0, coarse_bias=0,
    coarse_out=0, merge=0, merge_weight=0, coarse_qkv=0, coarse_t=0, merge_t=0, to_region_t=1,
)
SCRATCH = dict(
    heads2=((160, 128), BF16),
    heads2_c=((288, 128), BF16),
    send1=((2, 4, QUARTER, 512), BF16),
    region=((2, 4, QUARTER, 512), BF16),
    unit_x=((640, 512), BF16),
    unit_n=((640, 512), BF16),
    hat_f=((640, 512), F32),
    scale_f=((640, 128), F32),
    proj=((704, 1536), BF16),
    mask_left=((12, 2, 24), jnp.int32),
    bias_f=((3, 2, 4, 160, 128), F32),
    raised_f=((8, 4, 160, 128), BF16),
    recip_f=((640, 512), F32),
    heads_f=((640, 512), BF16),
    send2=((2, 4, QUARTER, 512), BF16),
    quarters=((2, 4, QUARTER, 512), BF16),
    hat_m=((144, 2048), F32),
    scale_m=((144, 128), F32),
    normed_m=((144, 2048), BF16),
    merged=((144, 1024), BF16),
    hat_c=((144, 1024), F32),
    scale_c=((144, 128), F32),
    normed_c=((144, 1024), BF16),
    proj_c=((256, 3072), BF16),
    bias_c=((16, 144, 256), F32),
    raised_c=((8, 288, 256), BF16),
    recip_c=((144, 1024), F32),
    heads_c=((144, 1024), BF16),
    result=((144, 1024), BF16),
    result2=((2, 6, 6, 2, 1024), BF16),
    cot2=((2, 6, 6, 2, 1024), BF16),
    cot=((144, 1024), BF16),
    dheads_c=((144, 1024), BF16),
    dprod_c=((144, 1024), BF16),
    dproj_c=((144, 3072), BF16),
    grad_c=((144, 1024), F32),
    dmerged=((144, 1024), BF16),
    grad_m=((144, 2048), F32),
    send3=((2, 4, QUARTER, 512), BF16),
    part=((2, 4, QUARTER, 512), BF16),
    dmixed=((640, 512), BF16),
    dheads_f=((640, 512), BF16),
    dprod_f=((640, 512), BF16),
    dproj_f=((640, 1536), BF16),
    send4=((2, 4, QUARTER, 512), BF16),
    region4=((2, 4, QUARTER, 512), BF16),
)
def kernel(n_lat, n_lon, *refs):
    rest = list(refs)
    hbm = Box(**{name: rest.pop(0) for name in ARGS})
    result_ref, grad_ref = rest.pop(0), rest.pop(0)
    vm = Box(**{name: rest.pop(0) for name in SCRATCH})
    ld = Box(**{name: rest.pop(0) for name in LOADED})
    load_sem, send_sem, recv_sem, near_sem = rest

    i, j = lax.axis_index("lat"), lax.axis_index("lon")
    odd = lax.rem(j, 2)
    even = odd == 0

    def device(di, dj):
        return (lax.rem(i + di + n_lat, n_lat), lax.rem(j + dj + n_lon, n_lon))

    def remote(src, dst, sem, l, target):
        return pltpu.make_async_remote_copy(
            src_ref=src,
            dst_ref=dst,
            send_sem=send_sem.at[sem, l],
            recv_sem=recv_sem.at[sem, l],
            device_id=target,
            device_id_type=MESH,
        )

    vm.mask_left[...] = jnp.zeros((12, 2, 24), jnp.int32)
    barrier = pltpu.get_barrier_semaphore()
    for di, dj in NEIGHBOURS:
        pl.semaphore_signal(barrier, inc=1, device_id=device(di, dj), device_id_type=MESH)

    loads = Box()
    for at, (name, paired) in enumerate(LOADED.items()):
        src = getattr(hbm, name)
        if paired:
            src = src.at[odd]
        copy = pltpu.make_async_copy(src, getattr(ld, name), load_sem.at[at])
        copy.start()
        setattr(loads, name, copy)
    own_cot = pltpu.make_async_copy(
        hbm.cotangent.at[pl.ds(6 * odd, 6)], vm.cot2.at[odd], near_sem.at[16, 0]
    )
    own_cot.start()

    for end in (320, 640):
        vm.proj[end : end + 64, :] = jnp.zeros((64, 1536), BF16)
    vm.proj_c[144:, :] = jnp.zeros((112, 3072), BF16)
    for ref in (vm.heads2, vm.heads2_c):
        low = lax.broadcasted_iota(jnp.int32, ref.shape, 1) < 64
        first = lax.broadcasted_iota(jnp.int32, ref.shape, 0) < ref.shape[0] // 2
        ref[...] = jnp.where(low == first, 1.0, 0.0).astype(BF16)

    def two_heads(x, mask):
        return jnp.concatenate([x, x], axis=0) * mask[...]

    loads.tokens.wait()
    loads.to_region.wait()
    pl.semaphore_wait(barrier, len(NEIGHBOURS))

    whole, top, low = (0, 96), (0, 64), (64, 32)
    left, right, far_left, far_right = (0, -1), (0, 1), (0, -2), (0, 2)
    plans = [
        (
            vm.send1,
            vm.region,
            [
                (2, 3, low, (-1, -1)), (3, 0, low, (-1, 1)), (2, 3, top, left), (3, 0, top, right),
                (0, 1, whole, None), (1, 2, whole, None),
            ],
            [
                (0, 1, low, (-1, 0)), (1, 2, low, (-1, 0)), (2, 3, whole, left), (3, 0, whole, right),
                (0, 1, top, None), (1, 2, top, None),
            ],
        ),
        (
            vm.send2,
            vm.quarters,
            [
                (0, 3, top, far_left), (0, 3, low, left), (1, 0, low, right), (2, 1, low, right),
                (3, 2, low, right), (1, 0, top, None), (2, 1, top, None), (3, 2, top, None),
            ],
            [
                (3, 0, top, far_right), (3, 0, low, (1, 1)), (0, 1, low, (1, -1)), (1, 2, low, (1, -1)),
                (2, 3, low, (1, -1)), (0, 1, top, None), (1, 2, top, None), (2, 3, top, None),
            ],
        ),
    ]
    for (_, _, of_even, of_odd), src, dst in ((plans[1], vm.send3, vm.part), (plans[0], vm.send4, vm.region4)):
        back_even, back_odd = [], []
        for mine, ours in ((of_even, 0), (of_odd, 1)):
            for at, into, rows, to in mine:
                if to is None:
                    target = ours
                    way = None
                else:
                    target = (ours + to[1]) % 2
                    way = (-to[0], -to[1])
                (back_odd if target else back_even).append((into, at, rows, way))
        plans.append((src, dst, back_even, back_odd))

    def transfer(phase, l, plan):
        at, into, (start, size), to = plan
        src, dst = plans[phase][:2]
        src, dst = src.at[l, at, pl.ds(start, size)], dst.at[l, into, pl.ds(start, size)]
        sem = phase * 8 + into * 2 + (start > 0)
        if to is None:
            return pltpu.make_async_copy(src, dst, near_sem.at[phase * 4 + into, l])
        return remote(src, dst, sem, l, device(*to))

    def by_parity(of_even, of_odd):
        @pl.when(even)
        def _():
            of_even()

        @pl.when(odd == 1)
        def _():
            of_odd()

    def send(phase, l, keep=None):
        def start(mine):
            for plan in mine:
                if keep is None or plan[0] in keep:
                    transfer(phase, l, plan).start()

        by_parity(lambda: start(plans[phase][2]), lambda: start(plans[phase][3]))

    def arrivals(phase, parity):
        got = []
        for ours in range(2):
            for plan in plans[phase][2 + ours]:
                to = plan[3]
                if (ours if to is None else (ours + to[1]) % 2) == parity:
                    got.append(plan)
        return got

    def take(phase, l, keep=None):
        def wait(parity):
            for plan in arrivals(phase, parity):
                if keep is None or plan[1] in keep:
                    copy = transfer(phase, l, plan)
                    copy.wait() if plan[3] is None else copy.wait_recv()

        by_parity(lambda: wait(0), lambda: wait(1))

    def sent(phase, l):
        def wait(mine):
            for plan in mine:
                if plan[3] is not None:
                    transfer(phase, l, plan).wait_send()

        by_parity(lambda: wait(plans[phase][2]), lambda: wait(plans[phase][3]))

    def at_strip(strip, of_strip):
        @pl.when(strip == 0)
        def _():
            of_strip((0, 1))

        @pl.when(strip == 1)
        def _():
            of_strip((2, 3))

    def regions(l):
        vm.send1[l] = dot(ld.to_region[...], ld.tokens[l]).astype(BF16).reshape(4, QUARTER, 512)
        send(0, l)

    for l in range(2):
        regions(l)
    partner_cot = remote(
        hbm.cotangent.at[pl.ds(6 - 6 * odd, 6)], vm.cot2.at[odd], 32, 0, device(0, 1 - 2 * odd)
    )
    partner_cot.start()
    left_mask = remote(hbm.mask_ids, vm.mask_left, 34, 0, device(0, 1))
    by_parity(left_mask.start, lambda: None)

    loads.fine_bias.wait()
    by_parity(lambda: None, left_mask.wait_recv)
    lanes = lax.broadcasted_iota(jnp.int32, (UNIT, 128), 1)
    subs = lax.broadcasted_iota(jnp.int32, (UNIT, 128), 0)
    past = jnp.where(lanes >= 72, MASKED, 0.0).astype(F32)
    for level in range(2):
        masks = [past]
        for ids in (vm.mask_left, hbm.mask_ids):
            spread = dot(hbm.id_col[...], ids[:, level, :].astype(F32))
            id_of = jnp.sum(spread * hbm.id_row[...], axis=-1, keepdims=True)
            id_at = dot(jnp.ones((8, UNIT), F32), jnp.where(lanes == subs, id_of, 0.0))[:1]
            masks.append(jnp.where(id_of == id_at, past, MASKED))
        for head in range(8):
            span = slice(72 * level, 72 * level + 72)
            block = ld.fine_bias[head, span, span]
            block = jnp.concatenate([block, jnp.zeros((72, 56), F32)], axis=1)
            block = jnp.concatenate([block, jnp.zeros((8, 128), F32)], axis=0)
            at = slice(UNIT * (head % 2), UNIT * (head % 2) + UNIT)
            for kind, mask in enumerate(masks):
                vm.bias_f[kind, level, head // 2, at, :] = block + mask

    loads.to_unit.wait()
    loads.fine_qkv.wait()
    loads.fine_out.wait()
    loads.to_unit_t.wait()

    def fine_forward(turn):
        strip = lax.rem(1 - odd + turn, 2)
        base = strip * 320
        level_at = lambda l: rows_at(base + l * 160, 160)
        both_levels = rows_at(base, 320)
        at_strip(strip, lambda keep: [take(0, l, keep) for l in range(2)])

        for l in range(2):
            source = vm.region[l, pl.ds(2 * strip, 2)].reshape(2 * QUARTER, 512)
            x = dot(ld.to_unit[...], source)
            hat, scale = normed_rows(x)
            vm.unit_x[level_at(l), :] = x.astype(BF16)
            vm.hat_f[level_at(l), :] = hat
            vm.scale_f[level_at(l), :] = jnp.broadcast_to(scale, (160, 128))
            vm.unit_n[level_at(l), :] = hat.astype(BF16)

        projected = dot(vm.unit_n[both_levels, :], ld.fine_qkv[...])
        vm.proj[both_levels, :512] = (projected[:, :512] * 0.125).astype(BF16)
        vm.proj[both_levels, 512:] = projected[:, 512:].astype(BF16)

        def fine_attend(n):
            l, m = lax.div(n, 2), lax.rem(n, 2)
            last = odd * m * (1 + strip)
            start = base + n * UNIT
            at, wide = rows_at(start, UNIT), rows_at(start, 128)
            pairs = [slice(128 * p, 128 * p + 128) for p in range(4)]
            ones = jnp.ones((128, 128), BF16)
            scores = [
                dot_nt(
                    two_heads(vm.proj[at, pair], vm.heads2), vm.proj[wide, 512 + pair.start : 512 + pair.stop]
                )
                + vm.bias_f[last, 1 - l, p]
                for p, pair in enumerate(pairs)
            ]
            tops = [jnp.max(s, axis=-1, keepdims=True) for s in scores]
            raised = [jnp.exp(s - t).astype(BF16) for s, t in zip(scores, tops)]
            sums = [
                dot(e, jnp.concatenate([vm.proj[wide, 1024 + pair.start : 1024 + pair.stop], ones], axis=1))
                for e, pair in zip(raised, pairs)
            ]
            for p, pair in enumerate(pairs):
                recip = 1.0 / one_row(sums[p][:, 128:])
                vm.raised_f[strip * 4 + n, p] = raised[p]
                vm.recip_f[at, pair] = recip
                vm.heads_f[at, pair] = (one_row(sums[p][:, :128]) * recip).astype(BF16)

        def fine_level(l):
            for m in range(2):
                fine_attend(2 * l + m)
            mixed = vm.unit_x[level_at(l), :].astype(F32) + dot(vm.heads_f[level_at(l), :], ld.fine_out[...])
            ordered = dot(ld.to_unit_t[...], mixed.astype(BF16)).astype(BF16)
            vm.send2[l, pl.ds(2 * strip, 2)] = ordered.reshape(2, QUARTER, 512)
            at_strip(strip, lambda keep: send(1, l, keep))

        loop(2, fine_level)

    loop(2, fine_forward)
    loads.coarse_bias.wait()

    def coarse_pad(h):
        vm.bias_c[h] = jnp.concatenate([ld.coarse_bias[h], jnp.full((144, 112), MASKED, F32)], axis=1)

    loop(16, coarse_pad)
    own_cot.wait()
    partner_cot.wait()
    loads.coarse.wait()
    vm.cot[...] = dot(ld.coarse[...], vm.cot2[...].reshape(144, 1024)).astype(BF16)
    loads.coarse_out.wait()

    vm.grad_c[...] = dot_nt(vm.cot[...], ld.coarse_out[...])
    loads.merge.wait()
    loads.merge_weight.wait()
    loads.coarse_qkv.wait()
    loads.coarse_t.wait()

    for l in range(2):
        take(1, l)
    for l in range(2):
        gathered = dot(ld.merge[...], vm.quarters[l].reshape(4 * QUARTER, 512))
        for k in range(4):
            vm.hat_m[72 * l : 72 * l + 72, 512 * k : 512 * k + 512] = gathered[72 * k : 72 * k + 72]

    def merge_norm(t):
        at = rows_at(t * 48, 48)
        hat, scale = normed_rows(vm.hat_m[at, :])
        vm.hat_m[at, :] = hat
        vm.scale_m[at, :] = jnp.broadcast_to(scale, (48, 128))
        vm.normed_m[at, :] = hat.astype(BF16)

    for t in range(3):
        merge_norm(t)

    vm.merged[...] = dot(vm.normed_m[...], ld.merge_weight[...]).astype(BF16)

    def coarse_norm(t):
        at = rows_at(t * 48, 48)
        hat, scale = normed_rows(vm.merged[at, :].astype(F32))
        vm.hat_c[at, :] = hat
        vm.scale_c[at, :] = jnp.broadcast_to(scale, (48, 128))
        vm.normed_c[at, :] = hat.astype(BF16)

    for t in range(3):
        coarse_norm(t)

    projected = dot(vm.normed_c[...], ld.coarse_qkv[...])
    vm.proj_c[:144, :1024] = (projected[:, :1024] * 0.125).astype(BF16)
    vm.proj_c[:144, 1024:] = projected[:, 1024:].astype(BF16)

    def cols_at(p, base):
        return rows_at(p * 128 + base, 128, 128)

    def coarse_attend(t):
        pairs = [2 * t, 2 * t + 1]
        ones = jnp.ones((256, 128), BF16)
        scores = [
            dot_nt(two_heads(vm.proj_c[:144, cols_at(p, 0)], vm.heads2_c), vm.proj_c[:, cols_at(p, 1024)])
            + vm.bias_c[pl.ds(2 * p, 2)].reshape(288, 256)
            for p in pairs
        ]
        tops = [jnp.max(s, axis=-1, keepdims=True) for s in scores]
        raised = [jnp.exp(s - top).astype(BF16) for s, top in zip(scores, tops)]
        sums = [
            dot(e, jnp.concatenate([vm.proj_c[:, cols_at(p, 2048)], ones], axis=1))
            for e, p in zip(raised, pairs)
        ]
        for p, e, total in zip(pairs, raised, sums):
            recip = 1.0 / one_row(total[:, 128:])
            vm.raised_c[p] = e
            vm.recip_c[:, cols_at(p, 0)] = recip
            vm.heads_c[:, cols_at(p, 0)] = (one_row(total[:, :128]) * recip).astype(BF16)

    loop(4, coarse_attend, 2)

    mixed = dot(vm.heads_c[...], ld.coarse_out[...])
    vm.result[...] = (vm.merged[...].astype(F32) + mixed).astype(BF16)
    grad = vm.grad_c[...] * vm.recip_c[...]
    vm.dheads_c[...] = grad.astype(BF16)
    vm.dprod_c[...] = (grad * vm.heads_c[...].astype(F32)).astype(BF16)
    vm.result2[...] = dot(ld.coarse_t[...], vm.result[...]).astype(BF16).reshape(2, 6, 6, 2, 1024)
    into = result_ref.at[pl.ds(6 * odd, 6)]
    result_near = pltpu.make_async_copy(vm.result2.at[odd], into, near_sem.at[17, 0])
    result_far = remote(vm.result2.at[1 - odd], into, 33, 0, device(0, 1 - 2 * odd))
    result_near.start()
    result_far.start()

    def coarse_attend_grad(t):
        pairs = [2 * t, 2 * t + 1]
        minus = jnp.full((256, 128), -1.0, BF16)
        grads = [two_heads(vm.dheads_c[:, cols_at(p, 0)], vm.heads2_c) for p in pairs]
        prods = [two_heads(vm.dprod_c[:, cols_at(p, 0)], vm.heads2_c) for p in pairs]
        queries = [two_heads(vm.proj_c[:144, cols_at(p, 0)], vm.heads2_c) for p in pairs]
        inner = [
            dot_nt(
                jnp.concatenate([g, d], axis=1), jnp.concatenate([vm.proj_c[:, cols_at(p, 2048)], minus], axis=1)
            )
            for p, g, d in zip(pairs, grads, prods)
        ]
        dscores = [(vm.raised_c[p].astype(F32) * x).astype(BF16) for p, x in zip(pairs, inner)]
        for p, g, q, ds in zip(pairs, grads, queries, dscores):
            vm.dproj_c[:, cols_at(p, 2048)] = dot_tn(vm.raised_c[p], g)[:144].astype(BF16)
            dq = one_row(dot(ds, vm.proj_c[:, cols_at(p, 1024)]))
            vm.dproj_c[:, cols_at(p, 0)] = (dq * 0.125).astype(BF16)
            vm.dproj_c[:, cols_at(p, 1024)] = dot_tn(ds, q)[:144].astype(BF16)

    loop(4, coarse_attend_grad, 2)

    vm.grad_c[...] = dot_nt(vm.dproj_c[...], ld.coarse_qkv[...])

    def coarse_norm_grad(t):
        at = rows_at(t * 48, 48)
        grad = norm_grad(vm.grad_c[at, :], vm.hat_c[at, :], vm.scale_c[at, :1])
        vm.dmerged[at, :] = (vm.cot[at, :].astype(F32) + grad).astype(BF16)

    for t in range(3):
        coarse_norm_grad(t)

    vm.grad_m[...] = dot_nt(vm.dmerged[...], ld.merge_weight[...])
    loads.merge_t.wait()

    for l in range(2):
        at = slice(72 * l, 72 * l + 72)
        grad = norm_grad(vm.grad_m[at, :], vm.hat_m[at, :], vm.scale_m[at, :1])
        grad = jnp.concatenate([grad[:, 512 * k : 512 * k + 512] for k in range(4)], axis=0)
        vm.send3[l] = dot(ld.merge_t[...], grad.astype(BF16)).astype(BF16).reshape(4, QUARTER, 512)
        send(2, l)
    loads.to_region_t.wait()

    def fine_backward(turn):
        strip = lax.rem(1 - odd + turn, 2)
        base = strip * 320
        level_at = lambda l: rows_at(base + l * 160, 160)
        both_levels = rows_at(base, 320)
        at_strip(strip, lambda keep: [take(2, l, keep) for l in range(2)])

        for l in range(2):
            source = vm.part[l, pl.ds(2 * strip, 2)].reshape(2 * QUARTER, 512)
            vm.dmixed[level_at(l), :] = dot(ld.to_unit[...], source).astype(BF16)

        grad = dot_nt(vm.dmixed[both_levels, :], ld.fine_out[...]) * vm.recip_f[both_levels, :]
        vm.dheads_f[both_levels, :] = grad.astype(BF16)
        vm.dprod_f[both_levels, :] = (grad * vm.heads_f[both_levels, :].astype(F32)).astype(BF16)

        def fine_attend_grad(n):
            start = base + n * UNIT
            at, wide = rows_at(start, UNIT), rows_at(start, 128)
            pairs = [slice(128 * p, 128 * p + 128) for p in range(4)]
            minus = jnp.full((128, 128), -1.0, BF16)
            grads = [two_heads(vm.dheads_f[at, pair], vm.heads2) for pair in pairs]
            prods = [two_heads(vm.dprod_f[at, pair], vm.heads2) for pair in pairs]
            queries = [two_heads(vm.proj[at, pair], vm.heads2) for pair in pairs]
            inner = [
                dot_nt(
                    jnp.concatenate([g, d], axis=1),
                    jnp.concatenate([vm.proj[wide, 1024 + pair.start : 1024 + pair.stop], minus], axis=1),
                )
                for pair, g, d in zip(pairs, grads, prods)
            ]
            raised = [vm.raised_f[strip * 4 + n, p] for p in range(4)]
            dscores = [(e.astype(F32) * x).astype(BF16) for e, x in zip(raised, inner)]
            dvalues = [dot_tn(e, g) for e, g in zip(raised, grads)]
            dkeys = [dot_tn(ds, q) for ds, q in zip(dscores, queries)]
            dqueries = [
                dot(ds, vm.proj[wide, 512 + pair.start : 512 + pair.stop]) for pair, ds in zip(pairs, dscores)
            ]
            for p, pair in enumerate(pairs):
                vm.dproj_f[at, pair] = (one_row(dqueries[p]) * 0.125).astype(BF16)
                vm.dproj_f[at, 512 + pair.start : 512 + pair.stop] = dkeys[p][:UNIT].astype(BF16)
                vm.dproj_f[at, 1024 + pair.start : 1024 + pair.stop] = dvalues[p][:UNIT].astype(BF16)

        def fine_level_back(l):
            for m in range(2):
                fine_attend_grad(2 * l + m)
            grad = dot_nt(vm.dproj_f[level_at(l), :], ld.fine_qkv[...])
            grad = norm_grad(grad, vm.hat_f[level_at(l), :], vm.scale_f[level_at(l), :1])
            dunit = (vm.dmixed[level_at(l), :].astype(F32) + grad).astype(BF16)
            ordered = dot(ld.to_unit_t[...], dunit).astype(BF16)
            vm.send4[l, pl.ds(2 * strip, 2)] = ordered.reshape(2, QUARTER, 512)
            at_strip(strip, lambda keep: send(3, l, keep))

        loop(2, fine_level_back)

    loop(2, fine_backward)
    by_parity(left_mask.wait_send, lambda: None)
    result_near.wait()
    result_far.wait()

    def grid_back(l):
        take(3, l)
        grad_ref[l] = dot(ld.to_region_t[...], vm.region4[l].reshape(4 * QUARTER, 512)).astype(BF16)
        for phase in range(4):
            sent(phase, l)

    loop(2, grid_back)


PIECES = 2


def hand_over(*refs):
    ins, outs = [], []
    for n in range(2):
        src, dst, held = refs[n], refs[2 + n], refs[4 + n]
        size = src.shape[0] // PIECES
        for piece in range(PIECES):
            at = pl.ds(piece * size, size)
            ins.append(pltpu.make_async_copy(src.at[at], held.at[at], refs[6].at[n, piece]))
            outs.append(pltpu.make_async_copy(held.at[at], dst.at[at], refs[7].at[n, piece]))
    for copy in ins:
        copy.start()
    for before, after in zip(ins, outs):
        before.wait()
        after.start()
    for copy in outs:
        copy.wait()


def per_device(n_lat, n_lon, *args):
    tokens, mask_ids, *middle, cotangent = args
    tokens = tokens.transpose(0, 2, 1, 3).reshape(2, 288, 512)
    operands = [tokens, mask_ids.transpose(2, 0, 1), *middle, cotangent.transpose(1, 2, 0, 3)]
    operands += [jnp.asarray(m) for m in row_orders()]
    shapes = dict(zip(ARGS, [(x.shape, x.dtype) for x in operands]))
    loaded = [
        pltpu.VMEM(shapes[name][0][1:] if paired else shapes[name][0], shapes[name][1])
        for name, paired in LOADED.items()
    ]
    result, grad = pl.pallas_call(
        functools.partial(kernel, n_lat, n_lon),
        out_shape=(
            jax.ShapeDtypeStruct((12, 6, 2, 1024), BF16),
            jax.ShapeDtypeStruct((2, 288, 512), BF16),
        ),
        in_specs=[
            pl.BlockSpec(memory_space=pltpu.VMEM if placed == 1 else pl.ANY) for placed in ARGS.values()
        ],
        out_specs=(pl.BlockSpec(memory_space=pltpu.VMEM), pl.BlockSpec(memory_space=pltpu.VMEM)),
        scratch_shapes=[pltpu.VMEM(*spec) for spec in SCRATCH.values()]
        + loaded
        + [
            pltpu.SemaphoreType.DMA((len(LOADED),)),
            pltpu.SemaphoreType.DMA((35, 2)),
            pltpu.SemaphoreType.DMA((35, 2)),
            pltpu.SemaphoreType.DMA((18, 2)),
        ],
        compiler_params=pltpu.CompilerParams(
            collective_id=0, has_side_effects=True, vmem_limit_bytes=60 * 2**20
        ),
    )(*operands)
    anywhere = pl.BlockSpec(memory_space=pl.ANY)
    result, grad = pl.pallas_call(
        hand_over,
        out_shape=(
            jax.ShapeDtypeStruct((12, 6, 2, 1024), BF16),
            jax.ShapeDtypeStruct((8, 72, 512), BF16),
        ),
        in_specs=[anywhere, anywhere],
        out_specs=(anywhere, anywhere),
        scratch_shapes=[
            pltpu.VMEM((12, 6, 2, 1024), BF16),
            pltpu.VMEM((8, 72, 512), BF16),
            pltpu.SemaphoreType.DMA((2, PIECES)),
            pltpu.SemaphoreType.DMA((2, PIECES)),
        ],
        compiler_params=pltpu.CompilerParams(vmem_limit_bytes=60 * 2**20),
    )(result, grad.reshape(8, 72, 512))
    return result.transpose(2, 0, 1, 3), grad.reshape(2, 12, 24, 512).transpose(0, 2, 1, 3)


def solution(mesh):
    grid = P(None, "lat", "lon", None)
    placed = (grid, P(None, "lat", "lon"), P(), P(), P(), P(), P(), P(), P(), grid)
    return jax.shard_map(
        functools.partial(per_device, mesh.shape["lat"], mesh.shape["lon"]),
        mesh=mesh,
        in_specs=placed,
        out_specs=(grid, grid),
        check_vma=False,
    )
```

```python
import functools

import jax
import jax.numpy as jnp
import numpy as np
from jax import lax
from jax.experimental import pallas as pl
from jax.experimental.pallas import tpu as pltpu
from jax.sharding import PartitionSpec as P

F32 = jnp.float32
BF16 = jnp.bfloat16
EPSILON = 1e-05
MASKED = -1e30
MESH = pl.DeviceIdType.MESH

UNIT = 80
QUARTER = 96
NEIGHBOURS = [(a, b) for a in (-1, 0, 1) for b in (-1, 0, 1) if (a, b) != (0, 0)] + [(0, 2), (0, -2)]


def one_hot(pairs, rows, columns):
    out = np.zeros((rows, columns), np.float32)
    for r, c in pairs:
        out[r, c] = 1.0
    return out


def in_quarter(row, col):
    return row * 6 + col if row < 9 else 64 + (row - 9) * 6 + col


@functools.cache
def row_orders():
    to_region = np.zeros((2, 4 * QUARTER, 288), np.float32)
    for odd in range(2):
        for half in range(2):
            for c in range(6):
                for a in range(12):
                    col = 24 * (6 * half + c)
                    upper = a + 3
                    lower = a + 15 if a < 9 else a - 9
                    kept, sent = (lower, upper) if odd else (upper, lower)
                    to_region[odd, half * QUARTER + in_quarter(a, c), col + kept] = 1.0
                    to_region[odd, (2 + half) * QUARTER + in_quarter(a, c), col + sent] = 1.0
    to_unit = one_hot(
        [
            (UNIT * (a // 6) + 12 * (a % 6) + o, (o // 6) * QUARTER + in_quarter(a, o % 6))
            for a in range(12)
            for o in range(12)
        ],
        2 * UNIT,
        2 * QUARTER,
    )
    merge = np.zeros((4 * 72, 4 * QUARTER), np.float32)
    for k, (dr, dc) in enumerate([(0, 0), (1, 0), (0, 1), (1, 1)]):
        for r in range(6):
            for c in range(12):
                quarter, col = divmod(2 * c + dc, 6)
                a = 2 * r + dr
                at = 64 + a * 6 + col if a < 3 else (a - 3) * 6 + col
                merge[k * 72 + r * 12 + c, quarter * QUARTER + at] = 1.0
    coarse = one_hot(
        [
            (l * 72 + r * 12 + c, (((c // 6) * 6 + r) * 6 + c % 6) * 2 + l)
            for l in range(2)
            for r in range(6)
            for c in range(12)
        ],
        144,
        144,
    )
    id_row = one_hot([(t, t // 12 + 18) for t in range(72)], UNIT, 24)
    id_col = one_hot([(t, t % 12) for t in range(72)], UNIT, 12)
    both = lambda m: [m, np.swapaxes(m, -1, -2)]
    orders = both(to_region) + both(to_unit) + both(merge) + both(coarse)
    return [np.ascontiguousarray(m).astype(jnp.bfloat16) for m in orders] + [id_row, id_col]


def dot(a, b):
    return lax.dot_general(a, b, (((1,), (0,)), ((), ())), preferred_element_type=F32)


def dot_nt(a, b):
    return lax.dot_general(a, b, (((1,), (1,)), ((), ())), preferred_element_type=F32)


def dot_tn(a, b):
    return lax.dot_general(a, b, (((0,), (0,)), ((), ())), preferred_element_type=F32)


def normed_rows(x):
    center = x - jnp.mean(x, axis=-1, keepdims=True)
    scale = lax.rsqrt(jnp.mean(center * center, axis=-1, keepdims=True) + EPSILON)
    return center * scale, scale


def norm_grad(grad, hat, scale):
    inner = jnp.mean(grad * hat, axis=-1, keepdims=True)
    return scale * (grad - jnp.mean(grad, axis=-1, keepdims=True) - hat * inner)


def one_row(x):
    span = x.shape[0] // 2
    low = lax.broadcasted_iota(jnp.int32, (span, 128), 1) < 64
    return jnp.where(low, x[:span], x[span:])


def rows_at(start, size, unit=16):
    return pl.ds(start if isinstance(start, int) else pl.multiple_of(start, unit), size)


def loop(count, body, together=1):
    def step(t, carry):
        for n in range(together):
            body(together * t + n)
        return carry

    lax.fori_loop(0, count // together, step, 0)


class Box:
    def __init__(self, **fields):
        self.__dict__.update(fields)


ARGS = dict(
    tokens=0, mask_ids=1, fine_bias=0, fine_qkv=0, fine_out=0, merge_weight=0, coarse_bias=0, coarse_qkv=0,
    coarse_out=0, cotangent=2, to_region=0, to_region_t=0, to_unit=0, to_unit_t=0,
    merge=0, merge_t=0, coarse=0, coarse_t=0, id_row=1, id_col=1,
)
LOADED = dict(
    tokens=0, to_region=1, fine_bias=0, to_unit=0, fine_qkv=0, fine_out=0, to_unit_t=0, coarse=0, coarse_bias=0,
    coarse_out=0, merge=0, merge_weight=0, coarse_qkv=0, coarse_t=0, merge_t=0, to_region_t=1,
)
SCRATCH = dict(
    heads2=((160, 128), BF16),
    heads2_c=((288, 128), BF16),
    send1=((2, 4, QUARTER, 512), BF16),
    region=((2, 4, QUARTER, 512), BF16),
    unit_x=((640, 512), BF16),
    unit_n=((640, 512), BF16),
    hat_f=((640, 512), F32),
    scale_f=((640, 128), F32),
    proj=((704, 1536), BF16),
    mask_left=((12, 2, 24), jnp.int32),
    bias_f=((3, 2, 4, 160, 128), F32),
    raised_f=((8, 4, 160, 128), BF16),
    recip_f=((640, 512), F32),
    heads_f=((640, 512), BF16),
    send2=((2, 4, QUARTER, 512), BF16),
    quarters=((2, 4, QUARTER, 512), BF16),
    hat_m=((144, 2048), F32),
    scale_m=((144, 128), F32),
    normed_m=((144, 2048), BF16),
    merged=((144, 1024), BF16),
    hat_c=((144, 1024), F32),
    scale_c=((144, 128), F32),
    normed_c=((144, 1024), BF16),
    proj_c=((256, 3072), BF16),
    bias_c=((16, 144, 256), F32),
    raised_c=((8, 288, 256), BF16),
    recip_c=((144, 1024), F32),
    heads_c=((144, 1024), BF16),
    result=((144, 1024), BF16),
    result2=((2, 6, 6, 2, 1024), BF16),
    cot2=((2, 6, 6, 2, 1024), BF16),
    cot=((144, 1024), BF16),
    dheads_c=((144, 1024), BF16),
    dprod_c=((144, 1024), BF16),
    dproj_c=((144, 3072), BF16),
    grad_c=((144, 1024), F32),
    dmerged=((144, 1024), BF16),
    grad_m=((144, 2048), F32),
    send3=((2, 4, QUARTER, 512), BF16),
    part=((2, 4, QUARTER, 512), BF16),
    dmixed=((640, 512), BF16),
    dheads_f=((640, 512), BF16),
    dprod_f=((640, 512), BF16),
    dproj_f=((640, 1536), BF16),
    send4=((2, 4, QUARTER, 512), BF16),
    region4=((2, 4, QUARTER, 512), BF16),
)
def kernel(n_lat, n_lon, *refs):
    rest = list(refs)
    hbm = Box(**{name: rest.pop(0) for name in ARGS})
    result_ref, grad_ref = rest.pop(0), rest.pop(0)
    vm = Box(**{name: rest.pop(0) for name in SCRATCH})
    ld = Box(**{name: rest.pop(0) for name in LOADED})
    load_sem, send_sem, recv_sem, near_sem = rest

    i, j = lax.axis_index("lat"), lax.axis_index("lon")
    odd = lax.rem(j, 2)
    even = odd == 0

    def device(di, dj):
        return (lax.rem(i + di + n_lat, n_lat), lax.rem(j + dj + n_lon, n_lon))

    def remote(src, dst, sem, l, target):
        return pltpu.make_async_remote_copy(
            src_ref=src,
            dst_ref=dst,
            send_sem=send_sem.at[sem, l],
            recv_sem=recv_sem.at[sem, l],
            device_id=target,
            device_id_type=MESH,
        )

    vm.mask_left[...] = jnp.zeros((12, 2, 24), jnp.int32)
    barrier = pltpu.get_barrier_semaphore()
    for di, dj in NEIGHBOURS:
        pl.semaphore_signal(barrier, inc=1, device_id=device(di, dj), device_id_type=MESH)

    loads = Box()
    for at, (name, paired) in enumerate(LOADED.items()):
        src = getattr(hbm, name)
        if paired:
            src = src.at[odd]
        copy = pltpu.make_async_copy(src, getattr(ld, name), load_sem.at[at])
        copy.start()
        setattr(loads, name, copy)
    own_cot = pltpu.make_async_copy(
        hbm.cotangent.at[pl.ds(6 * odd, 6)], vm.cot2.at[odd], near_sem.at[16, 0]
    )
    own_cot.start()

    for end in (320, 640):
        vm.proj[end : end + 64, :] = jnp.zeros((64, 1536), BF16)
    vm.proj_c[144:, :] = jnp.zeros((112, 3072), BF16)
    for ref in (vm.heads2, vm.heads2_c):
        low = lax.broadcasted_iota(jnp.int32, ref.shape, 1) < 64
        first = lax.broadcasted_iota(jnp.int32, ref.shape, 0) < ref.shape[0] // 2
        ref[...] = jnp.where(low == first, 1.0, 0.0).astype(BF16)

    def two_heads(x, mask):
        return jnp.concatenate([x, x], axis=0) * mask[...]

    loads.tokens.wait()
    loads.to_region.wait()
    pl.semaphore_wait(barrier, len(NEIGHBOURS))

    whole, top, low = (0, 96), (0, 64), (64, 32)
    left, right, far_left, far_right = (0, -1), (0, 1), (0, -2), (0, 2)
    plans = [
        (
            vm.send1,
            vm.region,
            [
                (2, 3, low, (-1, -1)), (3, 0, low, (-1, 1)), (2, 3, top, left), (3, 0, top, right),
                (0, 1, whole, None), (1, 2, whole, None),
            ],
            [
                (0, 1, low, (-1, 0)), (1, 2, low, (-1, 0)), (2, 3, whole, left), (3, 0, whole, right),
                (0, 1, top, None), (1, 2, top, None),
            ],
        ),
        (
            vm.send2,
            vm.quarters,
            [
                (0, 3, top, far_left), (0, 3, low, left), (1, 0, low, right), (2, 1, low, right),
                (3, 2, low, right), (1, 0, top, None), (2, 1, top, None), (3, 2, top, None),
            ],
            [
                (3, 0, top, far_right), (3, 0, low, (1, 1)), (0, 1, low, (1, -1)), (1, 2, low, (1, -1)),
                (2, 3, low, (1, -1)), (0, 1, top, None), (1, 2, top, None), (2, 3, top, None),
            ],
        ),
    ]
    for (_, _, of_even, of_odd), src, dst in ((plans[1], vm.send3, vm.part), (plans[0], vm.send4, vm.region4)):
        back_even, back_odd = [], []
        for mine, ours in ((of_even, 0), (of_odd, 1)):
            for at, into, rows, to in mine:
                if to is None:
                    target = ours
                    way = None
                else:
                    target = (ours + to[1]) % 2
                    way = (-to[0], -to[1])
                (back_odd if target else back_even).append((into, at, rows, way))
        plans.append((src, dst, back_even, back_odd))

    def transfer(phase, l, plan):
        at, into, (start, size), to = plan
        src, dst = plans[phase][:2]
        src, dst = src.at[l, at, pl.ds(start, size)], dst.at[l, into, pl.ds(start, size)]
        sem = phase * 8 + into * 2 + (start > 0)
        if to is None:
            return pltpu.make_async_copy(src, dst, near_sem.at[phase * 4 + into, l])
        return remote(src, dst, sem, l, device(*to))

    def by_parity(of_even, of_odd):
        @pl.when(even)
        def _():
            of_even()

        @pl.when(odd == 1)
        def _():
            of_odd()

    def send(phase, l, keep=None):
        def start(mine):
            for plan in mine:
                if keep is None or plan[0] in keep:
                    transfer(phase, l, plan).start()

        by_parity(lambda: start(plans[phase][2]), lambda: start(plans[phase][3]))

    def arrivals(phase, parity):
        got = []
        for ours in range(2):
            for plan in plans[phase][2 + ours]:
                to = plan[3]
                if (ours if to is None else (ours + to[1]) % 2) == parity:
                    got.append(plan)
        return got

    def take(phase, l, keep=None):
        def wait(parity):
            for plan in arrivals(phase, parity):
                if keep is None or plan[1] in keep:
                    copy = transfer(phase, l, plan)
                    copy.wait() if plan[3] is None else copy.wait_recv()

        by_parity(lambda: wait(0), lambda: wait(1))

    def sent(phase, l):
        def wait(mine):
            for plan in mine:
                if plan[3] is not None:
                    transfer(phase, l, plan).wait_send()

        by_parity(lambda: wait(plans[phase][2]), lambda: wait(plans[phase][3]))

    def at_strip(strip, of_strip):
        @pl.when(strip == 0)
        def _():
            of_strip((0, 1))

        @pl.when(strip == 1)
        def _():
            of_strip((2, 3))

    def regions(l):
        vm.send1[l] = dot(ld.to_region[...], ld.tokens[l]).astype(BF16).reshape(4, QUARTER, 512)
        send(0, l)

    for l in range(2):
        regions(l)
    partner_cot = remote(
        hbm.cotangent.at[pl.ds(6 - 6 * odd, 6)], vm.cot2.at[odd], 32, 0, device(0, 1 - 2 * odd)
    )
    partner_cot.start()
    left_mask = remote(hbm.mask_ids, vm.mask_left, 34, 0, device(0, 1))
    by_parity(left_mask.start, lambda: None)

    loads.fine_bias.wait()
    by_parity(lambda: None, left_mask.wait_recv)
    lanes = lax.broadcasted_iota(jnp.int32, (UNIT, 128), 1)
    subs = lax.broadcasted_iota(jnp.int32, (UNIT, 128), 0)
    past = jnp.where(lanes >= 72, MASKED, 0.0).astype(F32)
    for level in range(2):
        masks = [past]
        for ids in (vm.mask_left, hbm.mask_ids):
            spread = dot(hbm.id_col[...], ids[:, level, :].astype(F32))
            id_of = jnp.sum(spread * hbm.id_row[...], axis=-1, keepdims=True)
            id_at = dot(jnp.ones((8, UNIT), F32), jnp.where(lanes == subs, id_of, 0.0))[:1]
            masks.append(jnp.where(id_of == id_at, past, MASKED))
        for head in range(8):
            span = slice(72 * level, 72 * level + 72)
            block = ld.fine_bias[head, span, span]
            block = jnp.concatenate([block, jnp.zeros((72, 56), F32)], axis=1)
            block = jnp.concatenate([block, jnp.zeros((8, 128), F32)], axis=0)
            at = slice(UNIT * (head % 2), UNIT * (head % 2) + UNIT)
            for kind, mask in enumerate(masks):
                vm.bias_f[kind, level, head // 2, at, :] = block + mask

    loads.to_unit.wait()
    loads.fine_qkv.wait()
    loads.fine_out.wait()
    loads.to_unit_t.wait()

    def fine_forward(turn):
        strip = lax.rem(1 - odd + turn, 2)
        base = strip * 320
        level_at = lambda l: rows_at(base + l * 160, 160)
        both_levels = rows_at(base, 320)
        at_strip(strip, lambda keep: [take(0, l, keep) for l in range(2)])

        for l in range(2):
            source = vm.region[l, pl.ds(2 * strip, 2)].reshape(2 * QUARTER, 512)
            x = dot(ld.to_unit[...], source)
            hat, scale = normed_rows(x)
            vm.unit_x[level_at(l), :] = x.astype(BF16)
            vm.hat_f[level_at(l), :] = hat
            vm.scale_f[level_at(l), :] = jnp.broadcast_to(scale, (160, 128))
            vm.unit_n[level_at(l), :] = hat.astype(BF16)

        projected = dot(vm.unit_n[both_levels, :], ld.fine_qkv[...])
        vm.proj[both_levels, :512] = (projected[:, :512] * 0.125).astype(BF16)
        vm.proj[both_levels, 512:] = projected[:, 512:].astype(BF16)

        def fine_attend(n):
            l, m = lax.div(n, 2), lax.rem(n, 2)
            last = odd * m * (1 + strip)
            start = base + n * UNIT
            at, wide = rows_at(start, UNIT), rows_at(start, 128)
            pairs = [slice(128 * p, 128 * p + 128) for p in range(4)]
            ones = jnp.ones((128, 128), BF16)
            scores = [
                dot_nt(
                    two_heads(vm.proj[at, pair], vm.heads2), vm.proj[wide, 512 + pair.start : 512 + pair.stop]
                )
                + vm.bias_f[last, 1 - l, p]
                for p, pair in enumerate(pairs)
            ]
            tops = [jnp.max(s, axis=-1, keepdims=True) for s in scores]
            raised = [jnp.exp(s - t).astype(BF16) for s, t in zip(scores, tops)]
            sums = [
                dot(e, jnp.concatenate([vm.proj[wide, 1024 + pair.start : 1024 + pair.stop], ones], axis=1))
                for e, pair in zip(raised, pairs)
            ]
            for p, pair in enumerate(pairs):
                recip = 1.0 / one_row(sums[p][:, 128:])
                vm.raised_f[strip * 4 + n, p] = raised[p]
                vm.recip_f[at, pair] = recip
                vm.heads_f[at, pair] = (one_row(sums[p][:, :128]) * recip).astype(BF16)

        def fine_level(l):
            for m in range(2):
                fine_attend(2 * l + m)
            mixed = vm.unit_x[level_at(l), :].astype(F32) + dot(vm.heads_f[level_at(l), :], ld.fine_out[...])
            ordered = dot(ld.to_unit_t[...], mixed.astype(BF16)).astype(BF16)
            vm.send2[l, pl.ds(2 * strip, 2)] = ordered.reshape(2, QUARTER, 512)
            at_strip(strip, lambda keep: send(1, l, keep))

        loop(2, fine_level)

    loop(2, fine_forward)
    loads.coarse_bias.wait()

    def coarse_pad(h):
        vm.bias_c[h] = jnp.concatenate([ld.coarse_bias[h], jnp.full((144, 112), MASKED, F32)], axis=1)

    loop(16, coarse_pad)
    own_cot.wait()
    partner_cot.wait()
    loads.coarse.wait()
    vm.cot[...] = dot(ld.coarse[...], vm.cot2[...].reshape(144, 1024)).astype(BF16)
    loads.coarse_out.wait()

    vm.grad_c[...] = dot_nt(vm.cot[...], ld.coarse_out[...])
    loads.merge.wait()
    loads.merge_weight.wait()
    loads.coarse_qkv.wait()
    loads.coarse_t.wait()

    for l in range(2):
        take(1, l)
    for l in range(2):
        gathered = dot(ld.merge[...], vm.quarters[l].reshape(4 * QUARTER, 512))
        for k in range(4):
            vm.hat_m[72 * l : 72 * l + 72, 512 * k : 512 * k + 512] = gathered[72 * k : 72 * k + 72]

    def merge_norm(t):
        at = rows_at(t * 48, 48)
        hat, scale = normed_rows(vm.hat_m[at, :])
        vm.hat_m[at, :] = hat
        vm.scale_m[at, :] = jnp.broadcast_to(scale, (48, 128))
        vm.normed_m[at, :] = hat.astype(BF16)

    for t in range(3):
        merge_norm(t)

    vm.merged[...] = dot(vm.normed_m[...], ld.merge_weight[...]).astype(BF16)

    def coarse_norm(t):
        at = rows_at(t * 48, 48)
        hat, scale = normed_rows(vm.merged[at, :].astype(F32))
        vm.hat_c[at, :] = hat
        vm.scale_c[at, :] = jnp.broadcast_to(scale, (48, 128))
        vm.normed_c[at, :] = hat.astype(BF16)

    for t in range(3):
        coarse_norm(t)

    projected = dot(vm.normed_c[...], ld.coarse_qkv[...])
    vm.proj_c[:144, :1024] = (projected[:, :1024] * 0.125).astype(BF16)
    vm.proj_c[:144, 1024:] = projected[:, 1024:].astype(BF16)

    def cols_at(p, base):
        return rows_at(p * 128 + base, 128, 128)

    def coarse_attend(t):
        pairs = [2 * t, 2 * t + 1]
        ones = jnp.ones((256, 128), BF16)
        scores = [
            dot_nt(two_heads(vm.proj_c[:144, cols_at(p, 0)], vm.heads2_c), vm.proj_c[:, cols_at(p, 1024)])
            + vm.bias_c[pl.ds(2 * p, 2)].reshape(288, 256)
            for p in pairs
        ]
        tops = [jnp.max(s, axis=-1, keepdims=True) for s in scores]
        raised = [jnp.exp(s - top).astype(BF16) for s, top in zip(scores, tops)]
        sums = [
            dot(e, jnp.concatenate([vm.proj_c[:, cols_at(p, 2048)], ones], axis=1))
            for e, p in zip(raised, pairs)
        ]
        for p, e, total in zip(pairs, raised, sums):
            recip = 1.0 / one_row(total[:, 128:])
            vm.raised_c[p] = e
            vm.recip_c[:, cols_at(p, 0)] = recip
            vm.heads_c[:, cols_at(p, 0)] = (one_row(total[:, :128]) * recip).astype(BF16)

    loop(4, coarse_attend, 2)

    mixed = dot(vm.heads_c[...], ld.coarse_out[...])
    vm.result[...] = (vm.merged[...].astype(F32) + mixed).astype(BF16)
    grad = vm.grad_c[...] * vm.recip_c[...]
    vm.dheads_c[...] = grad.astype(BF16)
    vm.dprod_c[...] = (grad * vm.heads_c[...].astype(F32)).astype(BF16)
    vm.result2[...] = dot(ld.coarse_t[...], vm.result[...]).astype(BF16).reshape(2, 6, 6, 2, 1024)
    into = result_ref.at[pl.ds(6 * odd, 6)]
    result_near = pltpu.make_async_copy(vm.result2.at[odd], into, near_sem.at[17, 0])
    result_far = remote(vm.result2.at[1 - odd], into, 33, 0, device(0, 1 - 2 * odd))
    result_near.start()
    result_far.start()

    def coarse_attend_grad(t):
        pairs = [2 * t, 2 * t + 1]
        minus = jnp.full((256, 128), -1.0, BF16)
        grads = [two_heads(vm.dheads_c[:, cols_at(p, 0)], vm.heads2_c) for p in pairs]
        prods = [two_heads(vm.dprod_c[:, cols_at(p, 0)], vm.heads2_c) for p in pairs]
        queries = [two_heads(vm.proj_c[:144, cols_at(p, 0)], vm.heads2_c) for p in pairs]
        inner = [
            dot_nt(
                jnp.concatenate([g, d], axis=1), jnp.concatenate([vm.proj_c[:, cols_at(p, 2048)], minus], axis=1)
            )
            for p, g, d in zip(pairs, grads, prods)
        ]
        dscores = [(vm.raised_c[p].astype(F32) * x).astype(BF16) for p, x in zip(pairs, inner)]
        for p, g, q, ds in zip(pairs, grads, queries, dscores):
            vm.dproj_c[:, cols_at(p, 2048)] = dot_tn(vm.raised_c[p], g)[:144].astype(BF16)
            dq = one_row(dot(ds, vm.proj_c[:, cols_at(p, 1024)]))
            vm.dproj_c[:, cols_at(p, 0)] = (dq * 0.125).astype(BF16)
            vm.dproj_c[:, cols_at(p, 1024)] = dot_tn(ds, q)[:144].astype(BF16)

    loop(4, coarse_attend_grad, 2)

    vm.grad_c[...] = dot_nt(vm.dproj_c[...], ld.coarse_qkv[...])

    def coarse_norm_grad(t):
        at = rows_at(t * 48, 48)
        grad = norm_grad(vm.grad_c[at, :], vm.hat_c[at, :], vm.scale_c[at, :1])
        vm.dmerged[at, :] = (vm.cot[at, :].astype(F32) + grad).astype(BF16)

    for t in range(3):
        coarse_norm_grad(t)

    vm.grad_m[...] = dot_nt(vm.dmerged[...], ld.merge_weight[...])
    loads.merge_t.wait()

    for l in range(2):
        at = slice(72 * l, 72 * l + 72)
        grad = norm_grad(vm.grad_m[at, :], vm.hat_m[at, :], vm.scale_m[at, :1])
        grad = jnp.concatenate([grad[:, 512 * k : 512 * k + 512] for k in range(4)], axis=0)
        vm.send3[l] = dot(ld.merge_t[...], grad.astype(BF16)).astype(BF16).reshape(4, QUARTER, 512)
        send(2, l)
    loads.to_region_t.wait()

    def fine_backward(turn):
        strip = lax.rem(1 - odd + turn, 2)
        base = strip * 320
        level_at = lambda l: rows_at(base + l * 160, 160)
        both_levels = rows_at(base, 320)
        at_strip(strip, lambda keep: [take(2, l, keep) for l in range(2)])

        for l in range(2):
            source = vm.part[l, pl.ds(2 * strip, 2)].reshape(2 * QUARTER, 512)
            vm.dmixed[level_at(l), :] = dot(ld.to_unit[...], source).astype(BF16)

        grad = dot_nt(vm.dmixed[both_levels, :], ld.fine_out[...]) * vm.recip_f[both_levels, :]
        vm.dheads_f[both_levels, :] = grad.astype(BF16)
        vm.dprod_f[both_levels, :] = (grad * vm.heads_f[both_levels, :].astype(F32)).astype(BF16)

        def fine_attend_grad(n):
            start = base + n * UNIT
            at, wide = rows_at(start, UNIT), rows_at(start, 128)
            pairs = [slice(128 * p, 128 * p + 128) for p in range(4)]
            minus = jnp.full((128, 128), -1.0, BF16)
            grads = [two_heads(vm.dheads_f[at, pair], vm.heads2) for pair in pairs]
            prods = [two_heads(vm.dprod_f[at, pair], vm.heads2) for pair in pairs]
            queries = [two_heads(vm.proj[at, pair], vm.heads2) for pair in pairs]
            inner = [
                dot_nt(
                    jnp.concatenate([g, d], axis=1),
                    jnp.concatenate([vm.proj[wide, 1024 + pair.start : 1024 + pair.stop], minus], axis=1),
                )
                for pair, g, d in zip(pairs, grads, prods)
            ]
            raised = [vm.raised_f[strip * 4 + n, p] for p in range(4)]
            dscores = [(e.astype(F32) * x).astype(BF16) for e, x in zip(raised, inner)]
            dvalues = [dot_tn(e, g) for e, g in zip(raised, grads)]
            dkeys = [dot_tn(ds, q) for ds, q in zip(dscores, queries)]
            dqueries = [
                dot(ds, vm.proj[wide, 512 + pair.start : 512 + pair.stop]) for pair, ds in zip(pairs, dscores)
            ]
            for p, pair in enumerate(pairs):
                vm.dproj_f[at, pair] = (one_row(dqueries[p]) * 0.125).astype(BF16)
                vm.dproj_f[at, 512 + pair.start : 512 + pair.stop] = dkeys[p][:UNIT].astype(BF16)
                vm.dproj_f[at, 1024 + pair.start : 1024 + pair.stop] = dvalues[p][:UNIT].astype(BF16)

        loop(4, fine_attend_grad, 2)
        grad = dot_nt(vm.dproj_f[both_levels, :], ld.fine_qkv[...])
        grad = norm_grad(grad, vm.hat_f[both_levels, :], vm.scale_f[both_levels, :1])
        dunit = (vm.dmixed[both_levels, :].astype(F32) + grad).astype(BF16)
        for l in range(2):
            ordered = dot(ld.to_unit_t[...], dunit[160 * l : 160 * l + 160]).astype(BF16)
            vm.send4[l, pl.ds(2 * strip, 2)] = ordered.reshape(2, QUARTER, 512)
            at_strip(strip, lambda keep: send(3, l, keep))

    loop(2, fine_backward)
    by_parity(left_mask.wait_send, lambda: None)
    result_near.wait()
    result_far.wait()

    def grid_back(l):
        take(3, l)
        grad_ref[l] = dot(ld.to_region_t[...], vm.region4[l].reshape(4 * QUARTER, 512)).astype(BF16)
        for phase in range(4):
            sent(phase, l)

    loop(2, grid_back)


PIECES = 2


def hand_over(*refs):
    ins, outs = [], []
    for n in range(2):
        src, dst, held = refs[n], refs[2 + n], refs[4 + n]
        size = src.shape[0] // PIECES
        for piece in range(PIECES):
            at = pl.ds(piece * size, size)
            ins.append(pltpu.make_async_copy(src.at[at], held.at[at], refs[6].at[n, piece]))
            outs.append(pltpu.make_async_copy(held.at[at], dst.at[at], refs[7].at[n, piece]))
    for copy in ins:
        copy.start()
    for before, after in zip(ins, outs):
        before.wait()
        after.start()
    for copy in outs:
        copy.wait()


def per_device(n_lat, n_lon, *args):
    tokens, mask_ids, *middle, cotangent = args
    tokens = tokens.transpose(0, 2, 1, 3).reshape(2, 288, 512)
    operands = [tokens, mask_ids.transpose(2, 0, 1), *middle, cotangent.transpose(1, 2, 0, 3)]
    operands += [jnp.asarray(m) for m in row_orders()]
    shapes = dict(zip(ARGS, [(x.shape, x.dtype) for x in operands]))
    loaded = [
        pltpu.VMEM(shapes[name][0][1:] if paired else shapes[name][0], shapes[name][1])
        for name, paired in LOADED.items()
    ]
    result, grad = pl.pallas_call(
        functools.partial(kernel, n_lat, n_lon),
        out_shape=(
            jax.ShapeDtypeStruct((12, 6, 2, 1024), BF16),
            jax.ShapeDtypeStruct((2, 288, 512), BF16),
        ),
        in_specs=[
            pl.BlockSpec(memory_space=pltpu.VMEM if placed == 1 else pl.ANY) for placed in ARGS.values()
        ],
        out_specs=(pl.BlockSpec(memory_space=pltpu.VMEM), pl.BlockSpec(memory_space=pltpu.VMEM)),
        scratch_shapes=[pltpu.VMEM(*spec) for spec in SCRATCH.values()]
        + loaded
        + [
            pltpu.SemaphoreType.DMA((len(LOADED),)),
            pltpu.SemaphoreType.DMA((35, 2)),
            pltpu.SemaphoreType.DMA((35, 2)),
            pltpu.SemaphoreType.DMA((18, 2)),
        ],
        compiler_params=pltpu.CompilerParams(
            collective_id=0, has_side_effects=True, vmem_limit_bytes=60 * 2**20
        ),
    )(*operands)
    anywhere = pl.BlockSpec(memory_space=pl.ANY)
    result, grad = pl.pallas_call(
        hand_over,
        out_shape=(
            jax.ShapeDtypeStruct((12, 6, 2, 1024), BF16),
            jax.ShapeDtypeStruct((8, 72, 512), BF16),
        ),
        in_specs=[anywhere, anywhere],
        out_specs=(anywhere, anywhere),
        scratch_shapes=[
            pltpu.VMEM((12, 6, 2, 1024), BF16),
            pltpu.VMEM((8, 72, 512), BF16),
            pltpu.SemaphoreType.DMA((2, PIECES)),
            pltpu.SemaphoreType.DMA((2, PIECES)),
        ],
        compiler_params=pltpu.CompilerParams(vmem_limit_bytes=60 * 2**20),
    )(result, grad.reshape(8, 72, 512))
    return result.transpose(2, 0, 1, 3), grad.reshape(2, 12, 24, 512).transpose(0, 2, 1, 3)


def solution(mesh):
    grid = P(None, "lat", "lon", None)
    placed = (grid, P(None, "lat", "lon"), P(), P(), P(), P(), P(), P(), P(), grid)
    return jax.shard_map(
        functools.partial(per_device, mesh.shape["lat"], mesh.shape["lon"]),
        mesh=mesh,
        in_specs=placed,
        out_specs=(grid, grid),
        check_vma=False,
    )
```
